128 devices in a mesh: stream: 4 (over x), tile: 32 (over y, z, core).
Axes of the slice: x: 4, y: 4, z: 4, core: 2. Of those that a mesh axis runs over, the one named last changes fastest.
Arguments:
- frame_in: bfloat16 [16, 64, 128, 384], P('stream', 'tile'), may hold values from -6 to 6
- cache_first: bfloat16 [16, 2, 64, 128, 384], P('stream', None, 'tile'), may hold values from -6 to 6
- cache_second: bfloat16 [16, 2, 64, 128, 384], P('stream', None, 'tile'), may hold values from -6 to 6
- gain_first: float32 [384], replicated, may hold values from 0.1 to 1.9
- gain_second: float32 [384], replicated, may hold values from 0.1 to 1.9
- conv_first: bfloat16 [3, 3, 3, 384, 384], replicated, may hold values from -0.0625 to 0.0625
- conv_second: bfloat16 [3, 3, 3, 384, 384], replicated, may hold values from -0.0625 to 0.0625
- bias_first: float32 [384], replicated, may hold values from -0.5 to 0.5
- bias_second: float32 [384], replicated, may hold values from -0.5 to 0.5
- old_slot: int32 [16], replicated, may hold values from 0 to 15, as said below
- new_slot: int32 [16], replicated, may hold values from 0 to 15, as said below
- old_shift: int32 [16], replicated, may hold values from 0 to 31
- new_shift: int32 [16], replicated, may hold values from 0 to 31
- frame_count: int32 [16], replicated, may hold values from 0 to 2
Outputs:
- mixed_frame: bfloat16 [16, 64, 128, 384], P('stream', 'tile')
- next_first: bfloat16 [16, 2, 64, 128, 384], P('stream', None, 'tile')
- next_second: bfloat16 [16, 2, 64, 128, 384], P('stream', None, 'tile')
The draws below stay inside these ranges and needn't reach their ends.
Inputs may be any that keep to these rules, and one draw needn't show every extreme that they name: `old_slot`: slot q is position q % 4 of group q // 4; every slot holds one stream. `new_slot`: every slot holds one stream; of the streams of one old group at most 2 go to any one new group, and from every old group exactly 2 go to one same group.
All inputs are finite; a program needn't handle non-finite values.
Results may differ from the reference program's by a relative error of at most 0.0025.
Values may be sent and summed in bfloat16 or wider, within the bound.
No kernel may reach another device: no remote copies, remote signals or barrier semaphores. Data moves between devices by JAX's collectives and lax.ppermute only.
A program may use at most 128 MiB of HBM per device.

```python
import jax
import jax.numpy as jnp
from jax import lax

C = 384
SLOTS = 4
ROWS = 2
COLS = 128
CAP = 2
FLIGHT = 16
TILES = 32
HROWS = 64


def slot_plan(key):
    groups = FLIGHT // SLOTS
    old_slots = jax.random.permutation(jax.random.fold_in(key, 11), FLIGHT).astype(jnp.int32)
    group_order = jax.random.permutation(jax.random.fold_in(key, 12), groups).astype(jnp.int32)
    positions_all = jnp.arange(SLOTS, dtype=jnp.int32)
    chosen = jnp.where(positions_all < CAP, 0, 1 + (positions_all - CAP) % max(groups - 1, 1))
    offsets = group_order[chosen]
    places = jax.vmap(lambda group_id: jax.random.permutation(jax.random.fold_in(key, 100 + group_id), SLOTS).astype(jnp.int32))(jnp.arange(groups, dtype=jnp.int32))
    old_group = old_slots // SLOTS
    new_position = places[old_group, old_slots % SLOTS]
    target_group = (old_group + offsets[new_position]) % groups
    new_slots = (target_group * SLOTS + new_position).astype(jnp.int32)
    return (old_slots, new_slots)


def draw_old_slot(key, part):
    return slot_plan(key)[0]


def draw_new_slot(key, part):
    return slot_plan(key)[1]


def touch_ends(entries, rng, smallest, top_value):
    index_at = [jax.random.randint(jax.random.fold_in(rng, axis), (), 0, length) for axis, length in enumerate(entries.shape)]
    main_axis = entries.shape.index(max(entries.shape))
    neighbour = index_at[:main_axis] + [(index_at[main_axis] + 1) % entries.shape[main_axis]] + index_at[main_axis + 1:]
    return entries.at[tuple(index_at)].set(smallest).at[tuple(neighbour)].set(top_value)


def levels(key, shape, cuts, smallest, high):
    def one(axis_at, shards_of):
        steps = jax.random.uniform(jax.random.fold_in(jax.random.fold_in(key, 6), axis_at), (shards_of,), jnp.float32, smallest / len(cuts), high / len(cuts))
        return jnp.repeat(jnp.exp(steps), shape[axis_at] // shards_of).reshape((-1,) + (1,) * (len(shape) - axis_at - 1))

    level = one(*cuts[0])
    for cut in cuts[1:]:
        level = level * one(*cut)
    return level


def scatter_about(rng, shape, width, limit, cuts=(), kind=jnp.bfloat16):
    array = jax.random.normal(rng, shape, jnp.float32) * width
    if len(cuts) > 0:
        array = levels(rng, shape, cuts, -0.22, 0.18) * array
    return jnp.clip(array, min=-limit, max=limit).astype(kind)


def setup_inputs(seed: int = 0) -> dict:
    keys = jax.random.split(jax.random.key(seed), 15)
    return {
        "frame_in": scatter_about(keys[0], (FLIGHT, HROWS, COLS, C), 1.0, 6.0, ((0, 4), (1, 32))),
        "cache_first": scatter_about(keys[1], (FLIGHT, 2, HROWS, COLS, C), 1.0, 6.0, ((0, 4), (2, 32))),
        "cache_second": scatter_about(keys[2], (FLIGHT, 2, HROWS, COLS, C), 1.0, 6.0, ((0, 4), (2, 32))),
        "gain_first": jnp.clip(1.0 + 0.18 * jax.random.normal(keys[3], (C,), jnp.float32), 0.1, 1.9),
        "gain_second": jnp.clip(1.0 + 0.18 * jax.random.normal(keys[4], (C,), jnp.float32), 0.1, 1.9),
        "conv_first": scatter_about(keys[5], (3, 3, 3, C, C), (27 * C) ** -0.5, 0.0625),
        "conv_second": scatter_about(keys[6], (3, 3, 3, C, C), (27 * C) ** -0.5, 0.0625),
        "bias_first": jnp.clip(jax.random.uniform(keys[7], (C,), jnp.float32, -0.5, 0.5), -0.5, 0.5),
        "bias_second": jnp.clip(jax.random.uniform(keys[8], (C,), jnp.float32, -0.5, 0.5), -0.5, 0.5),
        "old_slot": draw_old_slot(jax.random.fold_in(keys[14], 71), 0),
        "new_slot": draw_new_slot(jax.random.fold_in(keys[14], 71), 0),
        "old_shift": touch_ends(jax.random.randint(keys[11], (FLIGHT,), 0, TILES), jax.random.fold_in(keys[11], 1), 0, TILES - 1).astype(jnp.int32),
        "new_shift": touch_ends(jax.random.randint(keys[12], (FLIGHT,), 0, TILES), jax.random.fold_in(keys[12], 1), 0, TILES - 1).astype(jnp.int32),
        "frame_count": touch_ends(jax.random.randint(keys[13], (FLIGHT,), 0, 3), jax.random.fold_in(keys[13], 1), 0, 2).astype(jnp.int32),
    }


def activate(values, gain):
    scaled = values * lax.rsqrt(lax.optimization_barrier(jnp.mean(values * values, axis=-1, keepdims=True)) + 1e-06)
    return jax.nn.silu(scaled * gain)

def convolve(stacked, weight, bias_vec):
    n_rows = stacked.shape[1]
    n_cols = stacked.shape[2]
    channels = stacked.shape[3]
    padded = jnp.pad(stacked, ((0, 0), (1, 1), (1, 1), (0, 0)))
    pieces = [padded[t_step, y_step:y_step + n_rows, x_step:x_step + n_cols, :] for t_step in range(3) for y_step in range(3) for x_step in range(3)]
    patches = jnp.concatenate(pieces, axis=-1).reshape(-1, 27 * channels).astype(jnp.float32)
    kernel = weight.reshape(27 * channels, channels).astype(jnp.float32)
    result = jnp.dot(patches, kernel, preferred_element_type=jnp.float32, precision=lax.Precision.HIGHEST) + bias_vec
    return result.reshape(n_rows, n_cols, channels)

def reference(frame_in, cache_first, cache_second, gain_first, gain_second, conv_first, conv_second, bias_first, bias_second, old_slot, new_slot, old_shift, new_shift, frame_count):
    all_rows = frame_in.shape[1]
    row_ids = jnp.arange(all_rows, dtype=jnp.int32)

    def natural(stored, shift_rows):
        return jnp.take(stored, (row_ids + shift_rows * ROWS) % all_rows, axis=-3)

    def restored(natural_frame, shift_rows):
        return jnp.take(natural_frame, (row_ids - shift_rows * ROWS) % all_rows, axis=-3)

    def per_stream(stream):
        frames_done = frame_count[stream]
        frame_keep = jnp.stack([frames_done >= 2, frames_done >= 1]).astype(jnp.bfloat16)[:, None, None, None]
        prior_first = natural(cache_first[old_slot[stream]], old_shift[stream]) * frame_keep
        prior_second = natural(cache_second[old_slot[stream]], old_shift[stream]) * frame_keep
        current = natural(frame_in[new_slot[stream]], new_shift[stream])
        act_first = activate(current.astype(jnp.float32), gain_first).astype(jnp.bfloat16)
        hidden = convolve(jnp.concatenate([prior_first, act_first[None]], axis=0), conv_first, bias_first)
        act_second = activate(hidden, gain_second).astype(jnp.bfloat16)
        second_out = convolve(jnp.concatenate([prior_second, act_second[None]], axis=0), conv_second, bias_second)
        mixed = (second_out + current.astype(jnp.float32)).astype(jnp.bfloat16)
        shift_new = new_shift[stream]
        next_a = jnp.stack([prior_first[1], act_first], axis=0)
        next_b = jnp.stack([prior_second[1], act_second], axis=0)
        return (restored(mixed, shift_new), restored(next_a, shift_new), restored(next_b, shift_new))
    results = lax.map(per_stream, jnp.arange(FLIGHT, dtype=jnp.int32))
    inverse = jnp.zeros((FLIGHT,), jnp.int32).at[new_slot].set(jnp.arange(FLIGHT, dtype=jnp.int32))
    return (results[0][inverse], results[1][inverse], results[2][inverse])
```

```python
import jax
import jax.numpy as jnp
from jax import lax
from jax.experimental import pallas as pl
from jax.experimental.pallas import tpu as pltpu
from jax.sharding import PartitionSpec as P

BOTH = ("stream", "tile")
CB = 8


def lookup(held_table, values):
    return jnp.sum(jnp.where(held_table, values[None, :], 0), axis=1)


def activate(values, gain):
    scaled = values * lax.rsqrt(jnp.mean(values * values, axis=-1, keepdims=True) + 1e-06)
    return jax.nn.silu(scaled * gain)


def pack(first, second):
    n_slots, n_frames, n_rows, n_cols, ch = first.shape
    blocks = n_cols // CB

    def body(a_ref, b_ref, o_ref):
        for k, ref in enumerate((a_ref, b_ref)):
            for f in range(n_frames):
                for r in range(n_rows):
                    o_ref[r, k, f, :, 0] = ref[0, f, r].reshape(blocks, CB, ch)

    spec = pl.BlockSpec((1, n_frames, n_rows, n_cols, ch), lambda s: (s, 0, 0, 0, 0))
    return pl.pallas_call(
        body,
        grid=(n_slots,),
        in_specs=[spec, spec],
        out_specs=pl.BlockSpec(
            (n_rows, 2, n_frames, blocks, 1, CB, ch), lambda s: (0, 0, 0, 0, s, 0, 0)
        ),
        out_shape=jax.ShapeDtypeStruct(
            (n_rows, 2, n_frames, blocks, n_slots, CB, ch), first.dtype
        ),
        compiler_params=pltpu.CompilerParams(vmem_limit_bytes=32 << 20),
    )(first, second)


def permute(held, source, rotation, keep):
    n_groups, n_tiles, n_slots, cols, ch = held.shape

    def body(source_ref, rotation_ref, keep_ref, i_ref, o_ref):
        n = pl.program_id(0)
        by = rotation_ref[n]

        @pl.when(keep_ref[n] != 0)
        def _():
            def step(t, _):
                at = lax.rem(t + n_tiles - by, n_tiles)
                o_ref[0, t, 0] = i_ref[0, at, 0]
                return 0

            lax.fori_loop(0, n_tiles, step, 0, unroll=8)

        @pl.when(keep_ref[n] == 0)
        def _():
            o_ref[...] = jnp.zeros_like(o_ref)

    block = (1, n_tiles, 1, cols, ch)
    return pl.pallas_call(
        body,
        grid_spec=pltpu.PrefetchScalarGridSpec(
            num_scalar_prefetch=3,
            grid=(n_groups * n_slots,),
            in_specs=[
                pl.BlockSpec(
                    block,
                    lambda n, s, r, k: (lax.div(s[n], n_slots), 0, lax.rem(s[n], n_slots), 0, 0),
                )
            ],
            out_specs=pl.BlockSpec(
                block, lambda n, s, r, k: (lax.div(n, n_slots), 0, lax.rem(n, n_slots), 0, 0)
            ),
        ),
        out_shape=jax.ShapeDtypeStruct(held.shape, held.dtype),
        compiler_params=pltpu.CompilerParams(vmem_limit_bytes=32 << 20),
    )(source, rotation, keep, held)


def convolve(padded, weight, bias_vec):
    n_slots = padded.shape[0]
    n_rows = padded.shape[2] - 2
    n_cols = padded.shape[3]
    channels = padded.shape[4]
    widened = jnp.pad(padded, ((0, 0), (0, 0), (0, 0), (1, 1), (0, 0)))
    pieces = [
        widened[:, t_step, y_step : y_step + n_rows, x_step : x_step + n_cols, :]
        for t_step in range(3)
        for y_step in range(3)
        for x_step in range(3)
    ]
    patches = jnp.concatenate(pieces, axis=-1).reshape(-1, 27 * channels)
    result = (
        jnp.dot(
            patches, weight.reshape(27 * channels, channels), preferred_element_type=jnp.float32
        )
        + bias_vec
    )
    return result.reshape(n_slots, n_rows, n_cols, channels)


def local(
    frame_in,
    cache_first,
    cache_second,
    gain_first,
    gain_second,
    conv_first,
    conv_second,
    bias_first,
    bias_second,
    old_slot,
    new_slot,
    old_shift,
    new_shift,
    frame_count,
):
    n_slots, n_rows, n_cols, ch = frame_in.shape
    n_groups = lax.axis_size("stream")
    n_tiles = lax.axis_size("tile")
    my_group = lax.axis_index("stream")
    my_tile = lax.axis_index("tile")
    n_flight = old_slot.shape[0]
    blocks = n_cols // CB
    slot_ids = jnp.arange(n_flight, dtype=jnp.int32)
    held_new = new_slot[None, :] == slot_ids[:, None]
    source = lookup(held_new, old_slot)
    shift_after = lookup(held_new, new_shift)
    rotation = (shift_after - lookup(held_new, old_shift)) % n_tiles
    frames_done = lookup(held_new, frame_count)
    my_piece = my_group * n_tiles + my_tile
    my_frame = (my_piece // blocks) % 2
    keep = (frames_done >= 2 - my_frame).astype(jnp.int32)
    start = my_group * n_slots
    my_number = lax.dynamic_slice_in_dim((my_tile - shift_after) % n_tiles, start, n_slots)

    sent = pack(cache_first, cache_second).reshape(n_groups * n_tiles, n_slots, CB, ch)
    held = lax.all_to_all(sent, BOTH, 0, 0, tiled=True)
    moved = permute(held.reshape(n_groups, n_tiles, n_slots, CB, ch), source, rotation, keep)
    got = lax.all_to_all(
        moved.reshape(n_groups * n_tiles, n_slots, CB, ch), BOTH, 0, 0, tiled=True
    )
    got = got.reshape(n_rows, 2, 2, blocks, n_slots, CB, ch)

    down = [(i, (i + 1) % n_tiles) for i in range(n_tiles)]
    up = [((i + 1) % n_tiles, i) for i in range(n_tiles)]
    above = lax.ppermute(got[n_rows - 1], "tile", down)
    below = lax.ppermute(got[0], "tile", up)
    rows = jnp.concatenate([above[None], got, below[None]], axis=0)
    rows = rows.transpose(1, 4, 2, 0, 3, 5, 6).reshape(
        2, n_slots, 2, n_rows + 2, n_cols, ch
    )
    border = jnp.ones((n_slots, n_rows + 2), jnp.bfloat16)
    border = border.at[:, 0].set((my_number != 0).astype(jnp.bfloat16))
    border = border.at[:, -1].set((my_number != n_tiles - 1).astype(jnp.bfloat16))
    border = border[:, None, :, None, None]

    def conv_layer(kept, activation, weight, bias_vec):
        head = lax.ppermute(activation[:, -1:], "tile", down)
        tail = lax.ppermute(activation[:, :1], "tile", up)
        act = jnp.concatenate([head, activation, tail], axis=1)
        padded = jnp.concatenate([kept, act[:, None]], axis=1)
        return convolve(padded * border, weight, bias_vec)

    act_first = activate(frame_in.astype(jnp.float32), gain_first).astype(jnp.bfloat16)
    hidden = conv_layer(rows[0], act_first, conv_first, bias_first)
    act_second = activate(hidden, gain_second).astype(jnp.bfloat16)
    second_out = conv_layer(rows[1], act_second, conv_second, bias_second)
    mixed_frame = (second_out + frame_in.astype(jnp.float32)).astype(jnp.bfloat16)
    next_first = jnp.stack([rows[0, :, 1, 1:-1], act_first], axis=1)
    next_second = jnp.stack([rows[1, :, 1, 1:-1], act_second], axis=1)
    return (mixed_frame, next_first, next_second)


def solution(mesh):
    frame = P("stream", "tile", None, None)
    cache = P("stream", None, "tile", None, None)
    return jax.shard_map(
        local,
        mesh=mesh,
        in_specs=(frame, cache, cache) + (P(),) * 11,
        out_specs=(frame, cache, cache),
        check_vma=False,
    )
```

```python
import jax
import jax.numpy as jnp
from jax import lax
from jax.experimental import pallas as pl
from jax.experimental.pallas import tpu as pltpu
from jax.sharding import PartitionSpec as P

BOTH = ("stream", "tile")
CB = 8


def lookup(held_table, values):
    return jnp.sum(jnp.where(held_table, values[None, :], 0), axis=1)


def activate(values, gain):
    scaled = values * lax.rsqrt(jnp.mean(values * values, axis=-1, keepdims=True) + 1e-06)
    return jax.nn.silu(scaled * gain)


def pack(first, second):
    n_slots, n_frames, n_rows, n_cols, ch = first.shape
    blocks = n_cols // CB

    def body(a_ref, b_ref, o_ref):
        for k, ref in enumerate((a_ref, b_ref)):
            for f in range(n_frames):
                for r in range(n_rows):
                    o_ref[r, k, f, :, 0] = ref[0, f, r].reshape(blocks, CB, ch)

    spec = pl.BlockSpec((1, n_frames, n_rows, n_cols, ch), lambda s: (s, 0, 0, 0, 0))
    return pl.pallas_call(
        body,
        grid=(n_slots,),
        in_specs=[spec, spec],
        out_specs=pl.BlockSpec(
            (n_rows, 2, n_frames, blocks, 1, CB, ch), lambda s: (0, 0, 0, 0, s, 0, 0)
        ),
        out_shape=jax.ShapeDtypeStruct(
            (n_rows, 2, n_frames, blocks, n_slots, CB, ch), first.dtype
        ),
        compiler_params=pltpu.CompilerParams(vmem_limit_bytes=32 << 20),
    )(first, second)


def permute(held, source, rotation, keep):
    n_groups, n_tiles, n_slots, cols, ch = held.shape

    def body(source_ref, rotation_ref, keep_ref, i_ref, o_ref):
        n = pl.program_id(0)
        by = rotation_ref[n]

        @pl.when(keep_ref[n] != 0)
        def _():
            def step(t, _):
                at = lax.rem(t + n_tiles - by, n_tiles)
                o_ref[0, t, 0] = i_ref[0, at, 0]
                return 0

            lax.fori_loop(0, n_tiles, step, 0, unroll=8)

        @pl.when(keep_ref[n] == 0)
        def _():
            o_ref[...] = jnp.zeros_like(o_ref)

    block = (1, n_tiles, 1, cols, ch)
    return pl.pallas_call(
        body,
        grid_spec=pltpu.PrefetchScalarGridSpec(
            num_scalar_prefetch=3,
            grid=(n_groups * n_slots,),
            in_specs=[
                pl.BlockSpec(
                    block,
                    lambda n, s, r, k: (lax.div(s[n], n_slots), 0, lax.rem(s[n], n_slots), 0, 0),
                )
            ],
            out_specs=pl.BlockSpec(
                block, lambda n, s, r, k: (lax.div(n, n_slots), 0, lax.rem(n, n_slots), 0, 0)
            ),
        ),
        out_shape=jax.ShapeDtypeStruct(held.shape, held.dtype),
        compiler_params=pltpu.CompilerParams(vmem_limit_bytes=32 << 20),
    )(source, rotation, keep, held)


def spread(weight):
    n_t, n_y, n_x, ci, co = weight.shape

    def body(w_ref, o_ref):
        o_ref[0] = w_ref[0, 0, 0]

    return pl.pallas_call(
        body,
        grid=(n_t, n_y, n_x),
        in_specs=[pl.BlockSpec((1, 1, 1, ci, co), lambda t, y, x: (t, y, x, 0, 0))],
        out_specs=pl.BlockSpec((1, ci, co), lambda t, y, x: (t, y, x)),
        out_shape=jax.ShapeDtypeStruct((n_t, n_y * ci, n_x * co), weight.dtype),
        cost_estimate=pl.CostEstimate(
            flops=0, bytes_accessed=4 * weight.size, transcendentals=0
        ),
        compiler_params=pltpu.CompilerParams(vmem_limit_bytes=16 << 20),
    )(weight)


def conv_layer(which, got, above, below, act, act_above, act_below, weight, bias, extra, edges, normed):
    n_slots, n_rows, n_cols, ch = act.shape
    blocks = n_cols // CB
    wide = weight.shape[2]
    m_all = n_slots * n_rows * n_cols

    def body(edge_ref, got_ref, above_ref, below_ref, act_ref, aa_ref, ab_ref, w_ref, b_ref, x_ref, o_ref, next_ref, lhs, acc):
        t = pl.program_id(0)

        def place(s, row, value):
            for y in range(n_rows):
                dy = row - y
                if 0 <= dy <= 2:
                    m = (s * n_rows + y) * n_cols
                    lhs[m : m + n_cols, dy * ch : (dy + 1) * ch] = value

        def edge(s, k, value):
            return jnp.where(edge_ref[k, s] != 0, value, jnp.zeros_like(value))

        @pl.when(t < 2)
        def _():
            for s in range(n_slots):
                place(s, 0, edge(s, 0, above_ref[0, 0, :, s].reshape(n_cols, ch)))
                place(s, n_rows + 1, edge(s, 1, below_ref[0, 0, :, s].reshape(n_cols, ch)))
                for r in range(n_rows):
                    own = got_ref[r, 0, 0, :, s].reshape(n_cols, ch)
                    place(s, r + 1, own)
                    next_ref[s, 0, r] = own

        @pl.when(t == 2)
        def _():
            for s in range(n_slots):
                place(s, 0, edge(s, 0, aa_ref[s]))
                place(s, n_rows + 1, edge(s, 1, ab_ref[s]))
                for r in range(n_rows):
                    own = act_ref[s, r]
                    place(s, r + 1, own)
                    next_ref[s, 0, r] = own

        half = m_all // 2

        def product(k):
            rows = pl.ds(k * half, half)
            return rows, jnp.dot(lhs[rows], w_ref[0], preferred_element_type=jnp.float32)

        @pl.when(t == 0)
        def _():
            for k in range(2):
                rows, value = product(k)
                acc[rows] = value

        @pl.when(t > 0)
        def _():
            for k in range(2):
                rows, value = product(k)
                acc[rows] += value

        @pl.when(t == 2)
        def _():
            col = lax.broadcasted_iota(jnp.int32, (n_cols, ch), 0)
            for s in range(n_slots):
                for y in range(n_rows):
                    m = (s * n_rows + y) * n_cols
                    left = pltpu.roll(acc[m : m + n_cols, 0:ch], 1, 0)
                    right = pltpu.roll(acc[m : m + n_cols, 2 * ch : 3 * ch], n_cols - 1, 0)
                    total = acc[m : m + n_cols, ch : 2 * ch] + b_ref[...]
                    total += jnp.where(col == 0, 0.0, left)
                    total += jnp.where(col == n_cols - 1, 0.0, right)
                    if normed:
                        scaled = total * lax.rsqrt(
                            jnp.mean(total * total, axis=-1, keepdims=True) + 1e-06
                        )
                        u = scaled * x_ref[...]
                        o_ref[s, y] = (u / (1.0 + jnp.exp(-u))).astype(o_ref.dtype)
                    else:
                        o_ref[s, y] = (total + x_ref[s, y].astype(jnp.float32)).astype(o_ref.dtype)

    def whole(shape):
        return pl.BlockSpec(shape, lambda t, e, zeros=(0,) * len(shape): zeros)

    side = pl.BlockSpec(
        (1, 1, blocks, n_slots, CB, ch), lambda t, e: (which, jnp.minimum(t, 1), 0, 0, 0, 0)
    )
    return pl.pallas_call(
        body,
        grid_spec=pltpu.PrefetchScalarGridSpec(
            num_scalar_prefetch=1,
            grid=(3,),
            in_specs=[
                pl.BlockSpec(
                    (n_rows, 1, 1, blocks, n_slots, CB, ch),
                    lambda t, e: (0, which, jnp.minimum(t, 1), 0, 0, 0, 0),
                ),
                side,
                side,
                whole(act.shape),
                whole(act_above.shape),
                whole(act_below.shape),
                pl.BlockSpec((1,) + weight.shape[1:], lambda t, e: (t, 0, 0)),
                whole(bias.shape),
                whole(extra.shape),
            ],
            out_specs=[
                whole(act.shape),
                pl.BlockSpec(
                    (n_slots, 1, n_rows, n_cols, ch),
                    lambda t, e: (0, jnp.maximum(t - 1, 0), 0, 0, 0),
                ),
            ],
            scratch_shapes=[
                pltpu.VMEM((m_all, 3 * ch), jnp.bfloat16),
                pltpu.VMEM((m_all, wide), jnp.float32),
            ],
        ),
        out_shape=[
            jax.ShapeDtypeStruct(act.shape, jnp.bfloat16),
            jax.ShapeDtypeStruct((n_slots, 2) + act.shape[1:], jnp.bfloat16),
        ],
        cost_estimate=pl.CostEstimate(
            flops=2 * m_all * weight.size,
            bytes_accessed=2 * weight.size + 8 * act.size,
            transcendentals=act.size,
        ),
        compiler_params=pltpu.CompilerParams(vmem_limit_bytes=40 << 20),
    )(edges, got, above, below, act, act_above, act_below, weight, bias, extra)


def local(
    frame_in,
    cache_first,
    cache_second,
    gain_first,
    gain_second,
    conv_first,
    conv_second,
    bias_first,
    bias_second,
    old_slot,
    new_slot,
    old_shift,
    new_shift,
    frame_count,
):
    n_slots, n_rows, n_cols, ch = frame_in.shape
    n_groups = lax.axis_size("stream")
    n_tiles = lax.axis_size("tile")
    my_group = lax.axis_index("stream")
    my_tile = lax.axis_index("tile")
    n_flight = old_slot.shape[0]
    blocks = n_cols // CB
    slot_ids = jnp.arange(n_flight, dtype=jnp.int32)
    held_new = new_slot[None, :] == slot_ids[:, None]
    source = lookup(held_new, old_slot)
    shift_after = lookup(held_new, new_shift)
    rotation = (shift_after - lookup(held_new, old_shift)) % n_tiles
    frames_done = lookup(held_new, frame_count)
    my_piece = my_group * n_tiles + my_tile
    my_frame = (my_piece // blocks) % 2
    keep = (frames_done >= 2 - my_frame).astype(jnp.int32)
    start = my_group * n_slots
    my_number = lax.dynamic_slice_in_dim((my_tile - shift_after) % n_tiles, start, n_slots)

    sent = pack(cache_first, cache_second).reshape(n_groups * n_tiles, n_slots, CB, ch)
    held = lax.all_to_all(sent, BOTH, 0, 0, tiled=True)
    moved = permute(held.reshape(n_groups, n_tiles, n_slots, CB, ch), source, rotation, keep)
    got = lax.all_to_all(
        moved.reshape(n_groups * n_tiles, n_slots, CB, ch), BOTH, 0, 0, tiled=True
    )
    got = got.reshape(n_rows, 2, 2, blocks, n_slots, CB, ch)

    down = [(i, (i + 1) % n_tiles) for i in range(n_tiles)]
    up = [((i + 1) % n_tiles, i) for i in range(n_tiles)]
    above = lax.ppermute(got[n_rows - 1], "tile", down)
    below = lax.ppermute(got[0], "tile", up)
    edges = jnp.stack([my_number != 0, my_number != n_tiles - 1]).astype(jnp.int32)

    def sides(activation):
        return (
            lax.ppermute(activation[:, n_rows - 1], "tile", down),
            lax.ppermute(activation[:, 0], "tile", up),
        )

    wide_first = spread(conv_first)
    wide_second = spread(conv_second)
    act_first = activate(frame_in.astype(jnp.float32), gain_first).astype(jnp.bfloat16)
    act_second, next_first = conv_layer(
        0, got, above, below, act_first, *sides(act_first), wide_first,
        bias_first[None], gain_second[None], edges, True,
    )
    mixed_frame, next_second = conv_layer(
        1, got, above, below, act_second, *sides(act_second), wide_second,
        bias_second[None], frame_in, edges, False,
    )
    return (mixed_frame, next_first, next_second)


def solution(mesh):
    frame = P("stream", "tile", None, None)
    cache = P("stream", None, "tile", None, None)
    return jax.shard_map(
        local,
        mesh=mesh,
        in_specs=(frame, cache, cache) + (P(),) * 11,
        out_specs=(frame, cache, cache),
        check_vma=False,
    )
```

```python
import jax
import jax.numpy as jnp
from jax import lax
from jax.experimental import pallas as pl
from jax.experimental.pallas import tpu as pltpu
from jax.sharding import PartitionSpec as P

BOTH = ("stream", "tile")
CB = 8


def lookup(held_table, values):
    return jnp.sum(jnp.where(held_table, values[None, :], 0), axis=1)


def pack(first, second):
    n_slots, n_frames, n_rows, n_cols, ch = first.shape
    blocks = n_cols // CB

    def body(a_ref, b_ref, o_ref):
        for k, ref in enumerate((a_ref, b_ref)):
            for f in range(n_frames):
                for r in range(n_rows):
                    o_ref[r, k, f, :, 0] = ref[0, f, r].reshape(blocks, CB, ch)

    spec = pl.BlockSpec((1, n_frames, n_rows, n_cols, ch), lambda s: (s, 0, 0, 0, 0))
    return pl.pallas_call(
        body,
        grid=(n_slots,),
        in_specs=[spec, spec],
        out_specs=pl.BlockSpec(
            (n_rows, 2, n_frames, blocks, 1, CB, ch), lambda s: (0, 0, 0, 0, s, 0, 0)
        ),
        out_shape=jax.ShapeDtypeStruct(
            (n_rows, 2, n_frames, blocks, n_slots, CB, ch), first.dtype
        ),
        compiler_params=pltpu.CompilerParams(vmem_limit_bytes=32 << 20),
    )(first, second)


def permute(held, source, rotation, keep):
    n_groups, n_tiles, n_slots, cols, ch = held.shape

    def body(source_ref, rotation_ref, keep_ref, i_ref, o_ref):
        n = pl.program_id(0)
        by = rotation_ref[n]

        @pl.when(keep_ref[n] != 0)
        def _():
            def step(t, _):
                at = lax.rem(t + n_tiles - by, n_tiles)
                o_ref[0, t, 0] = i_ref[0, at, 0]
                return 0

            lax.fori_loop(0, n_tiles, step, 0, unroll=8)

        @pl.when(keep_ref[n] == 0)
        def _():
            o_ref[...] = jnp.zeros_like(o_ref)

    block = (1, n_tiles, 1, cols, ch)
    return pl.pallas_call(
        body,
        grid_spec=pltpu.PrefetchScalarGridSpec(
            num_scalar_prefetch=3,
            grid=(n_groups * n_slots,),
            in_specs=[
                pl.BlockSpec(
                    block,
                    lambda n, s, r, k: (lax.div(s[n], n_slots), 0, lax.rem(s[n], n_slots), 0, 0),
                )
            ],
            out_specs=pl.BlockSpec(
                block, lambda n, s, r, k: (lax.div(n, n_slots), 0, lax.rem(n, n_slots), 0, 0)
            ),
        ),
        out_shape=jax.ShapeDtypeStruct(held.shape, held.dtype),
        compiler_params=pltpu.CompilerParams(vmem_limit_bytes=32 << 20),
    )(source, rotation, keep, held)


VMEM_LIMIT = 40 << 20


def call(body, out_shape, operands, scalars=(), scratch=(), flops=0, moved=0, anywhere=()):
    in_specs = [pl.BlockSpec(memory_space=pltpu.SMEM) for _ in scalars]
    for k, _ in enumerate(operands):
        space = pl.ANY if k in anywhere else pltpu.VMEM
        in_specs.append(pl.BlockSpec(memory_space=space))
    return pl.pallas_call(
        body,
        in_specs=in_specs,
        out_specs=[pl.BlockSpec(memory_space=pltpu.VMEM) for _ in out_shape],
        out_shape=list(out_shape),
        scratch_shapes=list(scratch),
        cost_estimate=pl.CostEstimate(flops=flops, bytes_accessed=moved, transcendentals=0),
        compiler_params=pltpu.CompilerParams(vmem_limit_bytes=VMEM_LIMIT),
    )(*scalars, *operands)


def spread(weight):
    n_t, n_y, n_x, ci, co = weight.shape

    def body(w_ref, p_ref, a_ref):
        for x in range(n_x):
            for t in range(n_t - 1):
                p_ref[t * ci : (t + 1) * ci, x * co : (x + 1) * co] = w_ref[t, 0, x]
            a_ref[:, x * co : (x + 1) * co] = w_ref[n_t - 1, 0, x]

    return pl.pallas_call(
        body,
        grid=(n_y,),
        in_specs=[pl.BlockSpec((n_t, 1, n_x, ci, co), lambda y: (0, y, 0, 0, 0))],
        out_specs=[
            pl.BlockSpec(((n_t - 1) * ci, n_x * co), lambda y: (y, 0)),
            pl.BlockSpec((ci, n_x * co), lambda y: (y, 0)),
        ],
        out_shape=[
            jax.ShapeDtypeStruct((n_y * (n_t - 1) * ci, n_x * co), weight.dtype),
            jax.ShapeDtypeStruct((n_y * ci, n_x * co), weight.dtype),
        ],
        cost_estimate=pl.CostEstimate(flops=0, bytes_accessed=4 * weight.size, transcendentals=0),
        compiler_params=pltpu.CompilerParams(vmem_limit_bytes=24 << 20),
    )(weight)


def activated(values, gain):
    u = values * lax.rsqrt(jnp.mean(values * values, axis=-1, keepdims=True) + 1e-06) * gain
    return u / (1.0 + jnp.exp(-u))


def first_activation(frame, gain):
    n_slots, n_rows, n_cols, ch = frame.shape

    def body(f_ref, g_ref, o_ref, top_ref, bottom_ref):
        for s in range(n_slots):
            for r in range(n_rows):
                value = activated(f_ref[s, r].astype(jnp.float32), g_ref[...]).astype(jnp.bfloat16)
                o_ref[s, r] = value
                if r == 0:
                    top_ref[s] = value
                if r == n_rows - 1:
                    bottom_ref[s] = value

    row = jax.ShapeDtypeStruct((n_slots, n_cols, ch), jnp.bfloat16)
    return call(
        body,
        [jax.ShapeDtypeStruct(frame.shape, jnp.bfloat16), row, row],
        (frame, gain),
        flops=10 * frame.size,
        moved=6 * frame.size,
    )


def folded(acc, ch, cols_first):
    tiles = acc.shape[0] // CB
    n_slots = 4
    blocks = tiles // n_slots
    lead = (blocks, n_slots) if cols_first else (n_slots, blocks)
    axis = 0 if cols_first else 1

    def plane(k):
        value = acc[:, k * ch : (k + 1) * ch].reshape(tiles, CB, ch)
        return value

    at = lax.broadcasted_iota(jnp.int32, (1, 1, CB, ch), 2)
    before = pltpu.roll(plane(0), 1, 1).reshape(lead + (CB, ch))
    after = pltpu.roll(plane(2), CB - 1, 1).reshape(lead + (CB, ch))
    gap = list(lead) + [CB, ch]
    gap[axis] = 1
    gap = jnp.zeros(gap, jnp.float32)
    before_prev = jnp.concatenate([gap, lax.slice_in_dim(before, 0, blocks - 1, axis=axis)], axis)
    after_next = jnp.concatenate([lax.slice_in_dim(after, 1, blocks, axis=axis), gap], axis)
    total = plane(1).reshape(lead + (CB, ch))
    total += jnp.where(at == 0, before_prev, before)
    total += jnp.where(at == CB - 1, after_next, after)
    return total


def add_into(o_ref, y, total, cols_first, base=None):
    if cols_first:
        o_ref[y] = total if base is None else base[y] + total
        return
    for s in range(total.shape[0]):
        o_ref[y, :, s] = total[s] if base is None else base[y, :, s] + total[s]


def masked(edge_ref, k, s, value):
    return jnp.where(edge_ref[k, s] != 0, value, jnp.zeros_like(value))


def dot(a, b):
    return jnp.dot(a, b, preferred_element_type=jnp.float32)


def sums_shape(blocks, n_slots, n_rows, ch):
    return jax.ShapeDtypeStruct((n_rows, blocks, n_slots, CB, ch), jnp.float32)


def current_part(act, above, below, weight, edges):
    n_slots, n_rows, n_cols, ch = act.shape
    half = n_slots * n_cols

    def body(edge_ref, act_ref, above_ref, below_ref, w_ref, o_ref, lhs):
        for y in range(n_rows):
            for s in range(n_slots):
                m = s * n_cols
                rows = [masked(edge_ref, 0, s, above_ref[s])]
                rows += [act_ref[s, r] for r in range(n_rows)]
                rows += [masked(edge_ref, 1, s, below_ref[s])]
                for dy in range(3):
                    lhs[m : m + n_cols, dy * ch : (dy + 1) * ch] = rows[y + dy]
            add_into(o_ref, y, folded(dot(lhs[...], w_ref[...]), ch, False), False)

    return call(
        body,
        [sums_shape(n_cols // CB, n_slots, n_rows, ch)],
        (act, above, below, weight),
        scalars=(edges,),
        scratch=[pltpu.VMEM((half, 3 * ch), jnp.bfloat16)],
        flops=2 * n_rows * half * weight.size,
        moved=2 * weight.size + 8 * act.size,
    )[0]


def own_part(got, weights, sums):
    n_rows, n_caches, n_frames, blocks, n_slots, _, ch = got.shape
    half = blocks * n_slots * CB
    deep = n_frames * ch

    def body(got_ref, w0_ref, w1_ref, z_ref, o0_ref, o1_ref, w0, w1, lhs, sems):
        copies = []
        for k, (src, dst) in enumerate(((w0_ref, w0), (w1_ref, w1))):
            for d in range(3):
                rows = pl.ds(d * deep, deep)
                copies.append(pltpu.make_async_copy(src.at[rows], dst.at[rows], sems.at[3 * k + d]))
        for c in copies:
            c.start()
        for k, (w, o_ref, base) in enumerate(((w0, o0_ref, z_ref), (w1, o1_ref, None))):
            for r in range(n_rows):
                for f in range(n_frames):
                    lo = r * deep + f * ch
                    lhs[:, lo : lo + ch] = got_ref[r, k, f].reshape(half, ch)
            copies[3 * k].wait()
            copies[3 * k + 1].wait()
            add_into(o_ref, 1, folded(dot(lhs[...], w[0 : 2 * deep]), ch, True), True, base)
            copies[3 * k + 2].wait()
            add_into(o_ref, 0, folded(dot(lhs[...], w[deep : 3 * deep]), ch, True), True, base)

    out = sums_shape(blocks, n_slots, n_rows, ch)
    whole = weights[0]
    return call(
        body,
        [out, out],
        (got, *weights, sums),
        scratch=[
            pltpu.VMEM(whole.shape, whole.dtype),
            pltpu.VMEM(whole.shape, whole.dtype),
            pltpu.VMEM((half, n_rows * deep), jnp.bfloat16),
            pltpu.SemaphoreType.DMA((6,)),
        ],
        flops=2 * 4 * half * 2 * deep * whole.shape[1],
        moved=4 * whole.size,
        anywhere=(1, 2),
    )


def side_sums(edge_ref, k, side_ref, w, lhs):
    n_frames, blocks, n_slots, _, ch = side_ref.shape
    for s in range(n_slots):
        for f in range(n_frames):
            value = masked(edge_ref, k, s, side_ref[f, :, s])
            lhs[:, s, :, f * ch : (f + 1) * ch] = value
    half = blocks * n_slots * CB
    return folded(dot(lhs[...].reshape(half, n_frames * ch), w), ch, True)


def second_activation(above, below, weight, sums, bias, gain, edges):
    n_frames, blocks, n_slots, _, ch = above.shape
    n_rows, n_cols, deep = sums.shape[0], blocks * CB, n_frames * ch

    def body(edge_ref, above_ref, below_ref, w_ref, z_ref, b_ref, g_ref, o_ref, top_ref, bottom_ref, lhs, wv, sems):
        copies = [
            pltpu.make_async_copy(w_ref.at[pl.ds(2 * k * deep, deep)], wv.at[k], sems.at[k])
            for k in range(2)
        ]
        for c in copies:
            c.start()
        for y, side in enumerate((above_ref, below_ref)):
            copies[y].wait()
            total = side_sums(edge_ref, y, side, wv[y], lhs) + z_ref[y] + b_ref[...]
            for s in range(n_slots):
                value = activated(total[:, s].reshape(n_cols, ch), g_ref[...]).astype(jnp.bfloat16)
                o_ref[s, y] = value
                if y == 0:
                    top_ref[s] = value
                else:
                    bottom_ref[s] = value

    row = jax.ShapeDtypeStruct((n_slots, n_cols, ch), jnp.bfloat16)
    return call(
        body,
        [jax.ShapeDtypeStruct((n_slots, n_rows, n_cols, ch), jnp.bfloat16), row, row],
        (above, below, weight, sums, bias, gain),
        scalars=(edges,),
        scratch=[
            pltpu.VMEM((blocks, n_slots, CB, deep), jnp.bfloat16),
            pltpu.VMEM((2, deep, weight.shape[1]), weight.dtype),
            pltpu.SemaphoreType.DMA((2,)),
        ],
        flops=4 * n_slots * n_cols * deep * weight.shape[1],
        moved=4 * deep * weight.shape[1],
        anywhere=(2,),
    )


def before_sides(above, below, act, w_prior, w_act, sums, got, act_first, edges):
    n_frames, blocks, n_slots, _, ch = above.shape
    n_rows, n_cols, deep = sums.shape[0], blocks * CB, n_frames * ch

    def body(edge_ref, above_ref, below_ref, act_ref, w_ref, wa_ref, z_ref, got_ref, act1_ref, o_ref, n1_ref, n2_ref, lhs, lhs2, wv, wa, sems):
        copies = [pltpu.make_async_copy(wa_ref, wa, sems.at[2])]
        copies += [
            pltpu.make_async_copy(w_ref.at[pl.ds(2 * k * deep, deep)], wv.at[k], sems.at[k])
            for k in range(2)
        ]
        for c in copies:
            c.start()
        for s in range(n_slots):
            for r in range(n_rows):
                own = act_ref[s, r]
                lhs2[s * n_cols : (s + 1) * n_cols, r * ch : (r + 1) * ch] = own
                n2_ref[s, 1, r] = own
                n1_ref[s, 1, r] = act1_ref[s, r]
                n1_ref[s, 0, r] = got_ref[r, 0, 1, :, s].reshape(n_cols, ch)
                n2_ref[s, 0, r] = got_ref[r, 1, 1, :, s].reshape(n_cols, ch)
        copies[0].wait()
        for y in range(n_rows):
            lo = (1 - y) * ch
            add_into(o_ref, y, folded(dot(lhs2[...], wa[lo : lo + 2 * ch]), ch, False), False, z_ref)
        for y, side in enumerate((above_ref, below_ref)):
            copies[1 + y].wait()
            o_ref[y] += side_sums(edge_ref, y, side, wv[y], lhs)

    nxt = jax.ShapeDtypeStruct((n_slots, 2, n_rows, n_cols, ch), jnp.bfloat16)
    return call(
        body,
        [jax.ShapeDtypeStruct(sums.shape, jnp.float32), nxt, nxt],
        (above, below, act, w_prior, w_act, sums, got, act_first),
        scalars=(edges,),
        scratch=[
            pltpu.VMEM((blocks, n_slots, CB, deep), jnp.bfloat16),
            pltpu.VMEM((n_slots * n_cols, 2 * ch), jnp.bfloat16),
            pltpu.VMEM((2, deep, w_prior.shape[1]), w_prior.dtype),
            pltpu.VMEM(w_act.shape, w_act.dtype),
            pltpu.SemaphoreType.DMA((3,)),
        ],
        flops=8 * n_slots * n_cols * deep * w_prior.shape[1],
        moved=4 * deep * w_prior.shape[1],
        anywhere=(3, 4),
    )


def last_part(above, below, w_act, sums, bias, frame, edges):
    n_slots, n_rows, n_cols, ch = frame.shape

    def body(edge_ref, above_ref, below_ref, w_ref, z_ref, b_ref, f_ref, o_ref, lhs, wv, sems):
        copies = [
            pltpu.make_async_copy(w_ref.at[pl.ds(2 * k * ch, ch)], wv.at[k], sems.at[k])
            for k in range(2)
        ]
        for c in copies:
            c.start()
        for y, side in enumerate((above_ref, below_ref)):
            for s in range(n_slots):
                lhs[s * n_cols : (s + 1) * n_cols] = masked(edge_ref, y, s, side[s])
            copies[y].wait()
            total = folded(dot(lhs[...], wv[y]), ch, False)
            for s in range(n_slots):
                value = (total[s] + z_ref[y, :, s] + b_ref[...]).reshape(n_cols, ch)
                o_ref[s, y] = (value + f_ref[s, y].astype(jnp.float32)).astype(jnp.bfloat16)

    return call(
        body,
        [jax.ShapeDtypeStruct(frame.shape, jnp.bfloat16)],
        (above, below, w_act, sums, bias, frame),
        scalars=(edges,),
        scratch=[
            pltpu.VMEM((n_slots * n_cols, ch), jnp.bfloat16),
            pltpu.VMEM((2, ch, w_act.shape[1]), w_act.dtype),
            pltpu.SemaphoreType.DMA((2,)),
        ],
        flops=4 * n_slots * n_cols * ch * w_act.shape[1],
        moved=4 * ch * w_act.shape[1],
        anywhere=(2,),
    )[0]


def local(
    frame_in,
    cache_first,
    cache_second,
    gain_first,
    gain_second,
    conv_first,
    conv_second,
    bias_first,
    bias_second,
    old_slot,
    new_slot,
    old_shift,
    new_shift,
    frame_count,
):
    n_slots, n_rows, n_cols, ch = frame_in.shape
    n_groups = lax.axis_size("stream")
    n_tiles = lax.axis_size("tile")
    my_group = lax.axis_index("stream")
    my_tile = lax.axis_index("tile")
    n_flight = old_slot.shape[0]
    blocks = n_cols // CB
    slot_ids = jnp.arange(n_flight, dtype=jnp.int32)
    held_new = new_slot[None, :] == slot_ids[:, None]
    source = lookup(held_new, old_slot)
    shift_after = lookup(held_new, new_shift)
    rotation = (shift_after - lookup(held_new, old_shift)) % n_tiles
    frames_done = lookup(held_new, frame_count)
    my_piece = my_group * n_tiles + my_tile
    my_frame = (my_piece // blocks) % 2
    keep = (frames_done >= 2 - my_frame).astype(jnp.int32)
    start = my_group * n_slots
    my_number = lax.dynamic_slice_in_dim((my_tile - shift_after) % n_tiles, start, n_slots)

    edges = jnp.stack([my_number != 0, my_number != n_tiles - 1]).astype(jnp.int32)
    down = [(i, (i + 1) % n_tiles) for i in range(n_tiles)]
    up = [((i + 1) % n_tiles, i) for i in range(n_tiles)]

    def from_above(row):
        return lax.ppermute(row, "tile", down)

    def from_below(row):
        return lax.ppermute(row, "tile", up)

    sent = pack(cache_first, cache_second).reshape(n_groups * n_tiles, n_slots, CB, ch)
    held = lax.all_to_all(sent, BOTH, 0, 0, tiled=True)

    w_prior_1, w_act_1 = spread(conv_first)
    w_prior_2, w_act_2 = spread(conv_second)
    act_first, top, bottom = first_activation(frame_in, gain_first[None])
    sums_1 = current_part(act_first, from_above(bottom), from_below(top), w_act_1, edges)
    held, sums_1, w_prior_1, w_prior_2, w_act_2 = lax.optimization_barrier(
        (held, sums_1, w_prior_1, w_prior_2, w_act_2)
    )

    moved = permute(held.reshape(n_groups, n_tiles, n_slots, CB, ch), source, rotation, keep)
    got = lax.all_to_all(
        moved.reshape(n_groups * n_tiles, n_slots, CB, ch), BOTH, 0, 0, tiled=True
    )
    got = got.reshape(n_rows, 2, 2, blocks, n_slots, CB, ch)

    above_1 = from_above(got[n_rows - 1, 0])
    below_1 = from_below(got[0, 0])
    above_2 = from_above(got[n_rows - 1, 1])
    below_2 = from_below(got[0, 1])
    sums_1, sums_2 = own_part(got, (w_prior_1, w_prior_2), sums_1)
    act_second, top, bottom = second_activation(
        above_1, below_1, w_prior_1, sums_1, bias_first[None], gain_second[None], edges
    )
    side_above, side_below = from_above(bottom), from_below(top)
    sums_2, next_first, next_second = before_sides(
        above_2, below_2, act_second, w_prior_2, w_act_2, sums_2, got, act_first, edges
    )
    mixed_frame = last_part(
        side_above, side_below, w_act_2, sums_2, bias_second[None], frame_in, edges
    )
    return (mixed_frame, next_first, next_second)


def solution(mesh):
    frame = P("stream", "tile", None, None)
    cache = P("stream", None, "tile", None, None)
    return jax.shard_map(
        local,
        mesh=mesh,
        in_specs=(frame, cache, cache) + (P(),) * 11,
        out_specs=(frame, cache, cache),
        check_vma=False,
    )
```

```python
import jax
import jax.numpy as jnp
from jax import lax
from jax.experimental import pallas as pl
from jax.experimental.pallas import tpu as pltpu
from jax.sharding import PartitionSpec as P

BOTH = ("stream", "tile")
CB = 8


def lookup(held_table, values):
    return jnp.sum(jnp.where(held_table, values[None, :], 0), axis=1)


def pack(first, second):
    n_slots, n_frames, n_rows, n_cols, ch = first.shape
    blocks = n_cols // CB

    def body(a_ref, b_ref, o_ref):
        for k, ref in enumerate((a_ref, b_ref)):
            for f in range(n_frames):
                for r in range(n_rows):
                    o_ref[r, k, f, :, 0] = ref[0, f, r].reshape(blocks, CB, ch)

    spec = pl.BlockSpec((1, n_frames, n_rows, n_cols, ch), lambda s: (s, 0, 0, 0, 0))
    return pl.pallas_call(
        body,
        grid=(n_slots,),
        in_specs=[spec, spec],
        out_specs=pl.BlockSpec(
            (n_rows, 2, n_frames, blocks, 1, CB, ch), lambda s: (0, 0, 0, 0, s, 0, 0)
        ),
        out_shape=jax.ShapeDtypeStruct(
            (n_rows, 2, n_frames, blocks, n_slots, CB, ch), first.dtype
        ),
        compiler_params=pltpu.CompilerParams(vmem_limit_bytes=58 << 20),
    )(first, second)


def permute(held, source, rotation, keep):
    n_groups, n_tiles, n_slots, cols, ch = held.shape

    def body(source_ref, rotation_ref, keep_ref, i_ref, o_ref):
        n = pl.program_id(0)
        by = rotation_ref[n]

        @pl.when(keep_ref[n] != 0)
        def _():
            def step(t, _):
                at = lax.rem(t + n_tiles - by, n_tiles)
                o_ref[0, t, 0] = i_ref[0, at, 0]
                return 0

            lax.fori_loop(0, n_tiles, step, 0, unroll=8)

        @pl.when(keep_ref[n] == 0)
        def _():
            o_ref[...] = jnp.zeros_like(o_ref)

    block = (1, n_tiles, 1, cols, ch)
    return pl.pallas_call(
        body,
        grid_spec=pltpu.PrefetchScalarGridSpec(
            num_scalar_prefetch=3,
            grid=(n_groups * n_slots,),
            in_specs=[
                pl.BlockSpec(
                    block,
                    lambda n, s, r, k: (lax.div(s[n], n_slots), 0, lax.rem(s[n], n_slots), 0, 0),
                )
            ],
            out_specs=pl.BlockSpec(
                block, lambda n, s, r, k: (lax.div(n, n_slots), 0, lax.rem(n, n_slots), 0, 0)
            ),
        ),
        out_shape=jax.ShapeDtypeStruct(held.shape, held.dtype),
        compiler_params=pltpu.CompilerParams(vmem_limit_bytes=32 << 20),
    )(source, rotation, keep, held)


VMEM_LIMIT = 24 << 20


def call(body, out_shape, operands, scalars=(), scratch=(), flops=0, moved=0):
    in_specs = [pl.BlockSpec(memory_space=pltpu.SMEM) for _ in scalars]
    in_specs += [pl.BlockSpec(memory_space=pltpu.VMEM) for _ in operands]
    return pl.pallas_call(
        body,
        in_specs=in_specs,
        out_specs=[pl.BlockSpec(memory_space=pltpu.VMEM) for _ in out_shape],
        out_shape=list(out_shape),
        scratch_shapes=list(scratch),
        cost_estimate=pl.CostEstimate(flops=flops, bytes_accessed=moved, transcendentals=0),
        compiler_params=pltpu.CompilerParams(vmem_limit_bytes=VMEM_LIMIT),
    )(*scalars, *operands)


def spread(weight):
    n_t, n_y, n_x, ci, co = weight.shape
    wide = n_x * co
    past = n_t - 1

    def body(w_ref, po_ref, ps_ref, ao_ref, as_ref):
        dy = pl.program_id(0)

        def at(t, x):
            return w_ref[t, 0, x]

        def side(y):
            for x in range(n_x):
                cols = slice(x * co, (x + 1) * co)
                for t in range(past):
                    ps_ref[y, t * ci : (t + 1) * ci, cols] = at(t, x)
                as_ref[y, :, cols] = at(past, x)

        def own(row, y):
            for x in range(n_x):
                cols = slice(y * wide + x * co, y * wide + (x + 1) * co)
                for t in range(past):
                    lo = (row * past + t) * ci
                    po_ref[lo : lo + ci, cols] = at(t, x)
                ao_ref[row * ci : (row + 1) * ci, cols] = at(past, x)

        @pl.when(dy == 0)
        def _():
            side(0)
            own(0, 1)

        @pl.when(dy == 1)
        def _():
            own(0, 0)
            own(1, 1)

        @pl.when(dy == 2)
        def _():
            side(1)
            own(1, 0)

    shapes = [(2 * past * ci, 2 * wide), (2, past * ci, wide), (2 * ci, 2 * wide), (2, ci, wide)]
    return pl.pallas_call(
        body,
        grid=(n_y,),
        in_specs=[pl.BlockSpec((n_t, 1, n_x, ci, co), lambda y: (0, y, 0, 0, 0))],
        out_specs=[
            pl.BlockSpec(shape, lambda y, zeros=(0,) * len(shape): zeros) for shape in shapes
        ],
        out_shape=[jax.ShapeDtypeStruct(shape, weight.dtype) for shape in shapes],
        cost_estimate=pl.CostEstimate(flops=0, bytes_accessed=5 * weight.size, transcendentals=0),
        compiler_params=pltpu.CompilerParams(vmem_limit_bytes=40 << 20),
    )(weight)


def activated(values, gain):
    u = values * lax.rsqrt(jnp.mean(values * values, axis=-1, keepdims=True) + 1e-06) * gain
    return u / (1.0 + jnp.exp(-u))


def first_activation(frame, gain):
    n_slots, n_rows, n_cols, ch = frame.shape

    def body(f_ref, g_ref, o_ref, top_ref, bottom_ref):
        for s in range(n_slots):
            for r in range(n_rows):
                value = activated(f_ref[s, r].astype(jnp.float32), g_ref[...]).astype(jnp.bfloat16)
                o_ref[s, r] = value
                if r == 0:
                    top_ref[s] = value
                if r == n_rows - 1:
                    bottom_ref[s] = value

    row = jax.ShapeDtypeStruct((n_slots, n_cols, ch), jnp.bfloat16)
    return call(
        body,
        [jax.ShapeDtypeStruct(frame.shape, jnp.bfloat16), row, row],
        (frame, gain),
        flops=10 * frame.size,
        moved=6 * frame.size,
    )


def folded(acc, ch, cols_first):
    tiles = acc.shape[0] // CB
    n_slots = 4
    blocks = tiles // n_slots
    lead = (blocks, n_slots) if cols_first else (n_slots, blocks)
    axis = 0 if cols_first else 1

    def plane(k):
        value = acc[:, k * ch : (k + 1) * ch].reshape(tiles, CB, ch)
        return value

    at = lax.broadcasted_iota(jnp.int32, (1, 1, CB, ch), 2)
    before = pltpu.roll(plane(0), 1, 1).reshape(lead + (CB, ch))
    after = pltpu.roll(plane(2), CB - 1, 1).reshape(lead + (CB, ch))
    gap = list(lead) + [CB, ch]
    gap[axis] = 1
    gap = jnp.zeros(gap, jnp.float32)
    before_prev = jnp.concatenate([gap, lax.slice_in_dim(before, 0, blocks - 1, axis=axis)], axis)
    after_next = jnp.concatenate([lax.slice_in_dim(after, 1, blocks, axis=axis), gap], axis)
    total = plane(1).reshape(lead + (CB, ch))
    total += jnp.where(at == 0, before_prev, before)
    total += jnp.where(at == CB - 1, after_next, after)
    return total


def add_into(o_ref, y, total, cols_first, base=None):
    if cols_first:
        o_ref[y] = total if base is None else base[y] + total
        return
    for s in range(total.shape[0]):
        o_ref[y, :, s] = total[s] if base is None else base[y, :, s] + total[s]


def masked(edge_ref, k, s, value):
    return jnp.where(edge_ref[k, s] != 0, value, jnp.zeros_like(value))


def dot(a, b):
    return jnp.dot(a, b, preferred_element_type=jnp.float32)


def sums_shape(blocks, n_slots, n_rows, ch):
    return jax.ShapeDtypeStruct((n_rows, blocks, n_slots, CB, ch), jnp.float32)


def add_sides(edge_ref, sides, w_ref, lhs, o_ref):
    n_slots, n_cols, ch = sides[0].shape
    for y, side in enumerate(sides):
        for s in range(n_slots):
            lhs[s * n_cols : (s + 1) * n_cols] = masked(edge_ref, y, s, side[s])
        add_into(o_ref, y, folded(dot(lhs[...], w_ref[y]), ch, False), False, o_ref)


def add_own(act_ref, w_ref, lhs, o_ref, base):
    n_slots, n_rows, n_cols, ch = act_ref.shape
    for s in range(n_slots):
        for r in range(n_rows):
            lhs[s * n_cols : (s + 1) * n_cols, r * ch : (r + 1) * ch] = act_ref[s, r]
    both = dot(lhs[...], w_ref[...])
    wide = both.shape[1] // 2
    for y in range(n_rows):
        add_into(o_ref, y, folded(both[:, y * wide : (y + 1) * wide], ch, False), False, base)


def current_part(act, above, below, w_own, w_sides, edges):
    n_slots, n_rows, n_cols, ch = act.shape
    half = n_slots * n_cols

    def body(edge_ref, act_ref, above_ref, below_ref, wo_ref, ws_ref, o_ref, lhs, side):
        add_own(act_ref, wo_ref, lhs, o_ref, None)
        add_sides(edge_ref, (above_ref, below_ref), ws_ref, side, o_ref)

    return call(
        body,
        [sums_shape(n_cols // CB, n_slots, n_rows, ch)],
        (act, above, below, w_own, w_sides),
        scalars=(edges,),
        scratch=[
            pltpu.VMEM((half, n_rows * ch), jnp.bfloat16),
            pltpu.VMEM((half, ch), jnp.bfloat16),
        ],
        flops=2 * half * (w_own.size + w_sides.size),
        moved=2 * w_own.size + 8 * act.size,
    )[0]


def own_part(got, weights, sums):
    n_rows, n_caches, n_frames, blocks, n_slots, _, ch = got.shape
    half = blocks * n_slots * CB
    deep = n_frames * ch

    def body(got_ref, w0_ref, w1_ref, z_ref, o0_ref, o1_ref, lhs):
        for k, (w, o_ref, base) in enumerate(((w0_ref, o0_ref, z_ref), (w1_ref, o1_ref, None))):
            for r in range(n_rows):
                for f in range(n_frames):
                    lo = r * deep + f * ch
                    lhs[:, lo : lo + ch] = got_ref[r, k, f].reshape(half, ch)
            both = dot(lhs[...], w[...])
            wide = both.shape[1] // 2
            for y in range(n_rows):
                total = folded(both[:, y * wide : (y + 1) * wide], ch, True)
                add_into(o_ref, y, total, True, base)

    out = sums_shape(blocks, n_slots, n_rows, ch)
    whole = weights[0]
    return call(
        body,
        [out, out],
        (got, *weights, sums),
        scratch=[pltpu.VMEM((half, n_rows * deep), jnp.bfloat16)],
        flops=4 * half * whole.size,
        moved=4 * whole.size,
    )


def side_sums(edge_ref, k, side_ref, w, lhs):
    n_frames, blocks, n_slots, _, ch = side_ref.shape
    for s in range(n_slots):
        for f in range(n_frames):
            value = masked(edge_ref, k, s, side_ref[f, :, s])
            lhs[:, s, :, f * ch : (f + 1) * ch] = value
    half = blocks * n_slots * CB
    return folded(dot(lhs[...].reshape(half, n_frames * ch), w), ch, True)


def second_activation(above, below, w_sides, sums, bias, gain, edges):
    n_frames, blocks, n_slots, _, ch = above.shape
    n_rows, n_cols, deep = sums.shape[0], blocks * CB, n_frames * ch

    def body(edge_ref, above_ref, below_ref, w_ref, z_ref, b_ref, g_ref, o_ref, top_ref, bottom_ref, lhs):
        for y, side in enumerate((above_ref, below_ref)):
            total = side_sums(edge_ref, y, side, w_ref[y], lhs) + z_ref[y] + b_ref[...]
            for s in range(n_slots):
                value = activated(total[:, s].reshape(n_cols, ch), g_ref[...]).astype(jnp.bfloat16)
                o_ref[s, y] = value
                if y == 0:
                    top_ref[s] = value
                else:
                    bottom_ref[s] = value

    row = jax.ShapeDtypeStruct((n_slots, n_cols, ch), jnp.bfloat16)
    return call(
        body,
        [jax.ShapeDtypeStruct((n_slots, n_rows, n_cols, ch), jnp.bfloat16), row, row],
        (above, below, w_sides, sums, bias, gain),
        scalars=(edges,),
        scratch=[pltpu.VMEM((blocks, n_slots, CB, deep), jnp.bfloat16)],
        flops=2 * n_slots * n_cols * w_sides.size,
        moved=2 * w_sides.size,
    )


def before_sides(above, below, act, w_sides, w_act, sums, got, act_first, edges):
    n_frames, blocks, n_slots, _, ch = above.shape
    n_rows, n_cols, deep = sums.shape[0], blocks * CB, n_frames * ch

    def body(edge_ref, above_ref, below_ref, act_ref, w_ref, wa_ref, z_ref, got_ref, act1_ref, o_ref, n1_ref, n2_ref, lhs, lhs2):
        add_own(act_ref, wa_ref, lhs2, o_ref, z_ref)
        for y, side in enumerate((above_ref, below_ref)):
            o_ref[y] += side_sums(edge_ref, y, side, w_ref[y], lhs)
        for s in range(n_slots):
            for r in range(n_rows):
                n2_ref[s, 1, r] = act_ref[s, r]
                n1_ref[s, 1, r] = act1_ref[s, r]
                n1_ref[s, 0, r] = got_ref[r, 0, 1, :, s].reshape(n_cols, ch)
                n2_ref[s, 0, r] = got_ref[r, 1, 1, :, s].reshape(n_cols, ch)

    nxt = jax.ShapeDtypeStruct((n_slots, 2, n_rows, n_cols, ch), jnp.bfloat16)
    return call(
        body,
        [jax.ShapeDtypeStruct(sums.shape, jnp.float32), nxt, nxt],
        (above, below, act, w_sides, w_act, sums, got, act_first),
        scalars=(edges,),
        scratch=[
            pltpu.VMEM((blocks, n_slots, CB, deep), jnp.bfloat16),
            pltpu.VMEM((n_slots * n_cols, n_rows * ch), jnp.bfloat16),
        ],
        flops=2 * n_slots * n_cols * (w_sides.size + w_act.size),
        moved=2 * (w_sides.size + w_act.size),
    )


def last_part(above, below, w_sides, sums, bias, frame, edges):
    n_slots, n_rows, n_cols, ch = frame.shape

    def body(edge_ref, above_ref, below_ref, w_ref, z_ref, b_ref, f_ref, o_ref, lhs):
        for y, side in enumerate((above_ref, below_ref)):
            for s in range(n_slots):
                lhs[s * n_cols : (s + 1) * n_cols] = masked(edge_ref, y, s, side[s])
            total = folded(dot(lhs[...], w_ref[y]), ch, False)
            for s in range(n_slots):
                value = (total[s] + z_ref[y, :, s] + b_ref[...]).reshape(n_cols, ch)
                o_ref[s, y] = (value + f_ref[s, y].astype(jnp.float32)).astype(jnp.bfloat16)

    return call(
        body,
        [jax.ShapeDtypeStruct(frame.shape, jnp.bfloat16)],
        (above, below, w_sides, sums, bias, frame),
        scalars=(edges,),
        scratch=[pltpu.VMEM((n_slots * n_cols, ch), jnp.bfloat16)],
        flops=2 * n_slots * n_cols * w_sides.size,
        moved=2 * w_sides.size,
    )[0]


def local(
    frame_in,
    cache_first,
    cache_second,
    gain_first,
    gain_second,
    conv_first,
    conv_second,
    bias_first,
    bias_second,
    old_slot,
    new_slot,
    old_shift,
    new_shift,
    frame_count,
):
    n_slots, n_rows, n_cols, ch = frame_in.shape
    n_groups = lax.axis_size("stream")
    n_tiles = lax.axis_size("tile")
    my_group = lax.axis_index("stream")
    my_tile = lax.axis_index("tile")
    n_flight = old_slot.shape[0]
    blocks = n_cols // CB
    slot_ids = jnp.arange(n_flight, dtype=jnp.int32)
    held_new = new_slot[None, :] == slot_ids[:, None]
    source = lookup(held_new, old_slot)
    shift_after = lookup(held_new, new_shift)
    rotation = (shift_after - lookup(held_new, old_shift)) % n_tiles
    frames_done = lookup(held_new, frame_count)
    my_piece = my_group * n_tiles + my_tile
    my_frame = (my_piece // blocks) % 2
    keep = (frames_done >= 2 - my_frame).astype(jnp.int32)
    start = my_group * n_slots
    my_number = lax.dynamic_slice_in_dim((my_tile - shift_after) % n_tiles, start, n_slots)

    edges = jnp.stack([my_number != 0, my_number != n_tiles - 1]).astype(jnp.int32)
    down = [(i, (i + 1) % n_tiles) for i in range(n_tiles)]
    up = [((i + 1) % n_tiles, i) for i in range(n_tiles)]

    def from_above(row):
        return lax.ppermute(row, "tile", down)

    def from_below(row):
        return lax.ppermute(row, "tile", up)

    sent = pack(cache_first, cache_second).reshape(n_groups * n_tiles, n_slots, CB, ch)
    held = lax.all_to_all(sent, BOTH, 0, 0, tiled=True)

    own_1, sides_1, act_own_1, act_sides_1 = spread(conv_first)
    own_2, sides_2, act_own_2, act_sides_2 = spread(conv_second)
    act_first, top, bottom = first_activation(frame_in, gain_first[None])
    act_above, act_below = from_above(bottom), from_below(top)
    held, act_first, own_1, own_2 = lax.optimization_barrier((held, act_first, own_1, own_2))

    moved = permute(held.reshape(n_groups, n_tiles, n_slots, CB, ch), source, rotation, keep)
    moved, act_later = lax.optimization_barrier((moved, act_first))
    got = lax.all_to_all(
        moved.reshape(n_groups * n_tiles, n_slots, CB, ch), BOTH, 0, 0, tiled=True
    )
    sums_1 = current_part(act_later, act_above, act_below, act_own_1, act_sides_1, edges)
    got, sums_1 = lax.optimization_barrier((got, sums_1))
    got = got.reshape(n_rows, 2, 2, blocks, n_slots, CB, ch)

    above_1 = from_above(got[n_rows - 1, 0])
    below_1 = from_below(got[0, 0])
    above_2 = from_above(got[n_rows - 1, 1])
    below_2 = from_below(got[0, 1])
    sums_1, sums_2 = own_part(got, (own_1, own_2), sums_1)
    act_second, top, bottom = second_activation(
        above_1, below_1, sides_1, sums_1, bias_first[None], gain_second[None], edges
    )
    side_above, side_below = from_above(bottom), from_below(top)
    sums_2, next_first, next_second = before_sides(
        above_2, below_2, act_second, sides_2, act_own_2, sums_2, got, act_first, edges
    )
    mixed_frame = last_part(
        side_above, side_below, act_sides_2, sums_2, bias_second[None], frame_in, edges
    )
    return (mixed_frame, next_first, next_second)


def solution(mesh):
    frame = P("stream", "tile", None, None)
    cache = P("stream", None, "tile", None, None)
    return jax.shard_map(
        local,
        mesh=mesh,
        in_specs=(frame, cache, cache) + (P(),) * 11,
        out_specs=(frame, cache, cache),
        check_vma=False,
    )
```

```python
import jax
import jax.numpy as jnp
from jax import lax
from jax.experimental import pallas as pl
from jax.experimental.pallas import tpu as pltpu
from jax.sharding import PartitionSpec as P

BOTH = ("stream", "tile")
CB = 8


def lookup(held_table, values):
    return jnp.sum(jnp.where(held_table, values[None, :], 0), axis=1)


def pack(first, second):
    n_slots, n_frames, n_rows, n_cols, ch = first.shape
    blocks = n_cols // CB

    def body(a_ref, b_ref, o_ref):
        for k, ref in enumerate((a_ref, b_ref)):
            for f in range(n_frames):
                for r in range(n_rows):
                    o_ref[r, k, f, :, 0] = ref[0, f, r].reshape(blocks, CB, ch)

    spec = pl.BlockSpec((1, n_frames, n_rows, n_cols, ch), lambda s: (s, 0, 0, 0, 0))
    return pl.pallas_call(
        body,
        grid=(n_slots,),
        in_specs=[spec, spec],
        out_specs=pl.BlockSpec(
            (n_rows, 2, n_frames, blocks, 1, CB, ch), lambda s: (0, 0, 0, 0, s, 0, 0)
        ),
        out_shape=jax.ShapeDtypeStruct(
            (n_rows, 2, n_frames, blocks, n_slots, CB, ch), first.dtype
        ),
        compiler_params=pltpu.CompilerParams(vmem_limit_bytes=58 << 20),
    )(first, second)


def permute(held, source, rotation, keep):
    n_groups, n_tiles, n_slots, cols, ch = held.shape

    def body(source_ref, rotation_ref, keep_ref, i_ref, o_ref):
        n = pl.program_id(0)
        by = rotation_ref[n]

        @pl.when(keep_ref[n] != 0)
        def _():
            def step(t, _):
                at = lax.rem(t + n_tiles - by, n_tiles)
                o_ref[0, t, 0] = i_ref[0, at, 0]
                return 0

            lax.fori_loop(0, n_tiles, step, 0, unroll=8)

        @pl.when(keep_ref[n] == 0)
        def _():
            o_ref[...] = jnp.zeros_like(o_ref)

    block = (1, n_tiles, 1, cols, ch)
    return pl.pallas_call(
        body,
        grid_spec=pltpu.PrefetchScalarGridSpec(
            num_scalar_prefetch=3,
            grid=(n_groups * n_slots,),
            in_specs=[
                pl.BlockSpec(
                    block,
                    lambda n, s, r, k: (lax.div(s[n], n_slots), 0, lax.rem(s[n], n_slots), 0, 0),
                )
            ],
            out_specs=pl.BlockSpec(
                block, lambda n, s, r, k: (lax.div(n, n_slots), 0, lax.rem(n, n_slots), 0, 0)
            ),
        ),
        out_shape=jax.ShapeDtypeStruct(held.shape, held.dtype),
        compiler_params=pltpu.CompilerParams(vmem_limit_bytes=58 << 20),
    )(source, rotation, keep, held)


VMEM_LIMIT = 36 << 20


def call(body, out_shape, operands, scalars=(), scratch=(), flops=0, moved=0, far=(), far_out=(), aliases=None):
    in_specs = [pl.BlockSpec(memory_space=pltpu.SMEM) for _ in scalars]
    for k, _ in enumerate(operands):
        in_specs.append(pl.BlockSpec(memory_space=pl.ANY if k in far else pltpu.VMEM))
    out_specs = []
    for k, _ in enumerate(out_shape):
        out_specs.append(pl.BlockSpec(memory_space=pl.ANY if k in far_out else pltpu.VMEM))
    return pl.pallas_call(
        body,
        in_specs=in_specs,
        out_specs=out_specs,
        out_shape=list(out_shape),
        scratch_shapes=list(scratch),
        input_output_aliases=aliases or {},
        cost_estimate=pl.CostEstimate(flops=flops, bytes_accessed=moved, transcendentals=0),
        compiler_params=pltpu.CompilerParams(vmem_limit_bytes=VMEM_LIMIT),
    )(*scalars, *operands)


def spread(weight):
    n_t, n_y, n_x, ci, co = weight.shape
    wide = n_x * co
    past = n_t - 1

    def body(w_ref, po_ref, ps_ref, ao_ref, as_ref):
        dy = pl.program_id(0)

        def at(t, x):
            return w_ref[t, 0, x]

        def side(y):
            for x in range(n_x):
                cols = slice(x * co, (x + 1) * co)
                for t in range(past):
                    ps_ref[y, t * ci : (t + 1) * ci, cols] = at(t, x)
                as_ref[y, :, cols] = at(past, x)

        def own(row, y):
            for x in range(n_x):
                cols = slice(y * wide + x * co, y * wide + (x + 1) * co)
                for t in range(past):
                    lo = (row * past + t) * ci
                    po_ref[lo : lo + ci, cols] = at(t, x)
                ao_ref[row * ci : (row + 1) * ci, cols] = at(past, x)

        @pl.when(dy == 0)
        def _():
            side(0)
            own(0, 1)

        @pl.when(dy == 1)
        def _():
            own(0, 0)
            own(1, 1)

        @pl.when(dy == 2)
        def _():
            side(1)
            own(1, 0)

    shapes = [(2 * past * ci, 2 * wide), (2, past * ci, wide), (2 * ci, 2 * wide), (2, ci, wide)]
    return pl.pallas_call(
        body,
        grid=(n_y,),
        in_specs=[pl.BlockSpec((n_t, 1, n_x, ci, co), lambda y: (0, y, 0, 0, 0))],
        out_specs=[
            pl.BlockSpec(shape, lambda y, zeros=(0,) * len(shape): zeros) for shape in shapes
        ],
        out_shape=[jax.ShapeDtypeStruct(shape, weight.dtype) for shape in shapes],
        cost_estimate=pl.CostEstimate(flops=0, bytes_accessed=5 * weight.size, transcendentals=0),
        compiler_params=pltpu.CompilerParams(vmem_limit_bytes=40 << 20),
    )(weight)


def activated(values, gain):
    u = values * lax.rsqrt(jnp.mean(values * values, axis=-1, keepdims=True) + 1e-06) * gain
    return u / (1.0 + jnp.exp(-u))


def first_activation(frame, gain):
    n_slots, n_rows, n_cols, ch = frame.shape

    def body(f_ref, g_ref, o_ref, top_ref, bottom_ref):
        for s in range(n_slots):
            for r in range(n_rows):
                value = activated(f_ref[s, r].astype(jnp.float32), g_ref[...]).astype(jnp.bfloat16)
                o_ref[s, r] = value
                if r == 0:
                    top_ref[s] = value
                if r == n_rows - 1:
                    bottom_ref[s] = value

    row = jax.ShapeDtypeStruct((n_slots, n_cols, ch), jnp.bfloat16)
    return call(
        body,
        [jax.ShapeDtypeStruct(frame.shape, jnp.bfloat16), row, row],
        (frame, gain),
        flops=10 * frame.size,
        moved=6 * frame.size,
    )


def folded(acc, ch, cols_first):
    tiles = acc.shape[0] // CB
    n_slots = 4
    blocks = tiles // n_slots
    lead = (blocks, n_slots) if cols_first else (n_slots, blocks)
    axis = 0 if cols_first else 1

    def plane(k):
        value = acc[:, k * ch : (k + 1) * ch].reshape(tiles, CB, ch)
        return value

    at = lax.broadcasted_iota(jnp.int32, (1, 1, CB, ch), 2)
    before = pltpu.roll(plane(0), 1, 1).reshape(lead + (CB, ch))
    after = pltpu.roll(plane(2), CB - 1, 1).reshape(lead + (CB, ch))
    gap = list(lead) + [CB, ch]
    gap[axis] = 1
    gap = jnp.zeros(gap, jnp.float32)
    before_prev = jnp.concatenate([gap, lax.slice_in_dim(before, 0, blocks - 1, axis=axis)], axis)
    after_next = jnp.concatenate([lax.slice_in_dim(after, 1, blocks, axis=axis), gap], axis)
    total = plane(1).reshape(lead + (CB, ch))
    total += jnp.where(at == 0, before_prev, before)
    total += jnp.where(at == CB - 1, after_next, after)
    return total


def add_into(o_ref, y, total, cols_first, base=None):
    if cols_first:
        o_ref[y] = total if base is None else base[y] + total
        return
    for s in range(total.shape[0]):
        o_ref[y, :, s] = total[s] if base is None else base[y, :, s] + total[s]


def masked(edge_ref, k, s, value):
    return jnp.where(edge_ref[k, s] != 0, value, jnp.zeros_like(value))


def dot(a, b):
    return jnp.dot(a, b, preferred_element_type=jnp.float32)


def sums_shape(blocks, n_slots, n_rows, ch):
    return jax.ShapeDtypeStruct((n_rows, blocks, n_slots, CB, ch), jnp.float32)


def add_sides(edge_ref, sides, w_ref, lhs, o_ref):
    n_slots, n_cols, ch = sides[0].shape
    for y, side in enumerate(sides):
        for s in range(n_slots):
            lhs[s * n_cols : (s + 1) * n_cols] = masked(edge_ref, y, s, side[s])
        add_into(o_ref, y, folded(dot(lhs[...], w_ref[y]), ch, False), False, o_ref)


def add_own(act_ref, w_ref, lhs, o_ref, base):
    n_slots, n_rows, n_cols, ch = act_ref.shape
    for s in range(n_slots):
        for r in range(n_rows):
            lhs[s * n_cols : (s + 1) * n_cols, r * ch : (r + 1) * ch] = act_ref[s, r]
    both = dot(lhs[...], w_ref[...])
    wide = both.shape[1] // 2
    for y in range(n_rows):
        add_into(o_ref, y, folded(both[:, y * wide : (y + 1) * wide], ch, False), False, base)


def current_part(act, above, below, w_own, w_sides, edges):
    n_slots, n_rows, n_cols, ch = act.shape
    half = n_slots * n_cols

    def body(edge_ref, act_ref, above_ref, below_ref, wo_ref, ws_ref, o_ref, lhs, side):
        add_own(act_ref, wo_ref, lhs, o_ref, None)
        add_sides(edge_ref, (above_ref, below_ref), ws_ref, side, o_ref)

    return call(
        body,
        [sums_shape(n_cols // CB, n_slots, n_rows, ch)],
        (act, above, below, w_own, w_sides),
        scalars=(edges,),
        scratch=[
            pltpu.VMEM((half, n_rows * ch), jnp.bfloat16),
            pltpu.VMEM((half, ch), jnp.bfloat16),
        ],
        flops=2 * half * (w_own.size + w_sides.size),
        moved=2 * w_own.size + 8 * act.size,
    )[0]


def own_part(got, weights, sums, act):
    n_rows, n_caches, n_frames, blocks, n_slots, _, ch = got.shape
    half = blocks * n_slots * CB
    deep = n_frames * ch
    parts = 3
    whole = weights[0]
    part = whole.shape[1] // parts

    def body(got_ref, w0_ref, w1_ref, z_ref, act_ref, o0_ref, o1_ref, n1_ref, n2_ref, w, lhs, acc, sems, kept_sems, act_sem):
        loads = []
        for k, src in enumerate((w0_ref, w1_ref)):
            for p in range(parts):
                cols = pl.ds(p * part, part)
                n = k * parts + p
                loads.append(pltpu.make_async_copy(src.at[:, cols], w.at[k, :, cols], sems.at[n]))
        loads[0].start()
        loads[1].start()
        keeps = []
        for k, dst in enumerate((n1_ref, n2_ref)):
            for r in range(n_rows):
                for s in range(n_slots):
                    n = (k * n_rows + r) * n_slots + s
                    keeps.append(
                        pltpu.make_async_copy(
                            got_ref.at[r, k, n_frames - 1, :, s], dst.at[s, 0, r], kept_sems.at[n]
                        )
                    )
        keeps.append(pltpu.make_async_copy(act_ref, n1_ref.at[:, 1], act_sem))
        for k, (o_ref, base) in enumerate(((o0_ref, z_ref), (o1_ref, None))):
            for r in range(n_rows):
                for f in range(n_frames):
                    lo = r * deep + f * ch
                    lhs[:, lo : lo + ch] = got_ref[r, k, f].reshape(half, ch)
            for p in range(parts):
                n = k * parts + p
                loads[n].wait()
                if n + 2 < len(loads):
                    loads[n + 2].start()
                if n == 3:
                    for c in keeps:
                        c.start()
                cols = slice(p * part, (p + 1) * part)
                acc[:, cols] = dot(lhs[...], w[k, :, cols])
            wide = whole.shape[1] // 2
            for y in range(n_rows):
                total = folded(acc[:, y * wide : (y + 1) * wide], ch, True)
                add_into(o_ref, y, total, True, base)
        for c in keeps:
            c.wait()

    out = sums_shape(blocks, n_slots, n_rows, ch)
    nxt = jax.ShapeDtypeStruct((n_slots, 2, n_rows, blocks, CB, ch), jnp.bfloat16)
    return call(
        body,
        [out, out, nxt, nxt],
        (got, *weights, sums, act),
        scratch=[
            pltpu.VMEM((2,) + whole.shape, whole.dtype),
            pltpu.VMEM((half, n_rows * deep), jnp.bfloat16),
            pltpu.VMEM((half, whole.shape[1]), jnp.float32),
            pltpu.SemaphoreType.DMA((2 * parts,)),
            pltpu.SemaphoreType.DMA((2 * n_rows * n_slots,)),
            pltpu.SemaphoreType.DMA,
        ],
        flops=4 * half * whole.size,
        moved=4 * whole.size,
        far=(1, 2),
        far_out=(2, 3),
    )


def side_sums(edge_ref, k, side_ref, w, lhs):
    n_frames, blocks, n_slots, _, ch = side_ref.shape
    for s in range(n_slots):
        for f in range(n_frames):
            value = masked(edge_ref, k, s, side_ref[f, :, s])
            lhs[:, s, :, f * ch : (f + 1) * ch] = value
    half = blocks * n_slots * CB
    return folded(dot(lhs[...].reshape(half, n_frames * ch), w), ch, True)


def second_activation(above, below, w_sides, sums, bias, gain, edges):
    n_frames, blocks, n_slots, _, ch = above.shape
    n_rows, n_cols, deep = sums.shape[0], blocks * CB, n_frames * ch

    def body(edge_ref, above_ref, below_ref, w_ref, z_ref, b_ref, g_ref, o_ref, top_ref, bottom_ref, lhs):
        for y, side in enumerate((above_ref, below_ref)):
            total = side_sums(edge_ref, y, side, w_ref[y], lhs) + z_ref[y] + b_ref[...]
            for s in range(n_slots):
                value = activated(total[:, s].reshape(n_cols, ch), g_ref[...]).astype(jnp.bfloat16)
                o_ref[s, y] = value
                if y == 0:
                    top_ref[s] = value
                else:
                    bottom_ref[s] = value

    row = jax.ShapeDtypeStruct((n_slots, n_cols, ch), jnp.bfloat16)
    return call(
        body,
        [jax.ShapeDtypeStruct((n_slots, n_rows, n_cols, ch), jnp.bfloat16), row, row],
        (above, below, w_sides, sums, bias, gain),
        scalars=(edges,),
        scratch=[pltpu.VMEM((blocks, n_slots, CB, deep), jnp.bfloat16)],
        flops=2 * n_slots * n_cols * w_sides.size,
        moved=2 * w_sides.size,
    )


def before_sides(above, below, act, w_sides, w_act, sums, kept, edges):
    n_frames, blocks, n_slots, _, ch = above.shape
    n_rows, n_cols, deep = sums.shape[0], blocks * CB, n_frames * ch

    def body(edge_ref, above_ref, below_ref, act_ref, tiles_ref, w_ref, wa_ref, z_ref, kept_ref, o_ref, next_ref, lhs, lhs2, sem):
        copy = pltpu.make_async_copy(tiles_ref, next_ref.at[:, 1], sem)
        copy.start()
        add_own(act_ref, wa_ref, lhs2, o_ref, z_ref)
        for y, side in enumerate((above_ref, below_ref)):
            o_ref[y] += side_sums(edge_ref, y, side, w_ref[y], lhs)
        copy.wait()

    return call(
        body,
        [jax.ShapeDtypeStruct(sums.shape, jnp.float32), jax.ShapeDtypeStruct(kept.shape, kept.dtype)],
        (above, below, act, act.reshape(n_slots, n_rows, blocks, CB, ch), w_sides, w_act, sums, kept),
        scalars=(edges,),
        scratch=[
            pltpu.VMEM((blocks, n_slots, CB, deep), jnp.bfloat16),
            pltpu.VMEM((n_slots * n_cols, n_rows * ch), jnp.bfloat16),
            pltpu.SemaphoreType.DMA,
        ],
        flops=2 * n_slots * n_cols * (w_sides.size + w_act.size),
        moved=2 * (w_sides.size + w_act.size),
        far=(7,),
        far_out=(1,),
        aliases={8: 1},
    )


def last_part(above, below, w_sides, sums, bias, frame, edges):
    n_slots, n_rows, n_cols, ch = frame.shape

    def body(edge_ref, above_ref, below_ref, w_ref, z_ref, b_ref, f_ref, o_ref, lhs):
        for y, side in enumerate((above_ref, below_ref)):
            for s in range(n_slots):
                lhs[s * n_cols : (s + 1) * n_cols] = masked(edge_ref, y, s, side[s])
            total = folded(dot(lhs[...], w_ref[y]), ch, False)
            for s in range(n_slots):
                value = (total[s] + z_ref[y, :, s] + b_ref[...]).reshape(n_cols, ch)
                o_ref[s, y] = (value + f_ref[s, y].astype(jnp.float32)).astype(jnp.bfloat16)

    return call(
        body,
        [jax.ShapeDtypeStruct(frame.shape, jnp.bfloat16)],
        (above, below, w_sides, sums, bias, frame),
        scalars=(edges,),
        scratch=[pltpu.VMEM((n_slots * n_cols, ch), jnp.bfloat16)],
        flops=2 * n_slots * n_cols * w_sides.size,
        moved=2 * w_sides.size,
    )[0]


def local(
    frame_in,
    cache_first,
    cache_second,
    gain_first,
    gain_second,
    conv_first,
    conv_second,
    bias_first,
    bias_second,
    old_slot,
    new_slot,
    old_shift,
    new_shift,
    frame_count,
):
    n_slots, n_rows, n_cols, ch = frame_in.shape
    n_groups = lax.axis_size("stream")
    n_tiles = lax.axis_size("tile")
    my_group = lax.axis_index("stream")
    my_tile = lax.axis_index("tile")
    n_flight = old_slot.shape[0]
    blocks = n_cols // CB
    slot_ids = jnp.arange(n_flight, dtype=jnp.int32)
    held_new = new_slot[None, :] == slot_ids[:, None]
    source = lookup(held_new, old_slot)
    shift_after = lookup(held_new, new_shift)
    rotation = (shift_after - lookup(held_new, old_shift)) % n_tiles
    frames_done = lookup(held_new, frame_count)
    my_piece = my_group * n_tiles + my_tile
    my_frame = (my_piece // blocks) % 2
    keep = (frames_done >= 2 - my_frame).astype(jnp.int32)
    start = my_group * n_slots
    my_number = lax.dynamic_slice_in_dim((my_tile - shift_after) % n_tiles, start, n_slots)

    edges = jnp.stack([my_number != 0, my_number != n_tiles - 1]).astype(jnp.int32)
    down = [(i, (i + 1) % n_tiles) for i in range(n_tiles)]
    up = [((i + 1) % n_tiles, i) for i in range(n_tiles)]

    def from_above(row):
        return lax.ppermute(row, "tile", down)

    def from_below(row):
        return lax.ppermute(row, "tile", up)

    sent = pack(cache_first, cache_second).reshape(n_groups * n_tiles, n_slots, CB, ch)
    held = lax.all_to_all(sent, BOTH, 0, 0, tiled=True)

    own_1, sides_1, act_own_1, act_sides_1 = spread(conv_first)
    own_2, sides_2, act_own_2, act_sides_2 = spread(conv_second)
    act_first, top, bottom = first_activation(frame_in, gain_first[None])
    act_above, act_below = from_above(bottom), from_below(top)
    held, act_first, act_above, act_below, own_1, own_2 = lax.optimization_barrier(
        (held, act_first, act_above, act_below, own_1, own_2)
    )

    moved = permute(held.reshape(n_groups, n_tiles, n_slots, CB, ch), source, rotation, keep)
    moved, act_later = lax.optimization_barrier((moved, act_first))
    got = lax.all_to_all(
        moved.reshape(n_groups * n_tiles, n_slots, CB, ch), BOTH, 0, 0, tiled=True
    )
    sums_1 = current_part(act_later, act_above, act_below, act_own_1, act_sides_1, edges)
    got, sums_1 = lax.optimization_barrier((got, sums_1))
    got = got.reshape(n_rows, 2, 2, blocks, n_slots, CB, ch)

    above_1 = from_above(got[n_rows - 1, 0])
    below_1 = from_below(got[0, 0])
    above_2 = from_above(got[n_rows - 1, 1])
    below_2 = from_below(got[0, 1])
    act_tiles = act_first.reshape(n_slots, n_rows, blocks, CB, ch)
    sums_1, sums_2, next_first, kept = own_part(got, (own_1, own_2), sums_1, act_tiles)
    act_second, top, bottom = second_activation(
        above_1, below_1, sides_1, sums_1, bias_first[None], gain_second[None], edges
    )
    side_above, side_below = from_above(bottom), from_below(top)
    sums_2, next_second = before_sides(
        above_2, below_2, act_second, sides_2, act_own_2, sums_2, kept, edges
    )
    mixed_frame = last_part(
        side_above, side_below, act_sides_2, sums_2, bias_second[None], frame_in, edges
    )
    whole = (n_slots, 2, n_rows, n_cols, ch)
    return (mixed_frame, next_first.reshape(whole), next_second.reshape(whole))


def solution(mesh):
    frame = P("stream", "tile", None, None)
    cache = P("stream", None, "tile", None, None)
    return jax.shard_map(
        local,
        mesh=mesh,
        in_specs=(frame, cache, cache) + (P(),) * 11,
        out_specs=(frame, cache, cache),
        check_vma=False,
    )
```

```python
import jax
import jax.numpy as jnp
from jax import lax
from jax.experimental import pallas as pl
from jax.experimental.pallas import tpu as pltpu
from jax.sharding import PartitionSpec as P

BOTH = ("stream", "tile")
CB = 8


def lookup(held_table, values):
    return jnp.sum(jnp.where(held_table, values[None, :], 0), axis=1)


def pack(first, second):
    n_slots, n_frames, n_rows, n_cols, ch = first.shape
    blocks = n_cols // CB

    def body(a_ref, b_ref, o_ref):
        for k, ref in enumerate((a_ref, b_ref)):
            for f in range(n_frames):
                for r in range(n_rows):
                    o_ref[r, k, f, :, 0] = ref[0, f, r].reshape(blocks, CB, ch)

    spec = pl.BlockSpec((1, n_frames, n_rows, n_cols, ch), lambda s: (s, 0, 0, 0, 0))
    return pl.pallas_call(
        body,
        grid=(n_slots,),
        in_specs=[spec, spec],
        out_specs=pl.BlockSpec(
            (n_rows, 2, n_frames, blocks, 1, CB, ch), lambda s: (0, 0, 0, 0, s, 0, 0)
        ),
        out_shape=jax.ShapeDtypeStruct(
            (n_rows, 2, n_frames, blocks, n_slots, CB, ch), first.dtype
        ),
        compiler_params=pltpu.CompilerParams(vmem_limit_bytes=58 << 20),
    )(first, second)


def permute(held, source, rotation, keep):
    n_groups, n_tiles, n_slots, cols, ch = held.shape

    def body(source_ref, rotation_ref, keep_ref, i_ref, o_ref):
        n = pl.program_id(0)
        by = rotation_ref[n]

        @pl.when(keep_ref[n] != 0)
        def _():
            def step(t, _):
                at = lax.rem(t + n_tiles - by, n_tiles)
                o_ref[0, t, 0] = i_ref[0, at, 0]
                return 0

            lax.fori_loop(0, n_tiles, step, 0, unroll=8)

        @pl.when(keep_ref[n] == 0)
        def _():
            o_ref[...] = jnp.zeros_like(o_ref)

    block = (1, n_tiles, 1, cols, ch)
    return pl.pallas_call(
        body,
        grid_spec=pltpu.PrefetchScalarGridSpec(
            num_scalar_prefetch=3,
            grid=(n_groups * n_slots,),
            in_specs=[
                pl.BlockSpec(
                    block,
                    lambda n, s, r, k: (lax.div(s[n], n_slots), 0, lax.rem(s[n], n_slots), 0, 0),
                )
            ],
            out_specs=pl.BlockSpec(
                block, lambda n, s, r, k: (lax.div(n, n_slots), 0, lax.rem(n, n_slots), 0, 0)
            ),
        ),
        out_shape=jax.ShapeDtypeStruct(held.shape, held.dtype),
        compiler_params=pltpu.CompilerParams(vmem_limit_bytes=32 << 20),
    )(source, rotation, keep, held)


VMEM_LIMIT = 16 << 20


def call(body, out_shape, operands, scalars=(), scratch=(), flops=0, moved=0, far=(), far_out=(), aliases=None):
    in_specs = [pl.BlockSpec(memory_space=pltpu.SMEM) for _ in scalars]
    for k, _ in enumerate(operands):
        in_specs.append(pl.BlockSpec(memory_space=pl.ANY if k in far else pltpu.VMEM))
    out_specs = []
    for k, _ in enumerate(out_shape):
        out_specs.append(pl.BlockSpec(memory_space=pl.ANY if k in far_out else pltpu.VMEM))
    return pl.pallas_call(
        body,
        in_specs=in_specs,
        out_specs=out_specs,
        out_shape=list(out_shape),
        scratch_shapes=list(scratch),
        input_output_aliases=aliases or {},
        cost_estimate=pl.CostEstimate(flops=flops, bytes_accessed=moved, transcendentals=0),
        compiler_params=pltpu.CompilerParams(vmem_limit_bytes=VMEM_LIMIT),
    )(*scalars, *operands)


def spread(weight, past):
    n_t, n_y, n_x, ci, co = weight.shape
    wide = n_x * co
    times = n_t - 1 if past else 1

    def body(w_ref, own_ref, side_ref):
        dy = pl.program_id(0)

        def side(y):
            for x in range(n_x):
                for t in range(times):
                    side_ref[y, t * ci : (t + 1) * ci, x * co : (x + 1) * co] = w_ref[t, 0, x]

        def own(row, y):
            for x in range(n_x):
                for t in range(times):
                    lo = (row * times + t) * ci
                    at = y * wide + x * co
                    own_ref[lo : lo + ci, at : at + co] = w_ref[t, 0, x]

        @pl.when(dy == 0)
        def _():
            side(0)
            own(0, 1)

        @pl.when(dy == 1)
        def _():
            own(0, 0)
            own(1, 1)

        @pl.when(dy == 2)
        def _():
            side(1)
            own(1, 0)

    shapes = [(2 * times * ci, 2 * wide), (2, times * ci, wide)]
    first = 0 if past else n_t - 1
    return pl.pallas_call(
        body,
        grid=(n_y,),
        in_specs=[pl.BlockSpec((times, 1, n_x, ci, co), lambda y: (first, y, 0, 0, 0))],
        out_specs=[pl.BlockSpec(memory_space=pltpu.VMEM) for _ in shapes],
        out_shape=[jax.ShapeDtypeStruct(shape, weight.dtype) for shape in shapes],
        cost_estimate=pl.CostEstimate(flops=0, bytes_accessed=4 * weight.size, transcendentals=0),
        compiler_params=pltpu.CompilerParams(vmem_limit_bytes=16 << 20),
    )(weight)


def activated(values, gain):
    u = values * lax.rsqrt(jnp.mean(values * values, axis=-1, keepdims=True) + 1e-06) * gain
    return u / (1.0 + jnp.exp(-u))


def first_activation(frame, gain):
    n_slots, n_rows, n_cols, ch = frame.shape

    def body(f_ref, g_ref, o_ref, top_ref, bottom_ref):
        for s in range(n_slots):
            for r in range(n_rows):
                value = activated(f_ref[s, r].astype(jnp.float32), g_ref[...]).astype(jnp.bfloat16)
                o_ref[s, r] = value
                if r == 0:
                    top_ref[s] = value
                if r == n_rows - 1:
                    bottom_ref[s] = value

    row = jax.ShapeDtypeStruct((n_slots, n_cols, ch), jnp.bfloat16)
    return call(
        body,
        [jax.ShapeDtypeStruct(frame.shape, jnp.bfloat16), row, row],
        (frame, gain),
        flops=10 * frame.size,
        moved=6 * frame.size,
    )


def folded(acc, ch, cols_first):
    tiles = acc.shape[0] // CB
    n_slots = 4
    blocks = tiles // n_slots
    lead = (blocks, n_slots) if cols_first else (n_slots, blocks)
    axis = 0 if cols_first else 1

    def plane(k):
        value = acc[:, k * ch : (k + 1) * ch].reshape(tiles, CB, ch)
        return value

    at = lax.broadcasted_iota(jnp.int32, (1, 1, CB, ch), 2)
    before = pltpu.roll(plane(0), 1, 1).reshape(lead + (CB, ch))
    after = pltpu.roll(plane(2), CB - 1, 1).reshape(lead + (CB, ch))
    gap = list(lead) + [CB, ch]
    gap[axis] = 1
    gap = jnp.zeros(gap, jnp.float32)
    before_prev = jnp.concatenate([gap, lax.slice_in_dim(before, 0, blocks - 1, axis=axis)], axis)
    after_next = jnp.concatenate([lax.slice_in_dim(after, 1, blocks, axis=axis), gap], axis)
    total = plane(1).reshape(lead + (CB, ch))
    total += jnp.where(at == 0, before_prev, before)
    total += jnp.where(at == CB - 1, after_next, after)
    return total


def add_into(o_ref, y, total, cols_first, base=None):
    if cols_first:
        o_ref[y] = total if base is None else base[y] + total
        return
    for s in range(total.shape[0]):
        o_ref[y, :, s] = total[s] if base is None else base[y, :, s] + total[s]


def masked(edge_ref, k, s, value):
    return jnp.where(edge_ref[k, s] != 0, value, jnp.zeros_like(value))


def dot(a, b):
    return jnp.dot(a, b, preferred_element_type=jnp.float32)


def sums_shape(blocks, n_slots, n_rows, ch):
    return jax.ShapeDtypeStruct((n_rows, blocks, n_slots, CB, ch), jnp.float32)


def add_sides(edge_ref, sides, w_ref, lhs, o_ref):
    n_slots, n_cols, ch = sides[0].shape
    for y, side in enumerate(sides):
        for s in range(n_slots):
            lhs[s * n_cols : (s + 1) * n_cols] = masked(edge_ref, y, s, side[s])
        add_into(o_ref, y, folded(dot(lhs[...], w_ref[y]), ch, False), False, o_ref)


def add_own(act_ref, w_ref, lhs, o_ref, base):
    n_slots, n_rows, n_cols, ch = act_ref.shape
    for s in range(n_slots):
        for r in range(n_rows):
            lhs[s * n_cols : (s + 1) * n_cols, r * ch : (r + 1) * ch] = act_ref[s, r]
    both = dot(lhs[...], w_ref[...])
    wide = both.shape[1] // 2
    for y in range(n_rows):
        add_into(o_ref, y, folded(both[:, y * wide : (y + 1) * wide], ch, False), False, base)


def current_part(act, above, below, w_own, w_sides, edges):
    n_slots, n_rows, n_cols, ch = act.shape
    half = n_slots * n_cols

    def body(edge_ref, act_ref, above_ref, below_ref, wo_ref, ws_ref, o_ref, lhs, side):
        add_own(act_ref, wo_ref, lhs, o_ref, None)
        add_sides(edge_ref, (above_ref, below_ref), ws_ref, side, o_ref)

    return call(
        body,
        [sums_shape(n_cols // CB, n_slots, n_rows, ch)],
        (act, above, below, w_own, w_sides),
        scalars=(edges,),
        scratch=[
            pltpu.VMEM((half, n_rows * ch), jnp.bfloat16),
            pltpu.VMEM((half, ch), jnp.bfloat16),
        ],
        flops=2 * half * (w_own.size + w_sides.size),
        moved=2 * w_own.size + 8 * act.size,
    )[0]


def own_part(got, weights, sums, act):
    n_rows, n_caches, n_frames, blocks, n_slots, _, ch = got.shape
    half = blocks * n_slots * CB
    deep = n_frames * ch
    whole = weights[0]

    def body(got_ref, w0_ref, w1_ref, z_ref, act_ref, o0_ref, o1_ref, n1_ref, n2_ref, lhs, sems, act_sem):
        keeps = []
        for k, dst in enumerate((n1_ref, n2_ref)):
            for r in range(n_rows):
                for s in range(n_slots):
                    n = (k * n_rows + r) * n_slots + s
                    keeps.append(
                        pltpu.make_async_copy(
                            got_ref.at[r, k, n_frames - 1, :, s], dst.at[s, 0, r], sems.at[n]
                        )
                    )
        keeps.append(pltpu.make_async_copy(act_ref, n1_ref.at[:, 1], act_sem))
        for c in keeps:
            c.start()
        for k, (w, o_ref, base) in enumerate(((w0_ref, o0_ref, z_ref), (w1_ref, o1_ref, None))):
            for r in range(n_rows):
                for f in range(n_frames):
                    lo = r * deep + f * ch
                    lhs[:, lo : lo + ch] = got_ref[r, k, f].reshape(half, ch)
            both = dot(lhs[...], w[...])
            wide = both.shape[1] // 2
            for y in range(n_rows):
                total = folded(both[:, y * wide : (y + 1) * wide], ch, True)
                add_into(o_ref, y, total, True, base)
        for c in keeps:
            c.wait()

    out = sums_shape(blocks, n_slots, n_rows, ch)
    nxt = jax.ShapeDtypeStruct((n_slots, 2, n_rows, blocks, CB, ch), jnp.bfloat16)
    return call(
        body,
        [out, out, nxt, nxt],
        (got, *weights, sums, act),
        scratch=[
            pltpu.VMEM((half, n_rows * deep), jnp.bfloat16),
            pltpu.SemaphoreType.DMA((2 * n_rows * n_slots,)),
            pltpu.SemaphoreType.DMA,
        ],
        flops=4 * half * whole.size,
        moved=4 * whole.size,
        far_out=(2, 3),
    )


def side_sums(edge_ref, k, side_ref, w, lhs):
    n_frames, blocks, n_slots, _, ch = side_ref.shape
    for s in range(n_slots):
        for f in range(n_frames):
            value = masked(edge_ref, k, s, side_ref[f, :, s])
            lhs[:, s, :, f * ch : (f + 1) * ch] = value
    half = blocks * n_slots * CB
    return folded(dot(lhs[...].reshape(half, n_frames * ch), w), ch, True)


def second_activation(above, below, w_sides, sums, bias, gain, edges):
    n_frames, blocks, n_slots, _, ch = above.shape
    n_rows, n_cols, deep = sums.shape[0], blocks * CB, n_frames * ch

    def body(edge_ref, above_ref, below_ref, w_ref, z_ref, b_ref, g_ref, o_ref, top_ref, bottom_ref, lhs):
        for y, side in enumerate((above_ref, below_ref)):
            total = side_sums(edge_ref, y, side, w_ref[y], lhs) + z_ref[y] + b_ref[...]
            for s in range(n_slots):
                value = activated(total[:, s].reshape(n_cols, ch), g_ref[...]).astype(jnp.bfloat16)
                o_ref[s, y] = value
                if y == 0:
                    top_ref[s] = value
                else:
                    bottom_ref[s] = value

    row = jax.ShapeDtypeStruct((n_slots, n_cols, ch), jnp.bfloat16)
    return call(
        body,
        [jax.ShapeDtypeStruct((n_slots, n_rows, n_cols, ch), jnp.bfloat16), row, row],
        (above, below, w_sides, sums, bias, gain),
        scalars=(edges,),
        scratch=[pltpu.VMEM((blocks, n_slots, CB, deep), jnp.bfloat16)],
        flops=2 * n_slots * n_cols * w_sides.size,
        moved=2 * w_sides.size,
    )


def before_sides(above, below, act, w_sides, w_act, sums, kept, edges):
    n_frames, blocks, n_slots, _, ch = above.shape
    n_rows, n_cols, deep = sums.shape[0], blocks * CB, n_frames * ch

    def body(edge_ref, above_ref, below_ref, act_ref, tiles_ref, w_ref, wa_ref, z_ref, kept_ref, o_ref, next_ref, lhs, lhs2, sem):
        copy = pltpu.make_async_copy(tiles_ref, next_ref.at[:, 1], sem)
        copy.start()
        add_own(act_ref, wa_ref, lhs2, o_ref, z_ref)
        for y, side in enumerate((above_ref, below_ref)):
            o_ref[y] += side_sums(edge_ref, y, side, w_ref[y], lhs)
        copy.wait()

    return call(
        body,
        [jax.ShapeDtypeStruct(sums.shape, jnp.float32), jax.ShapeDtypeStruct(kept.shape, kept.dtype)],
        (above, below, act, act.reshape(n_slots, n_rows, blocks, CB, ch), w_sides, w_act, sums, kept),
        scalars=(edges,),
        scratch=[
            pltpu.VMEM((blocks, n_slots, CB, deep), jnp.bfloat16),
            pltpu.VMEM((n_slots * n_cols, n_rows * ch), jnp.bfloat16),
            pltpu.SemaphoreType.DMA,
        ],
        flops=2 * n_slots * n_cols * (w_sides.size + w_act.size),
        moved=2 * (w_sides.size + w_act.size),
        far=(7,),
        far_out=(1,),
        aliases={8: 1},
    )


def last_part(above, below, w_sides, sums, bias, frame, edges):
    n_slots, n_rows, n_cols, ch = frame.shape

    def body(edge_ref, above_ref, below_ref, w_ref, z_ref, b_ref, f_ref, o_ref, lhs):
        for y, side in enumerate((above_ref, below_ref)):
            for s in range(n_slots):
                lhs[s * n_cols : (s + 1) * n_cols] = masked(edge_ref, y, s, side[s])
            total = folded(dot(lhs[...], w_ref[y]), ch, False)
            for s in range(n_slots):
                value = (total[s] + z_ref[y, :, s] + b_ref[...]).reshape(n_cols, ch)
                o_ref[s, y] = (value + f_ref[s, y].astype(jnp.float32)).astype(jnp.bfloat16)

    return call(
        body,
        [jax.ShapeDtypeStruct(frame.shape, jnp.bfloat16)],
        (above, below, w_sides, sums, bias, frame),
        scalars=(edges,),
        scratch=[pltpu.VMEM((n_slots * n_cols, ch), jnp.bfloat16)],
        flops=2 * n_slots * n_cols * w_sides.size,
        moved=2 * w_sides.size,
    )[0]


def local(
    frame_in,
    cache_first,
    cache_second,
    gain_first,
    gain_second,
    conv_first,
    conv_second,
    bias_first,
    bias_second,
    old_slot,
    new_slot,
    old_shift,
    new_shift,
    frame_count,
):
    n_slots, n_rows, n_cols, ch = frame_in.shape
    n_groups = lax.axis_size("stream")
    n_tiles = lax.axis_size("tile")
    my_group = lax.axis_index("stream")
    my_tile = lax.axis_index("tile")
    n_flight = old_slot.shape[0]
    blocks = n_cols // CB
    slot_ids = jnp.arange(n_flight, dtype=jnp.int32)
    held_new = new_slot[None, :] == slot_ids[:, None]
    source = lookup(held_new, old_slot)
    shift_after = lookup(held_new, new_shift)
    rotation = (shift_after - lookup(held_new, old_shift)) % n_tiles
    frames_done = lookup(held_new, frame_count)
    my_piece = my_group * n_tiles + my_tile
    my_frame = (my_piece // blocks) % 2
    keep = (frames_done >= 2 - my_frame).astype(jnp.int32)
    start = my_group * n_slots
    my_number = lax.dynamic_slice_in_dim((my_tile - shift_after) % n_tiles, start, n_slots)

    edges = jnp.stack([my_number != 0, my_number != n_tiles - 1]).astype(jnp.int32)
    down = [(i, (i + 1) % n_tiles) for i in range(n_tiles)]
    up = [((i + 1) % n_tiles, i) for i in range(n_tiles)]

    def from_above(row):
        return lax.ppermute(row, "tile", down)

    def from_below(row):
        return lax.ppermute(row, "tile", up)

    sent = pack(cache_first, cache_second).reshape(n_groups * n_tiles, n_slots, CB, ch)
    held = lax.all_to_all(sent, BOTH, 0, 0, tiled=True)

    act_own_1, act_sides_1 = spread(conv_first, False)
    act_first, top, bottom = first_activation(frame_in, gain_first[None])
    act_above, act_below = from_above(bottom), from_below(top)
    held, act_first, act_above, act_below, act_own_1, act_sides_1 = lax.optimization_barrier(
        (held, act_first, act_above, act_below, act_own_1, act_sides_1)
    )

    moved = permute(held.reshape(n_groups, n_tiles, n_slots, CB, ch), source, rotation, keep)
    moved, act_later = lax.optimization_barrier((moved, act_first))
    got = lax.all_to_all(
        moved.reshape(n_groups * n_tiles, n_slots, CB, ch), BOTH, 0, 0, tiled=True
    )
    sums_1 = current_part(act_later, act_above, act_below, act_own_1, act_sides_1, edges)
    sums_1, conv_first, conv_second = lax.optimization_barrier((sums_1, conv_first, conv_second))
    act_own_2, act_sides_2 = spread(conv_second, False)
    own_1, sides_1 = spread(conv_first, True)
    own_2, sides_2 = spread(conv_second, True)
    got, sums_1, own_1, own_2, sides_1, sides_2, act_own_2, act_sides_2 = lax.optimization_barrier(
        (got, sums_1, own_1, own_2, sides_1, sides_2, act_own_2, act_sides_2)
    )
    got = got.reshape(n_rows, 2, 2, blocks, n_slots, CB, ch)

    above_1 = from_above(got[n_rows - 1, 0])
    below_1 = from_below(got[0, 0])
    above_2 = from_above(got[n_rows - 1, 1])
    below_2 = from_below(got[0, 1])
    act_tiles = act_first.reshape(n_slots, n_rows, blocks, CB, ch)
    sums_1, sums_2, next_first, kept = own_part(got, (own_1, own_2), sums_1, act_tiles)
    act_second, top, bottom = second_activation(
        above_1, below_1, sides_1, sums_1, bias_first[None], gain_second[None], edges
    )
    side_above, side_below = from_above(bottom), from_below(top)
    sums_2, next_second = before_sides(
        above_2, below_2, act_second, sides_2, act_own_2, sums_2, kept, edges
    )
    mixed_frame = last_part(
        side_above, side_below, act_sides_2, sums_2, bias_second[None], frame_in, edges
    )
    whole = (n_slots, 2, n_rows, n_cols, ch)
    return (mixed_frame, next_first.reshape(whole), next_second.reshape(whole))


def solution(mesh):
    frame = P("stream", "tile", None, None)
    cache = P("stream", None, "tile", None, None)
    return jax.shard_map(
        local,
        mesh=mesh,
        in_specs=(frame, cache, cache) + (P(),) * 11,
        out_specs=(frame, cache, cache),
        check_vma=False,
    )
```

```python
import jax
import jax.numpy as jnp
from jax import lax
from jax.experimental import pallas as pl
from jax.experimental.pallas import tpu as pltpu
from jax.sharding import PartitionSpec as P

BOTH = ("stream", "tile")
CB = 8


SLOTS = 4
GROUPS = 4
CHOICES = 256


def plan(old_slot, new_slot, old_shift, new_shift, frame_count, place):
    flight = GROUPS * SLOTS

    def body(old_ref, new_ref, before_ref, after_ref, count_ref, place_ref, out_ref, src_ref, turn_ref, ok_ref, inv_old, inv_new, rank, colour, pos, packs):
        group, tile, shade, tiles = place_ref[0], place_ref[1], place_ref[2], place_ref[3]
        for s in range(flight):
            inv_old[old_ref[s]] = s
            inv_new[new_ref[s]] = s
        for n in range(8):
            out_ref[n] = 0
        for n in range(2 * flight + 1):
            packs[n] = 0
        for n in range(flight + 1):
            src_ref[n] = 0
            turn_ref[n] = 0
            ok_ref[n] = 0

        shape = (16, CHOICES)
        row = lax.broadcasted_iota(jnp.int32, shape, 0)
        pick = lax.broadcasted_iota(jnp.int32, shape, 1)
        total = jnp.zeros(shape, jnp.float32)
        for g in range(GROUPS):
            seen = jnp.int32(0)
            bits = (pick >> (2 * g)) & 3
            for p in range(SLOTS):
                s = inv_old[g * SLOTS + p]
                c = count_ref[s]
                one = c == 1
                rank[s] = seen
                to = new_ref[s] // SLOTS
                order = jnp.where(bits < 2, seen, seen >> 1)
                tint = (order + bits) & 1
                alone = (row == 2 * to + tint) | (row == 8 + 2 * g + tint)
                pair = ((row >> 1) == to) | ((row >> 1) == GROUPS + g)
                total += jnp.where(alone & one, 1.0, 0.0) + jnp.where(pair & (c >= 2), 1.0, 0.0)
                seen += one.astype(jnp.int32)
        worst = jnp.max(total, axis=0, keepdims=True)
        score = worst * float(CHOICES) + pick[0:1].astype(jnp.float32)
        low = jnp.min(score).astype(jnp.int32)
        out_ref[0] = low // CHOICES
        best = low % CHOICES

        for g in range(GROUPS):
            bits = (best >> (2 * g)) & 3
            used = [jnp.int32(0), jnp.int32(0)]
            for p in range(SLOTS):
                s = inv_old[g * SLOTS + p]
                c = count_ref[s]
                order = jnp.where(bits < 2, rank[s], rank[s] >> 1)
                tint = jnp.where(c >= 2, 1, (order + bits) & 1)
                colour[s] = tint
                newer = jnp.where(tint == 0, used[0], used[1])
                pos[2 * s] = used[0]
                pos[2 * s + 1] = newer
                spare = 2 * flight
                packs[jnp.where(c >= 2, g * 8 + used[0], spare)] = 2 * p
                packs[jnp.where(c >= 1, g * 8 + 4 * tint + newer, spare)] = 2 * p + 1
                first = (c >= 2) | ((c == 1) & (tint == 0))
                second = (c >= 1) & (tint == 1)
                used = [used[0] + first.astype(jnp.int32), used[1] + second.astype(jnp.int32)]
        for n in range(8):
            out_ref[8 + n] = packs[group * 8 + n]

        for g in range(GROUPS):
            used = [jnp.int32(0), jnp.int32(0)]
            for p in range(SLOTS):
                s = inv_new[g * SLOTS + p]
                c = count_ref[s]
                tint = colour[s]
                first = (c >= 2) | ((c == 1) & (tint == 0))
                second = (c >= 1) & (tint == 1)
                newer = jnp.where(tint == 0, used[0], used[1])

                @pl.when(group == g)
                def _(p=p, c=c, tint=tint, newer=newer, s=s, older=used[0]):
                    out_ref[16 + 2 * p] = jnp.where(c >= 2, older, -1)
                    out_ref[16 + 2 * p + 1] = jnp.where(c >= 1, 4 * tint + newer, -1)
                    number = lax.rem(tile + tiles - after_ref[s], tiles)
                    out_ref[24 + p] = (number != 0).astype(jnp.int32)
                    out_ref[28 + p] = (number != tiles - 1).astype(jnp.int32)

                here = jnp.where(shade == 0, first, second)
                j = jnp.where(shade == 0, used[0], used[1])
                at = jnp.where(here, g * 4 + j, flight)
                frame = jnp.where((c >= 2) & (shade == 0), 0, 1)
                src_ref[at] = (old_ref[s] // SLOTS) * 4 + pos[2 * s + frame]
                turn_ref[at] = lax.rem(after_ref[s] - before_ref[s] + tiles, tiles)
                ok_ref[at] = here.astype(jnp.int32)
                used = [used[0] + first.astype(jnp.int32), used[1] + second.astype(jnp.int32)]

    table = jax.ShapeDtypeStruct((flight + 1,), jnp.int32)
    smem = pl.BlockSpec(memory_space=pltpu.SMEM)
    return pl.pallas_call(
        body,
        in_specs=[smem] * 6,
        out_specs=[smem] * 4,
        out_shape=[jax.ShapeDtypeStruct((32,), jnp.int32), table, table, table],
        scratch_shapes=[
            pltpu.SMEM((flight,), jnp.int32),
            pltpu.SMEM((flight,), jnp.int32),
            pltpu.SMEM((flight,), jnp.int32),
            pltpu.SMEM((flight,), jnp.int32),
            pltpu.SMEM((2 * flight,), jnp.int32),
            pltpu.SMEM((2 * flight + 1,), jnp.int32),
        ],
    )(old_slot, new_slot, old_shift, new_shift, frame_count, place)


def pack(first, second, table, depth):
    n_slots, n_frames, n_rows, n_cols, ch = first.shape
    blocks = n_cols // CB

    def body(table_ref, a_ref, b_ref, o_ref):
        for k, ref in enumerate((a_ref, b_ref)):
            for r in range(n_rows):
                o_ref[r, k, 0, :, 0] = ref[0, 0, r].reshape(blocks, CB, ch)

    def source(n, table):
        at = table[8 + 4 * lax.div(n, depth) + lax.rem(n, depth)]
        return (lax.div(at, 2), lax.rem(at, 2), 0, 0, 0)

    spec = pl.BlockSpec((1, 1, n_rows, n_cols, ch), source)
    return pl.pallas_call(
        body,
        grid_spec=pltpu.PrefetchScalarGridSpec(
            num_scalar_prefetch=1,
            grid=(2 * depth,),
            in_specs=[spec, spec],
            out_specs=pl.BlockSpec(
                (n_rows, 2, 1, blocks, 1, CB, ch),
                lambda n, table: (0, 0, lax.div(n, depth), 0, lax.rem(n, depth), 0, 0),
            ),
        ),
        out_shape=jax.ShapeDtypeStruct((n_rows, 2, 2, blocks, depth, CB, ch), first.dtype),
        compiler_params=pltpu.CompilerParams(vmem_limit_bytes=58 << 20),
    )(table, first, second)


def permute(held, source, rotation, valid):
    n_groups, n_tiles, depth, cols, ch = held.shape

    def body(source_ref, rotation_ref, valid_ref, i_ref, o_ref):
        n = pl.program_id(0)
        n = lax.div(n, depth) * 4 + lax.rem(n, depth)
        by = rotation_ref[n]

        @pl.when(valid_ref[n] != 0)
        def _():
            def step(t, _):
                at = lax.rem(t + n_tiles - by, n_tiles)
                o_ref[0, t, 0] = i_ref[0, at, 0]
                return 0

            lax.fori_loop(0, n_tiles, step, 0, unroll=8)

        @pl.when(valid_ref[n] == 0)
        def _():
            o_ref[...] = jnp.zeros_like(o_ref)

    def origin(n, s, r, v):
        at = s[lax.div(n, depth) * 4 + lax.rem(n, depth)]
        return (lax.div(at, 4), 0, lax.rem(at, 4), 0, 0)

    block = (1, n_tiles, 1, cols, ch)
    return pl.pallas_call(
        body,
        grid_spec=pltpu.PrefetchScalarGridSpec(
            num_scalar_prefetch=3,
            grid=(n_groups * depth,),
            in_specs=[pl.BlockSpec(block, origin)],
            out_specs=pl.BlockSpec(
                block, lambda n, s, r, v: (lax.div(n, depth), 0, lax.rem(n, depth), 0, 0)
            ),
        ),
        out_shape=jax.ShapeDtypeStruct(held.shape, held.dtype),
        compiler_params=pltpu.CompilerParams(vmem_limit_bytes=32 << 20),
    )(source, rotation, valid, held)


VMEM_LIMIT = 16 << 20


def call(body, out_shape, operands, scalars=(), scratch=(), flops=0, moved=0, far=(), far_out=(), aliases=None, limit=VMEM_LIMIT):
    in_specs = [pl.BlockSpec(memory_space=pltpu.SMEM) for _ in scalars]
    for k, _ in enumerate(operands):
        in_specs.append(pl.BlockSpec(memory_space=pl.ANY if k in far else pltpu.VMEM))
    out_specs = []
    for k, _ in enumerate(out_shape):
        out_specs.append(pl.BlockSpec(memory_space=pl.ANY if k in far_out else pltpu.VMEM))
    return pl.pallas_call(
        body,
        in_specs=in_specs,
        out_specs=out_specs,
        out_shape=list(out_shape),
        scratch_shapes=list(scratch),
        input_output_aliases=aliases or {},
        cost_estimate=pl.CostEstimate(flops=flops, bytes_accessed=moved, transcendentals=0),
        compiler_params=pltpu.CompilerParams(vmem_limit_bytes=limit),
    )(*scalars, *operands)


def spread(weight, past):
    n_t, n_y, n_x, ci, co = weight.shape
    wide = n_x * co
    times = n_t - 1 if past else 1

    def body(w_ref, own_ref, side_ref):
        dy = pl.program_id(0)

        def side(y):
            for x in range(n_x):
                for t in range(times):
                    side_ref[y, t * ci : (t + 1) * ci, x * co : (x + 1) * co] = w_ref[t, 0, x]

        def own(row, y):
            for x in range(n_x):
                for t in range(times):
                    lo = (row * times + t) * ci
                    at = y * wide + x * co
                    own_ref[lo : lo + ci, at : at + co] = w_ref[t, 0, x]

        @pl.when(dy == 0)
        def _():
            side(0)
            own(0, 1)

        @pl.when(dy == 1)
        def _():
            own(0, 0)
            own(1, 1)

        @pl.when(dy == 2)
        def _():
            side(1)
            own(1, 0)

    shapes = [(2 * times * ci, 2 * wide), (2, times * ci, wide)]
    first = 0 if past else n_t - 1
    return pl.pallas_call(
        body,
        grid=(n_y,),
        in_specs=[pl.BlockSpec((times, 1, n_x, ci, co), lambda y: (first, y, 0, 0, 0))],
        out_specs=[pl.BlockSpec(memory_space=pltpu.VMEM) for _ in shapes],
        out_shape=[jax.ShapeDtypeStruct(shape, weight.dtype) for shape in shapes],
        cost_estimate=pl.CostEstimate(flops=0, bytes_accessed=4 * weight.size, transcendentals=0),
        compiler_params=pltpu.CompilerParams(vmem_limit_bytes=16 << 20),
    )(weight)


def activated(values, gain):
    u = values * lax.rsqrt(jnp.mean(values * values, axis=-1, keepdims=True) + 1e-06) * gain
    return u / (1.0 + jnp.exp(-u))


def first_activation(frame, gain):
    n_slots, n_rows, n_cols, ch = frame.shape

    def body(f_ref, g_ref, o_ref, top_ref, bottom_ref):
        for s in range(n_slots):
            for r in range(n_rows):
                value = activated(f_ref[s, r].astype(jnp.float32), g_ref[...]).astype(jnp.bfloat16)
                o_ref[s, r] = value
                if r == 0:
                    top_ref[s] = value
                if r == n_rows - 1:
                    bottom_ref[s] = value

    row = jax.ShapeDtypeStruct((n_slots, n_cols, ch), jnp.bfloat16)
    return call(
        body,
        [jax.ShapeDtypeStruct(frame.shape, jnp.bfloat16), row, row],
        (frame, gain),
        flops=10 * frame.size,
        moved=6 * frame.size,
    )


def folded(acc, ch, cols_first):
    tiles = acc.shape[0] // CB
    n_slots = 4
    blocks = tiles // n_slots
    lead = (blocks, n_slots) if cols_first else (n_slots, blocks)
    axis = 0 if cols_first else 1

    def plane(k):
        value = acc[:, k * ch : (k + 1) * ch].reshape(tiles, CB, ch)
        return value

    at = lax.broadcasted_iota(jnp.int32, (1, 1, CB, ch), 2)
    before = pltpu.roll(plane(0), 1, 1).reshape(lead + (CB, ch))
    after = pltpu.roll(plane(2), CB - 1, 1).reshape(lead + (CB, ch))
    gap = list(lead) + [CB, ch]
    gap[axis] = 1
    gap = jnp.zeros(gap, jnp.float32)
    before_prev = jnp.concatenate([gap, lax.slice_in_dim(before, 0, blocks - 1, axis=axis)], axis)
    after_next = jnp.concatenate([lax.slice_in_dim(after, 1, blocks, axis=axis), gap], axis)
    total = plane(1).reshape(lead + (CB, ch))
    total += jnp.where(at == 0, before_prev, before)
    total += jnp.where(at == CB - 1, after_next, after)
    return total


def add_into(o_ref, y, total, cols_first, base=None):
    if cols_first:
        o_ref[y] = total if base is None else base[y] + total
        return
    for s in range(total.shape[0]):
        o_ref[y, :, s] = total[s] if base is None else base[y, :, s] + total[s]


def masked(table_ref, k, s, value):
    return jnp.where(table_ref[24 + 4 * k + s] != 0, value, jnp.zeros_like(value))


def frame_of(table_ref, s, f, ref):
    at = table_ref[16 + 2 * s + f]
    here = jnp.maximum(at, 0)
    value = ref[lax.div(here, 4), :, lax.rem(here, 4)]
    return jnp.where(at >= 0, value, jnp.zeros_like(value))


def dot(a, b):
    return jnp.dot(a, b, preferred_element_type=jnp.float32)


def sums_shape(blocks, n_slots, n_rows, ch):
    return jax.ShapeDtypeStruct((n_rows, blocks, n_slots, CB, ch), jnp.float32)


def add_sides(edge_ref, sides, w_ref, lhs, o_ref):
    n_slots, n_cols, ch = sides[0].shape
    for y, side in enumerate(sides):
        for s in range(n_slots):
            lhs[s * n_cols : (s + 1) * n_cols] = masked(edge_ref, y, s, side[s])
        add_into(o_ref, y, folded(dot(lhs[...], w_ref[y]), ch, False), False, o_ref)


def add_own(act_ref, w_ref, lhs, o_ref, base):
    n_slots, n_rows, n_cols, ch = act_ref.shape
    for s in range(n_slots):
        for r in range(n_rows):
            lhs[s * n_cols : (s + 1) * n_cols, r * ch : (r + 1) * ch] = act_ref[s, r]
    both = dot(lhs[...], w_ref[...])
    wide = both.shape[1] // 2
    for y in range(n_rows):
        add_into(o_ref, y, folded(both[:, y * wide : (y + 1) * wide], ch, False), False, base)


def current_part(act, above, below, w_own, w_sides, edges):
    n_slots, n_rows, n_cols, ch = act.shape
    half = n_slots * n_cols

    def body(edge_ref, act_ref, above_ref, below_ref, wo_ref, ws_ref, o_ref, lhs, side):
        add_own(act_ref, wo_ref, lhs, o_ref, None)
        add_sides(edge_ref, (above_ref, below_ref), ws_ref, side, o_ref)

    return call(
        body,
        [sums_shape(n_cols // CB, n_slots, n_rows, ch)],
        (act, above, below, w_own, w_sides),
        scalars=(edges,),
        scratch=[
            pltpu.VMEM((half, n_rows * ch), jnp.bfloat16),
            pltpu.VMEM((half, ch), jnp.bfloat16),
        ],
        flops=2 * half * (w_own.size + w_sides.size),
        moved=2 * w_own.size + 8 * act.size,
    )[0]


def own_part(got, weights, sums, act, table):
    n_rows, _, n_frames, blocks, _, _, ch = got.shape
    n_slots = act.shape[0]
    half = blocks * n_slots * CB
    deep = n_frames * ch
    parts = 3
    whole = weights[0]
    part = whole.shape[1] // parts

    def body(table_ref, got_ref, w0_ref, w1_ref, z_ref, act_ref, o0_ref, o1_ref, n1_ref, n2_ref, w, lhs, acc, sems, keep_sems, act_sem):
        loads = []
        for k, src in enumerate((w0_ref, w1_ref)):
            for p in range(parts):
                cols = pl.ds(p * part, part)
                n = k * parts + p
                loads.append(pltpu.make_async_copy(src.at[:, cols], w.at[n], sems.at[n]))
        for n in range(parts):
            loads[n].start()
        keeps = [pltpu.make_async_copy(act_ref, n1_ref.at[:, 1], act_sem)]
        for k, dst in enumerate((n1_ref, n2_ref)):
            for r in range(n_rows):
                for s in range(n_slots):
                    for f in range(n_frames):
                        lo = r * deep + f * ch
                        lhs[k, :, s, :, lo : lo + ch] = frame_of(table_ref, s, f, got_ref.at[r, k])
                    n = (k * n_rows + r) * n_slots + s
                    cols = pl.ds(r * deep + (n_frames - 1) * ch, ch)
                    keeps.append(
                        pltpu.make_async_copy(
                            lhs.at[k, :, s, :, cols], dst.at[s, 0, r], keep_sems.at[n]
                        )
                    )
        for k, (o_ref, base) in enumerate(((o0_ref, z_ref), (o1_ref, None))):
            rows = lhs[k].reshape(half, n_rows * deep)
            for p in range(parts):
                n = k * parts + p
                loads[n].wait()
                if n + parts < len(loads):
                    loads[n + parts].start()
                if n == parts:
                    for c in keeps:
                        c.start()
                acc[:, p * part : (p + 1) * part] = dot(rows, w[n])
            wide = whole.shape[1] // 2
            for y in range(n_rows):
                total = folded(acc[:, y * wide : (y + 1) * wide], ch, True)
                add_into(o_ref, y, total, True, base)
        for c in keeps:
            c.wait()

    out = sums_shape(blocks, n_slots, n_rows, ch)
    nxt = jax.ShapeDtypeStruct((n_slots, 2, n_rows, blocks, CB, ch), jnp.bfloat16)
    return call(
        body,
        [out, out, nxt, nxt],
        (got, *weights, sums, act),
        scalars=(table,),
        scratch=[
            pltpu.VMEM((2 * parts, whole.shape[0], part), whole.dtype),
            pltpu.VMEM((2, blocks, n_slots, CB, n_rows * deep), jnp.bfloat16),
            pltpu.VMEM((half, whole.shape[1]), jnp.float32),
            pltpu.SemaphoreType.DMA((2 * parts,)),
            pltpu.SemaphoreType.DMA((2 * n_rows * n_slots,)),
            pltpu.SemaphoreType.DMA,
        ],
        flops=4 * half * whole.size,
        moved=4 * whole.size,
        far=(1, 2),
        far_out=(2, 3),
        limit=46 << 20,
    )


def side_sums(table_ref, k, side_ref, w, lhs):
    n_frames, blocks, _, _, ch = side_ref.shape
    n_slots = lhs.shape[1]
    for s in range(n_slots):
        for f in range(n_frames):
            value = masked(table_ref, k, s, frame_of(table_ref, s, f, side_ref))
            lhs[:, s, :, f * ch : (f + 1) * ch] = value
    half = blocks * n_slots * CB
    return folded(dot(lhs[...].reshape(half, n_frames * ch), w), ch, True)


def second_activation(above, below, w_sides, sums, bias, gain, edges):
    n_frames, blocks, _, _, ch = above.shape
    n_rows, n_slots = sums.shape[0], sums.shape[2]
    n_cols, deep = blocks * CB, n_frames * ch

    def body(edge_ref, above_ref, below_ref, w_ref, z_ref, b_ref, g_ref, o_ref, top_ref, bottom_ref, lhs):
        for y, side in enumerate((above_ref, below_ref)):
            total = side_sums(edge_ref, y, side, w_ref[y], lhs) + z_ref[y] + b_ref[...]
            for s in range(n_slots):
                value = activated(total[:, s].reshape(n_cols, ch), g_ref[...]).astype(jnp.bfloat16)
                o_ref[s, y] = value
                if y == 0:
                    top_ref[s] = value
                else:
                    bottom_ref[s] = value

    row = jax.ShapeDtypeStruct((n_slots, n_cols, ch), jnp.bfloat16)
    return call(
        body,
        [jax.ShapeDtypeStruct((n_slots, n_rows, n_cols, ch), jnp.bfloat16), row, row],
        (above, below, w_sides, sums, bias, gain),
        scalars=(edges,),
        scratch=[pltpu.VMEM((blocks, n_slots, CB, deep), jnp.bfloat16)],
        flops=2 * n_slots * n_cols * w_sides.size,
        moved=2 * w_sides.size,
    )


def before_sides(above, below, act, w_sides, w_act, sums, kept, edges):
    n_frames, blocks, _, _, ch = above.shape
    n_rows, n_slots = sums.shape[0], sums.shape[2]
    n_cols, deep = blocks * CB, n_frames * ch

    def body(edge_ref, above_ref, below_ref, act_ref, tiles_ref, w_ref, wa_ref, z_ref, kept_ref, o_ref, next_ref, lhs, lhs2, sem):
        copy = pltpu.make_async_copy(tiles_ref, next_ref.at[:, 1], sem)
        copy.start()
        add_own(act_ref, wa_ref, lhs2, o_ref, z_ref)
        for y, side in enumerate((above_ref, below_ref)):
            o_ref[y] += side_sums(edge_ref, y, side, w_ref[y], lhs)
        copy.wait()

    return call(
        body,
        [jax.ShapeDtypeStruct(sums.shape, jnp.float32), jax.ShapeDtypeStruct(kept.shape, kept.dtype)],
        (above, below, act, act.reshape(n_slots, n_rows, blocks, CB, ch), w_sides, w_act, sums, kept),
        scalars=(edges,),
        scratch=[
            pltpu.VMEM((blocks, n_slots, CB, deep), jnp.bfloat16),
            pltpu.VMEM((n_slots * n_cols, n_rows * ch), jnp.bfloat16),
            pltpu.SemaphoreType.DMA,
        ],
        flops=2 * n_slots * n_cols * (w_sides.size + w_act.size),
        moved=2 * (w_sides.size + w_act.size),
        far=(7,),
        far_out=(1,),
        aliases={8: 1},
    )


def last_part(above, below, w_sides, sums, bias, frame, edges):
    n_slots, n_rows, n_cols, ch = frame.shape

    def body(edge_ref, above_ref, below_ref, w_ref, z_ref, b_ref, f_ref, o_ref, lhs):
        for y, side in enumerate((above_ref, below_ref)):
            for s in range(n_slots):
                lhs[s * n_cols : (s + 1) * n_cols] = masked(edge_ref, y, s, side[s])
            total = folded(dot(lhs[...], w_ref[y]), ch, False)
            for s in range(n_slots):
                value = (total[s] + z_ref[y, :, s] + b_ref[...]).reshape(n_cols, ch)
                o_ref[s, y] = (value + f_ref[s, y].astype(jnp.float32)).astype(jnp.bfloat16)

    return call(
        body,
        [jax.ShapeDtypeStruct(frame.shape, jnp.bfloat16)],
        (above, below, w_sides, sums, bias, frame),
        scalars=(edges,),
        scratch=[pltpu.VMEM((n_slots * n_cols, ch), jnp.bfloat16)],
        flops=2 * n_slots * n_cols * w_sides.size,
        moved=2 * w_sides.size,
    )[0]


def local(
    frame_in,
    cache_first,
    cache_second,
    gain_first,
    gain_second,
    conv_first,
    conv_second,
    bias_first,
    bias_second,
    old_slot,
    new_slot,
    old_shift,
    new_shift,
    frame_count,
):
    n_slots, n_rows, n_cols, ch = frame_in.shape
    n_groups = lax.axis_size("stream")
    n_tiles = lax.axis_size("tile")
    my_group = lax.axis_index("stream")
    my_tile = lax.axis_index("tile")
    blocks = n_cols // CB
    my_colour = ((my_group * n_tiles + my_tile) // blocks) % 2
    place = jnp.stack([my_group, my_tile, my_colour, jnp.int32(n_tiles)]).astype(jnp.int32)
    table, source, rotation, valid = plan(
        old_slot, new_slot, old_shift, new_shift, frame_count, place
    )
    down = [(i, (i + 1) % n_tiles) for i in range(n_tiles)]
    up = [((i + 1) % n_tiles, i) for i in range(n_tiles)]

    def from_above(row):
        return lax.ppermute(row, "tile", down)

    def from_below(row):
        return lax.ppermute(row, "tile", up)

    def run(depth, conv_first, conv_second):
        pieces = (n_groups * n_tiles, depth, CB, ch)
        sent = pack(cache_first, cache_second, table, depth).reshape(pieces)
        held = lax.all_to_all(sent, BOTH, 0, 0, tiled=True)

        act_own_1, act_sides_1 = spread(conv_first, False)
        act_own_2, act_sides_2 = spread(conv_second, False)
        own_2, sides_2 = spread(conv_second, True)
        act_first, top, bottom = first_activation(frame_in, gain_first[None])
        act_above, act_below = from_above(bottom), from_below(top)
        (
            held, act_first, act_above, act_below, act_own_1, act_sides_1, act_own_2, act_sides_2, own_2, sides_2,
        ) = lax.optimization_barrier((
            held, act_first, act_above, act_below, act_own_1, act_sides_1, act_own_2, act_sides_2, own_2, sides_2,
        ))

        moved = permute(
            held.reshape(n_groups, n_tiles, depth, CB, ch), source, rotation, valid
        ).reshape(pieces)
        moved, act_later = lax.optimization_barrier((moved, act_first))
        got = lax.all_to_all(moved, BOTH, 0, 0, tiled=True)
        sums_1 = current_part(act_later, act_above, act_below, act_own_1, act_sides_1, table)
        sums_1, conv_first = lax.optimization_barrier((sums_1, conv_first))
        own_1, sides_1 = spread(conv_first, True)
        got, sums_1, own_1, sides_1 = lax.optimization_barrier((got, sums_1, own_1, sides_1))
        got = got.reshape(n_rows, 2, 2, blocks, depth, CB, ch)

        above_1 = from_above(got[n_rows - 1, 0])
        below_1 = from_below(got[0, 0])
        above_2 = from_above(got[n_rows - 1, 1])
        below_2 = from_below(got[0, 1])
        act_tiles = act_first.reshape(n_slots, n_rows, blocks, CB, ch)
        sums_1, sums_2, next_first, kept = own_part(got, (own_1, own_2), sums_1, act_tiles, table)
        act_second, top, bottom = second_activation(
            above_1, below_1, sides_1, sums_1, bias_first[None], gain_second[None], table
        )
        side_above, side_below = from_above(bottom), from_below(top)
        sums_2, next_second = before_sides(
            above_2, below_2, act_second, sides_2, act_own_2, sums_2, kept, table
        )
        mixed_frame = last_part(
            side_above, side_below, act_sides_2, sums_2, bias_second[None], frame_in, table
        )
        return mixed_frame, next_first, next_second

    def branch(depth):
        return lambda first, second: run(depth, first, second)

    mixed_frame, next_first, next_second = lax.switch(
        jnp.clip(table[0] - 2, 0, 2), [branch(2), branch(3), branch(4)], conv_first, conv_second
    )
    whole = (n_slots, 2, n_rows, n_cols, ch)
    return (mixed_frame, next_first.reshape(whole), next_second.reshape(whole))


def solution(mesh):
    frame = P("stream", "tile", None, None)
    cache = P("stream", None, "tile", None, None)
    return jax.shard_map(
        local,
        mesh=mesh,
        in_specs=(frame, cache, cache) + (P(),) * 11,
        out_specs=(frame, cache, cache),
        check_vma=False,
    )
```

```python
import jax
import jax.numpy as jnp
from jax import lax
from jax.experimental import pallas as pl
from jax.experimental.pallas import tpu as pltpu
from jax.sharding import PartitionSpec as P

BOTH = ("stream", "tile")
CB = 8


def lookup(held_table, values):
    return jnp.sum(jnp.where(held_table, values[None, :], 0), axis=1)


def pack(first, second):
    n_slots, n_frames, n_rows, n_cols, ch = first.shape
    blocks = n_cols // CB

    def body(a_ref, b_ref, o_ref):
        for k, ref in enumerate((a_ref, b_ref)):
            for f in range(n_frames):
                for r in range(n_rows):
                    o_ref[r, k, f, :, 0] = ref[0, f, r].reshape(blocks, CB, ch)

    spec = pl.BlockSpec((1, n_frames, n_rows, n_cols, ch), lambda s: (s, 0, 0, 0, 0))
    return pl.pallas_call(
        body,
        grid=(n_slots,),
        in_specs=[spec, spec],
        out_specs=pl.BlockSpec(
            (n_rows, 2, n_frames, blocks, 1, CB, ch), lambda s: (0, 0, 0, 0, s, 0, 0)
        ),
        out_shape=jax.ShapeDtypeStruct(
            (n_rows, 2, n_frames, blocks, n_slots, CB, ch), first.dtype
        ),
        compiler_params=pltpu.CompilerParams(vmem_limit_bytes=58 << 20),
    )(first, second)


def permute(held, source, rotation, keep):
    n_groups, n_tiles, n_slots, cols, ch = held.shape

    def body(source_ref, rotation_ref, keep_ref, i_ref, o_ref):
        def stream(n, _):
            by = rotation_ref[n]
            old = source_ref[n]
            to, slot = lax.div(n, n_slots), lax.rem(n, n_slots)
            of, place = lax.div(old, n_slots), lax.rem(old, n_slots)

            @pl.when(keep_ref[n] != 0)
            def _():
                for t in range(n_tiles):
                    at = lax.rem(t + n_tiles - by, n_tiles)
                    o_ref[to, t, slot] = i_ref[of, at, place]

            @pl.when(keep_ref[n] == 0)
            def _():
                o_ref[to, :, slot] = jnp.zeros((n_tiles, cols, ch), o_ref.dtype)

            return 0

        lax.fori_loop(0, n_groups * n_slots, stream, 0)

    smem, vmem = pl.BlockSpec(memory_space=pltpu.SMEM), pl.BlockSpec(memory_space=pltpu.VMEM)
    return pl.pallas_call(
        body,
        in_specs=[smem, smem, smem, vmem],
        out_specs=vmem,
        out_shape=jax.ShapeDtypeStruct(held.shape, held.dtype),
        compiler_params=pltpu.CompilerParams(vmem_limit_bytes=16 << 20),
    )(source, rotation, keep, held)


VMEM_LIMIT = 16 << 20


def call(body, out_shape, operands, scalars=(), scratch=(), flops=0, moved=0, far=(), far_out=(), aliases=None):
    in_specs = [pl.BlockSpec(memory_space=pltpu.SMEM) for _ in scalars]
    for k, _ in enumerate(operands):
        in_specs.append(pl.BlockSpec(memory_space=pl.ANY if k in far else pltpu.VMEM))
    out_specs = []
    for k, _ in enumerate(out_shape):
        out_specs.append(pl.BlockSpec(memory_space=pl.ANY if k in far_out else pltpu.VMEM))
    return pl.pallas_call(
        body,
        in_specs=in_specs,
        out_specs=out_specs,
        out_shape=list(out_shape),
        scratch_shapes=list(scratch),
        input_output_aliases=aliases or {},
        cost_estimate=pl.CostEstimate(flops=flops, bytes_accessed=moved, transcendentals=0),
        compiler_params=pltpu.CompilerParams(vmem_limit_bytes=VMEM_LIMIT),
    )(*scalars, *operands)


def spread_own(weight, first, times):
    _, n_y, n_x, ci, co = weight.shape
    wide = n_x * co

    def body(w_ref, o_ref):
        dy = pl.program_id(0)

        def fill(row, y):
            for x in range(n_x):
                for t in range(times):
                    lo = (row * times + t) * ci
                    at = y * wide + x * co
                    o_ref[lo : lo + ci, at : at + co] = w_ref[t, 0, x]

        @pl.when(dy == 0)
        def _():
            fill(0, 1)

        @pl.when(dy == 1)
        def _():
            fill(0, 0)
            fill(1, 1)

        @pl.when(dy == 2)
        def _():
            fill(1, 0)

    return pl.pallas_call(
        body,
        grid=(n_y,),
        in_specs=[
            pl.BlockSpec((times, 1, n_x, ci, co), lambda y: (first // times, y, 0, 0, 0))
        ],
        out_specs=pl.BlockSpec(memory_space=pltpu.VMEM),
        out_shape=jax.ShapeDtypeStruct((2 * times * ci, 2 * wide), weight.dtype),
        cost_estimate=pl.CostEstimate(flops=0, bytes_accessed=4 * weight.size, transcendentals=0),
        compiler_params=pltpu.CompilerParams(vmem_limit_bytes=16 << 20),
    )(weight)


def spread_sides(weight, first, times):
    _, _, n_x, ci, co = weight.shape

    def body(w_ref, o_ref):
        for x in range(n_x):
            for t in range(times):
                o_ref[0, t * ci : (t + 1) * ci, x * co : (x + 1) * co] = w_ref[t, 0, x]

    return pl.pallas_call(
        body,
        grid=(2,),
        in_specs=[
            pl.BlockSpec((times, 1, n_x, ci, co), lambda y: (first // times, 2 * y, 0, 0, 0))
        ],
        out_specs=pl.BlockSpec((1, times * ci, n_x * co), lambda y: (y, 0, 0)),
        out_shape=jax.ShapeDtypeStruct((2, times * ci, n_x * co), weight.dtype),
        cost_estimate=pl.CostEstimate(flops=0, bytes_accessed=4 * weight.size, transcendentals=0),
        compiler_params=pltpu.CompilerParams(vmem_limit_bytes=16 << 20),
    )(weight)


def activated(values, gain):
    u = values * lax.rsqrt(jnp.mean(values * values, axis=-1, keepdims=True) + 1e-06) * gain
    return u / (1.0 + jnp.exp(-u))


def first_activation(frame, gain):
    n_slots, n_rows, n_cols, ch = frame.shape

    def body(f_ref, g_ref, o_ref, top_ref, bottom_ref):
        for s in range(n_slots):
            for r in range(n_rows):
                value = activated(f_ref[s, r].astype(jnp.float32), g_ref[...]).astype(jnp.bfloat16)
                o_ref[s, r] = value
                if r == 0:
                    top_ref[s] = value
                if r == n_rows - 1:
                    bottom_ref[s] = value

    row = jax.ShapeDtypeStruct((n_slots, n_cols, ch), jnp.bfloat16)
    return call(
        body,
        [jax.ShapeDtypeStruct(frame.shape, jnp.bfloat16), row, row],
        (frame, gain),
        flops=10 * frame.size,
        moved=6 * frame.size,
    )


def folded(acc, ch, cols_first):
    tiles = acc.shape[0] // CB
    n_slots = 4
    blocks = tiles // n_slots
    lead = (blocks, n_slots) if cols_first else (n_slots, blocks)
    axis = 0 if cols_first else 1

    def plane(k):
        value = acc[:, k * ch : (k + 1) * ch].reshape(tiles, CB, ch)
        return value

    at = lax.broadcasted_iota(jnp.int32, (1, 1, CB, ch), 2)
    before = pltpu.roll(plane(0), 1, 1).reshape(lead + (CB, ch))
    after = pltpu.roll(plane(2), CB - 1, 1).reshape(lead + (CB, ch))
    gap = list(lead) + [CB, ch]
    gap[axis] = 1
    gap = jnp.zeros(gap, jnp.float32)
    before_prev = jnp.concatenate([gap, lax.slice_in_dim(before, 0, blocks - 1, axis=axis)], axis)
    after_next = jnp.concatenate([lax.slice_in_dim(after, 1, blocks, axis=axis), gap], axis)
    total = plane(1).reshape(lead + (CB, ch))
    total += jnp.where(at == 0, before_prev, before)
    total += jnp.where(at == CB - 1, after_next, after)
    return total


def add_into(o_ref, y, total, cols_first, base=None):
    if cols_first:
        o_ref[y] = total if base is None else base[y] + total
        return
    for s in range(total.shape[0]):
        o_ref[y, :, s] = total[s] if base is None else base[y, :, s] + total[s]


def masked(edge_ref, k, s, value):
    return jnp.where(edge_ref[k, s] != 0, value, jnp.zeros_like(value))


def dot(a, b):
    return jnp.dot(a, b, preferred_element_type=jnp.float32)


def sums_shape(blocks, n_slots, n_rows, ch):
    return jax.ShapeDtypeStruct((n_rows, blocks, n_slots, CB, ch), jnp.float32)


def add_own(act_ref, w_ref, lhs, o_ref, base):
    n_slots, n_rows, n_cols, ch = act_ref.shape
    for s in range(n_slots):
        for r in range(n_rows):
            lhs[s * n_cols : (s + 1) * n_cols, r * ch : (r + 1) * ch] = act_ref[s, r]
    both = dot(lhs[...], w_ref[...])
    wide = both.shape[1] // 2
    for y in range(n_rows):
        add_into(o_ref, y, folded(both[:, y * wide : (y + 1) * wide], ch, False), False, base)


def current_part(act, w_own):
    n_slots, n_rows, n_cols, ch = act.shape
    half = n_slots * n_cols

    def body(act_ref, w_ref, o_ref, lhs):
        add_own(act_ref, w_ref, lhs, o_ref, None)

    return call(
        body,
        [sums_shape(n_cols // CB, n_slots, n_rows, ch)],
        (act, w_own),
        scratch=[pltpu.VMEM((half, n_rows * ch), jnp.bfloat16)],
        flops=2 * half * w_own.size,
        moved=2 * w_own.size + 8 * act.size,
    )[0]


def own_part(got, weights, sums, act):
    n_rows, n_caches, n_frames, blocks, n_slots, _, ch = got.shape
    half = blocks * n_slots * CB
    deep = n_frames * ch
    whole = weights[0]

    def body(got_ref, w0_ref, w1_ref, z_ref, act_ref, o0_ref, o1_ref, n1_ref, n2_ref, lhs, sems, act_sem):
        keeps = []
        for k, dst in enumerate((n1_ref, n2_ref)):
            for r in range(n_rows):
                for s in range(n_slots):
                    n = (k * n_rows + r) * n_slots + s
                    keeps.append(
                        pltpu.make_async_copy(
                            got_ref.at[r, k, n_frames - 1, :, s], dst.at[s, 0, r], sems.at[n]
                        )
                    )
        keeps.append(pltpu.make_async_copy(act_ref, n1_ref.at[:, 1], act_sem))
        for c in keeps:
            c.start()
        for k, (w, o_ref, base) in enumerate(((w0_ref, o0_ref, z_ref), (w1_ref, o1_ref, None))):
            for r in range(n_rows):
                for f in range(n_frames):
                    lo = r * deep + f * ch
                    lhs[:, lo : lo + ch] = got_ref[r, k, f].reshape(half, ch)
            both = dot(lhs[...], w[...])
            wide = both.shape[1] // 2
            for y in range(n_rows):
                total = folded(both[:, y * wide : (y + 1) * wide], ch, True)
                add_into(o_ref, y, total, True, base)
        for c in keeps:
            c.wait()

    out = sums_shape(blocks, n_slots, n_rows, ch)
    nxt = jax.ShapeDtypeStruct((n_slots, 2, n_rows, blocks, CB, ch), jnp.bfloat16)
    return call(
        body,
        [out, out, nxt, nxt],
        (got, *weights, sums, act),
        scratch=[
            pltpu.VMEM((half, n_rows * deep), jnp.bfloat16),
            pltpu.SemaphoreType.DMA((2 * n_rows * n_slots,)),
            pltpu.SemaphoreType.DMA,
        ],
        flops=4 * half * whole.size,
        moved=4 * whole.size,
        far_out=(2, 3),
    )


def side_sums(edge_ref, k, side_ref, w, lhs, current=None):
    n_frames, blocks, n_slots, _, ch = side_ref.shape
    for s in range(n_slots):
        for f in range(n_frames):
            value = masked(edge_ref, k, s, side_ref[f, :, s])
            lhs[:, s, :, f * ch : (f + 1) * ch] = value
        if current is not None:
            value = masked(edge_ref, k, s, current[s]).reshape(blocks, CB, ch)
            lhs[:, s, :, n_frames * ch : (n_frames + 1) * ch] = value
    half = blocks * n_slots * CB
    return folded(dot(lhs[...].reshape(half, lhs.shape[3]), w), ch, True)


def second_activation(above, below, act_above, act_below, w_sides, sums, bias, gain, edges):
    n_frames, blocks, n_slots, _, ch = above.shape
    n_rows, n_cols, deep = sums.shape[0], blocks * CB, n_frames * ch

    def body(edge_ref, above_ref, below_ref, aa_ref, ab_ref, w_ref, z_ref, b_ref, g_ref, o_ref, top_ref, bottom_ref, lhs):
        for y, (side, row) in enumerate(((above_ref, aa_ref), (below_ref, ab_ref))):
            total = side_sums(edge_ref, y, side, w_ref[y], lhs, row) + z_ref[y] + b_ref[...]
            for s in range(n_slots):
                value = activated(total[:, s].reshape(n_cols, ch), g_ref[...]).astype(jnp.bfloat16)
                o_ref[s, y] = value
                if y == 0:
                    top_ref[s] = value
                else:
                    bottom_ref[s] = value

    row = jax.ShapeDtypeStruct((n_slots, n_cols, ch), jnp.bfloat16)
    return call(
        body,
        [jax.ShapeDtypeStruct((n_slots, n_rows, n_cols, ch), jnp.bfloat16), row, row],
        (above, below, act_above, act_below, w_sides, sums, bias, gain),
        scalars=(edges,),
        scratch=[pltpu.VMEM((blocks, n_slots, CB, deep + ch), jnp.bfloat16)],
        flops=2 * n_slots * n_cols * w_sides.size,
        moved=2 * w_sides.size,
    )


def before_sides(above, below, act, w_sides, w_act, sums, kept, edges):
    n_frames, blocks, n_slots, _, ch = above.shape
    n_rows, n_cols, deep = sums.shape[0], blocks * CB, n_frames * ch

    def body(edge_ref, above_ref, below_ref, act_ref, tiles_ref, w_ref, wa_ref, z_ref, kept_ref, o_ref, next_ref, lhs, lhs2, sem):
        copy = pltpu.make_async_copy(tiles_ref, next_ref.at[:, 1], sem)
        copy.start()
        add_own(act_ref, wa_ref, lhs2, o_ref, z_ref)
        for y, side in enumerate((above_ref, below_ref)):
            o_ref[y] += side_sums(edge_ref, y, side, w_ref[y], lhs)
        copy.wait()

    return call(
        body,
        [jax.ShapeDtypeStruct(sums.shape, jnp.float32), jax.ShapeDtypeStruct(kept.shape, kept.dtype)],
        (above, below, act, act.reshape(n_slots, n_rows, blocks, CB, ch), w_sides, w_act, sums, kept),
        scalars=(edges,),
        scratch=[
            pltpu.VMEM((blocks, n_slots, CB, deep), jnp.bfloat16),
            pltpu.VMEM((n_slots * n_cols, n_rows * ch), jnp.bfloat16),
            pltpu.SemaphoreType.DMA,
        ],
        flops=2 * n_slots * n_cols * (w_sides.size + w_act.size),
        moved=2 * (w_sides.size + w_act.size),
        far=(7,),
        far_out=(1,),
        aliases={8: 1},
    )


def last_part(above, below, w_sides, sums, bias, frame, edges):
    n_slots, n_rows, n_cols, ch = frame.shape

    def body(edge_ref, above_ref, below_ref, w_ref, z_ref, b_ref, f_ref, o_ref, lhs):
        for y, side in enumerate((above_ref, below_ref)):
            for s in range(n_slots):
                lhs[s * n_cols : (s + 1) * n_cols] = masked(edge_ref, y, s, side[s])
            total = folded(dot(lhs[...], w_ref[y]), ch, False)
            for s in range(n_slots):
                value = (total[s] + z_ref[y, :, s] + b_ref[...]).reshape(n_cols, ch)
                o_ref[s, y] = (value + f_ref[s, y].astype(jnp.float32)).astype(jnp.bfloat16)

    return call(
        body,
        [jax.ShapeDtypeStruct(frame.shape, jnp.bfloat16)],
        (above, below, w_sides, sums, bias, frame),
        scalars=(edges,),
        scratch=[pltpu.VMEM((n_slots * n_cols, ch), jnp.bfloat16)],
        flops=2 * n_slots * n_cols * w_sides.size,
        moved=2 * w_sides.size,
    )[0]


def local(
    frame_in,
    cache_first,
    cache_second,
    gain_first,
    gain_second,
    conv_first,
    conv_second,
    bias_first,
    bias_second,
    old_slot,
    new_slot,
    old_shift,
    new_shift,
    frame_count,
):
    n_slots, n_rows, n_cols, ch = frame_in.shape
    n_groups = lax.axis_size("stream")
    n_tiles = lax.axis_size("tile")
    my_group = lax.axis_index("stream")
    my_tile = lax.axis_index("tile")
    n_flight = old_slot.shape[0]
    blocks = n_cols // CB
    slot_ids = jnp.arange(n_flight, dtype=jnp.int32)
    held_new = new_slot[None, :] == slot_ids[:, None]
    source = lookup(held_new, old_slot)
    shift_after = lookup(held_new, new_shift)
    rotation = (shift_after - lookup(held_new, old_shift)) % n_tiles
    frames_done = lookup(held_new, frame_count)
    my_piece = my_group * n_tiles + my_tile
    my_frame = (my_piece // blocks) % 2
    keep = (frames_done >= 2 - my_frame).astype(jnp.int32)
    start = my_group * n_slots
    my_number = lax.dynamic_slice_in_dim((my_tile - shift_after) % n_tiles, start, n_slots)

    edges = jnp.stack([my_number != 0, my_number != n_tiles - 1]).astype(jnp.int32)
    down = [(i, (i + 1) % n_tiles) for i in range(n_tiles)]
    up = [((i + 1) % n_tiles, i) for i in range(n_tiles)]

    def from_above(row):
        return lax.ppermute(row, "tile", down)

    def from_below(row):
        return lax.ppermute(row, "tile", up)

    sent = pack(cache_first, cache_second).reshape(n_groups * n_tiles, n_slots, CB, ch)
    held = lax.all_to_all(sent, BOTH, 0, 0, tiled=True)

    act_own_1 = spread_own(conv_first, 2, 1)
    act_first, top, bottom = first_activation(frame_in, gain_first[None])
    act_above, act_below = from_above(bottom), from_below(top)
    sums_1 = current_part(act_first, act_own_1)
    own_1, sides_1 = spread_own(conv_first, 0, 2), spread_sides(conv_first, 0, 3)
    own_2, sides_2 = spread_own(conv_second, 0, 2), spread_sides(conv_second, 0, 2)
    act_own_2, act_sides_2 = spread_own(conv_second, 2, 1), spread_sides(conv_second, 2, 1)
    held, sums_1, own_1, sides_1, own_2, sides_2, act_own_2, act_sides_2 = lax.optimization_barrier(
        (held, sums_1, own_1, sides_1, own_2, sides_2, act_own_2, act_sides_2)
    )

    moved = permute(held.reshape(n_groups, n_tiles, n_slots, CB, ch), source, rotation, keep)
    got = lax.all_to_all(
        moved.reshape(n_groups * n_tiles, n_slots, CB, ch), BOTH, 0, 0, tiled=True
    )
    got = got.reshape(n_rows, 2, 2, blocks, n_slots, CB, ch)

    above_1 = from_above(got[n_rows - 1, 0])
    below_1 = from_below(got[0, 0])
    above_2 = from_above(got[n_rows - 1, 1])
    below_2 = from_below(got[0, 1])
    act_tiles = act_first.reshape(n_slots, n_rows, blocks, CB, ch)
    sums_1, sums_2, next_first, kept = own_part(got, (own_1, own_2), sums_1, act_tiles)
    act_second, top, bottom = second_activation(
        above_1, below_1, act_above, act_below, sides_1, sums_1, bias_first[None],
        gain_second[None], edges,
    )
    side_above, side_below = from_above(bottom), from_below(top)
    sums_2, next_second = before_sides(
        above_2, below_2, act_second, sides_2, act_own_2, sums_2, kept, edges
    )
    mixed_frame = last_part(
        side_above, side_below, act_sides_2, sums_2, bias_second[None], frame_in, edges
    )
    whole = (n_slots, 2, n_rows, n_cols, ch)
    return (mixed_frame, next_first.reshape(whole), next_second.reshape(whole))


def solution(mesh):
    frame = P("stream", "tile", None, None)
    cache = P("stream", None, "tile", None, None)
    return jax.shard_map(
        local,
        mesh=mesh,
        in_specs=(frame, cache, cache) + (P(),) * 11,
        out_specs=(frame, cache, cache),
        check_vma=False,
    )
```

```python
import jax
import jax.numpy as jnp
from jax import lax
from jax.experimental import pallas as pl
from jax.experimental.pallas import tpu as pltpu
from jax.sharding import PartitionSpec as P

BOTH = ("stream", "tile")
CB = 8


def lookup(held_table, values):
    return jnp.sum(jnp.where(held_table, values[None, :], 0), axis=1)


def pack(first, second):
    n_slots, n_frames, n_rows, n_cols, ch = first.shape
    blocks = n_cols // CB
    parts = n_rows * 2 * n_frames

    def body(a_ref, b_ref, o_ref, held, in_sems, out_sems):
        whole = []
        for r in range(n_rows):
            for k, ref in enumerate((a_ref, b_ref)):
                for f in range(n_frames):
                    whole.append((r, k, f, ref))
        loads = []
        for p, (r, k, f, ref) in enumerate(whole):
            for s in range(n_slots):
                n = p * n_slots + s
                loads.append(
                    pltpu.make_async_copy(ref.at[s, f, r], held.at[r, k, f, :, s], in_sems.at[n])
                )
                loads[-1].start()
        stores = []
        for p, (r, k, f, _) in enumerate(whole):
            for s in range(n_slots):
                loads[p * n_slots + s].wait()
            stores.append(pltpu.make_async_copy(held.at[r, k, f], o_ref.at[r, k, f], out_sems.at[p]))
            stores[-1].start()
        for c in stores:
            c.wait()

    shape = (n_rows, 2, n_frames, blocks, n_slots, CB, ch)
    tiles = (n_slots, n_frames, n_rows, blocks, CB, ch)
    far = pl.BlockSpec(memory_space=pl.ANY)
    return pl.pallas_call(
        body,
        in_specs=[far, far],
        out_specs=far,
        out_shape=jax.ShapeDtypeStruct(shape, first.dtype),
        scratch_shapes=[
            pltpu.VMEM(shape, first.dtype),
            pltpu.SemaphoreType.DMA((parts * n_slots,)),
            pltpu.SemaphoreType.DMA((parts,)),
        ],
        compiler_params=pltpu.CompilerParams(vmem_limit_bytes=58 << 20),
    )(first.reshape(tiles), second.reshape(tiles))


def permute(held, source, rotation, keep):
    n_groups, n_tiles, n_slots, cols, ch = held.shape

    def body(source_ref, rotation_ref, keep_ref, i_ref, o_ref, made, sems):
        def stream(n, to):
            by = rotation_ref[n]
            old = source_ref[n]
            slot = lax.rem(n, n_slots)
            of, place = lax.div(old, n_slots), lax.rem(old, n_slots)

            @pl.when(keep_ref[n] != 0)
            def _():
                for t in range(n_tiles):
                    at = lax.rem(t + n_tiles - by, n_tiles)
                    made[to, t, slot] = i_ref[of, at, place]

            @pl.when(keep_ref[n] == 0)
            def _():
                made[to, :, slot] = jnp.zeros((n_tiles, cols, ch), made.dtype)

            return to

        copies = []
        for to in range(n_groups):
            lax.fori_loop(to * n_slots, (to + 1) * n_slots, stream, to)
            copies.append(pltpu.make_async_copy(made.at[to], o_ref.at[to], sems.at[to]))
            copies[-1].start()
        for c in copies:
            c.wait()

    smem = pl.BlockSpec(memory_space=pltpu.SMEM)
    return pl.pallas_call(
        body,
        in_specs=[smem, smem, smem, pl.BlockSpec(memory_space=pltpu.VMEM)],
        out_specs=pl.BlockSpec(memory_space=pl.ANY),
        out_shape=jax.ShapeDtypeStruct(held.shape, held.dtype),
        scratch_shapes=[
            pltpu.VMEM(held.shape, held.dtype),
            pltpu.SemaphoreType.DMA((n_groups,)),
        ],
        compiler_params=pltpu.CompilerParams(vmem_limit_bytes=52 << 20),
    )(source, rotation, keep, held)


VMEM_LIMIT = 16 << 20


def call(body, out_shape, operands, scalars=(), scratch=(), flops=0, moved=0, far=(), far_out=(), aliases=None, limit=VMEM_LIMIT):
    in_specs = [pl.BlockSpec(memory_space=pltpu.SMEM) for _ in scalars]
    for k, _ in enumerate(operands):
        in_specs.append(pl.BlockSpec(memory_space=pl.ANY if k in far else pltpu.VMEM))
    out_specs = []
    for k, _ in enumerate(out_shape):
        out_specs.append(pl.BlockSpec(memory_space=pl.ANY if k in far_out else pltpu.VMEM))
    return pl.pallas_call(
        body,
        in_specs=in_specs,
        out_specs=out_specs,
        out_shape=list(out_shape),
        scratch_shapes=list(scratch),
        input_output_aliases=aliases or {},
        cost_estimate=pl.CostEstimate(flops=flops, bytes_accessed=moved, transcendentals=0),
        compiler_params=pltpu.CompilerParams(vmem_limit_bytes=limit),
    )(*scalars, *operands)


def spread(weight, past):
    n_t, n_y, n_x, ci, co = weight.shape
    wide = n_x * co
    times = n_t - 1 if past else 1

    def body(w_ref, own_ref, side_ref):
        dy = pl.program_id(0)

        def side(y):
            for x in range(n_x):
                for t in range(times):
                    side_ref[y, t * ci : (t + 1) * ci, x * co : (x + 1) * co] = w_ref[t, 0, x]

        def own(row, y):
            for x in range(n_x):
                for t in range(times):
                    lo = (row * times + t) * ci
                    at = y * wide + x * co
                    own_ref[lo : lo + ci, at : at + co] = w_ref[t, 0, x]

        @pl.when(dy == 0)
        def _():
            side(0)
            own(0, 1)

        @pl.when(dy == 1)
        def _():
            own(0, 0)
            own(1, 1)

        @pl.when(dy == 2)
        def _():
            side(1)
            own(1, 0)

    shapes = [(2 * times * ci, 2 * wide), (2, times * ci, wide)]
    first = 0 if past else n_t - 1
    return pl.pallas_call(
        body,
        grid=(n_y,),
        in_specs=[pl.BlockSpec((times, 1, n_x, ci, co), lambda y: (first, y, 0, 0, 0))],
        out_specs=[pl.BlockSpec(memory_space=pltpu.VMEM) for _ in shapes],
        out_shape=[jax.ShapeDtypeStruct(shape, weight.dtype) for shape in shapes],
        cost_estimate=pl.CostEstimate(flops=0, bytes_accessed=4 * weight.size, transcendentals=0),
        compiler_params=pltpu.CompilerParams(vmem_limit_bytes=16 << 20),
    )(weight)


def activated(values, gain):
    u = values * lax.rsqrt(jnp.mean(values * values, axis=-1, keepdims=True) + 1e-06) * gain
    return u / (1.0 + jnp.exp(-u))


def first_activation(frame, gain):
    n_slots, n_rows, n_cols, ch = frame.shape

    def body(f_ref, g_ref, o_ref, top_ref, bottom_ref):
        for s in range(n_slots):
            for r in range(n_rows):
                value = activated(f_ref[s, r].astype(jnp.float32), g_ref[...]).astype(jnp.bfloat16)
                o_ref[s, r] = value
                if r == 0:
                    top_ref[s] = value
                if r == n_rows - 1:
                    bottom_ref[s] = value

    row = jax.ShapeDtypeStruct((n_slots, n_cols, ch), jnp.bfloat16)
    return call(
        body,
        [jax.ShapeDtypeStruct(frame.shape, jnp.bfloat16), row, row],
        (frame, gain),
        flops=10 * frame.size,
        moved=6 * frame.size,
    )


def folded(acc, ch, cols_first):
    tiles = acc.shape[0] // CB
    n_slots = 4
    blocks = tiles // n_slots
    lead = (blocks, n_slots) if cols_first else (n_slots, blocks)
    axis = 0 if cols_first else 1

    def plane(k):
        value = acc[:, k * ch : (k + 1) * ch].reshape(tiles, CB, ch)
        return value

    at = lax.broadcasted_iota(jnp.int32, (1, 1, CB, ch), 2)
    before = pltpu.roll(plane(0), 1, 1).reshape(lead + (CB, ch))
    after = pltpu.roll(plane(2), CB - 1, 1).reshape(lead + (CB, ch))
    gap = list(lead) + [CB, ch]
    gap[axis] = 1
    gap = jnp.zeros(gap, jnp.float32)
    before_prev = jnp.concatenate([gap, lax.slice_in_dim(before, 0, blocks - 1, axis=axis)], axis)
    after_next = jnp.concatenate([lax.slice_in_dim(after, 1, blocks, axis=axis), gap], axis)
    total = plane(1).reshape(lead + (CB, ch))
    total += jnp.where(at == 0, before_prev, before)
    total += jnp.where(at == CB - 1, after_next, after)
    return total


def add_into(o_ref, y, total, cols_first, base=None):
    if cols_first:
        o_ref[y] = total if base is None else base[y] + total
        return
    for s in range(total.shape[0]):
        o_ref[y, :, s] = total[s] if base is None else base[y, :, s] + total[s]


def masked(edge_ref, k, s, value):
    return jnp.where(edge_ref[k, s] != 0, value, jnp.zeros_like(value))


def dot(a, b):
    return jnp.dot(a, b, preferred_element_type=jnp.float32)


def sums_shape(blocks, n_slots, n_rows, ch):
    return jax.ShapeDtypeStruct((n_rows, blocks, n_slots, CB, ch), jnp.float32)


def add_sides(edge_ref, sides, w_ref, lhs, o_ref):
    n_slots, n_cols, ch = sides[0].shape
    for y, side in enumerate(sides):
        for s in range(n_slots):
            lhs[s * n_cols : (s + 1) * n_cols] = masked(edge_ref, y, s, side[s])
        add_into(o_ref, y, folded(dot(lhs[...], w_ref[y]), ch, False), False, o_ref)


def add_own(act_ref, w_ref, lhs, o_ref, base):
    n_slots, n_rows, n_cols, ch = act_ref.shape
    for s in range(n_slots):
        for r in range(n_rows):
            lhs[s * n_cols : (s + 1) * n_cols, r * ch : (r + 1) * ch] = act_ref[s, r]
    both = dot(lhs[...], w_ref[...])
    wide = both.shape[1] // 2
    for y in range(n_rows):
        add_into(o_ref, y, folded(both[:, y * wide : (y + 1) * wide], ch, False), False, base)


def current_part(act, above, below, w_own, w_sides, edges):
    n_slots, n_rows, n_cols, ch = act.shape
    half = n_slots * n_cols

    def body(edge_ref, act_ref, above_ref, below_ref, wo_ref, ws_ref, o_ref, lhs, side):
        add_own(act_ref, wo_ref, lhs, o_ref, None)
        add_sides(edge_ref, (above_ref, below_ref), ws_ref, side, o_ref)

    return call(
        body,
        [sums_shape(n_cols // CB, n_slots, n_rows, ch)],
        (act, above, below, w_own, w_sides),
        scalars=(edges,),
        scratch=[
            pltpu.VMEM((half, n_rows * ch), jnp.bfloat16),
            pltpu.VMEM((half, ch), jnp.bfloat16),
        ],
        flops=2 * half * (w_own.size + w_sides.size),
        moved=2 * w_own.size + 8 * act.size,
    )[0]


def own_part(got, weights, sums, act, sides):
    n_rows, n_caches, n_frames, blocks, n_slots, _, ch = got.shape
    half = blocks * n_slots * CB
    deep = n_frames * ch
    whole = weights[0]

    def body(got_ref, w0_ref, w1_ref, z_ref, act_ref, sides_ref, o0_ref, o1_ref, n1_ref, n2_ref, near_ref, w0, w1, lhs, acc, sems, keep_sems):
        loads = []
        for r in range(n_rows):
            rows = pl.ds(r * deep, deep)
            loads.append(pltpu.make_async_copy(w0_ref.at[rows], w0.at[r], sems.at[r]))
        loads.append(pltpu.make_async_copy(w1_ref, w1, sems.at[2]))
        near = pltpu.make_async_copy(sides_ref, near_ref, sems.at[3])
        keeps = [pltpu.make_async_copy(act_ref, n1_ref.at[:, 1], sems.at[4])]
        for k, dst in enumerate((n1_ref, n2_ref)):
            for r in range(n_rows):
                for s in range(n_slots):
                    n = (k * n_rows + r) * n_slots + s
                    keeps.append(
                        pltpu.make_async_copy(
                            got_ref.at[r, k, n_frames - 1, :, s], dst.at[s, 0, r], keep_sems.at[n]
                        )
                    )
        for c in loads:
            c.start()
        near.start()

        def fill(k, r, f):
            lo = r * deep + f * ch
            lhs[:, lo : lo + ch] = got_ref[r, k, f].reshape(half, ch)

        def give(o_ref, base):
            wide = whole.shape[1] // 2
            for y in range(n_rows):
                total = folded(acc[:, y * wide : (y + 1) * wide], ch, True)
                add_into(o_ref, y, total, True, base)

        for r in range(n_rows):
            for f in range(n_frames):
                fill(0, r, f)
        loads[0].wait()
        acc[...] = dot(lhs[:, 0:deep], w0[0])
        loads[1].wait()
        acc[...] += dot(lhs[:, deep : 2 * deep], w0[1])
        give(o0_ref, z_ref)
        for r in range(n_rows):
            for f in range(n_frames):
                fill(1, r, f)
        for c in keeps:
            c.start()
        loads[2].wait()
        acc[...] = dot(lhs[...], w1[...])
        give(o1_ref, None)
        for c in keeps:
            c.wait()
        near.wait()

    out = sums_shape(blocks, n_slots, n_rows, ch)
    nxt = jax.ShapeDtypeStruct((n_slots, 2, n_rows, blocks, CB, ch), jnp.bfloat16)
    return call(
        body,
        [out, out, nxt, nxt, jax.ShapeDtypeStruct(sides.shape, sides.dtype)],
        (got, *weights, sums, act, sides),
        scratch=[
            pltpu.VMEM((n_rows, deep, whole.shape[1]), whole.dtype),
            pltpu.VMEM(whole.shape, whole.dtype),
            pltpu.VMEM((half, n_rows * deep), jnp.bfloat16),
            pltpu.VMEM((half, whole.shape[1]), jnp.float32),
            pltpu.SemaphoreType.DMA((5,)),
            pltpu.SemaphoreType.DMA((2 * n_rows * n_slots,)),
        ],
        flops=4 * half * whole.size,
        moved=4 * whole.size,
        far=(1, 2, 5),
        far_out=(2, 3),
        limit=45 << 20,
    )


def side_sums(edge_ref, k, side_ref, w, lhs):
    n_frames, blocks, n_slots, _, ch = side_ref.shape
    for s in range(n_slots):
        for f in range(n_frames):
            value = masked(edge_ref, k, s, side_ref[f, :, s])
            lhs[:, s, :, f * ch : (f + 1) * ch] = value
    half = blocks * n_slots * CB
    return folded(dot(lhs[...].reshape(half, n_frames * ch), w), ch, True)


def second_activation(above, below, w_sides, sums, bias, gain, edges):
    n_frames, blocks, n_slots, _, ch = above.shape
    n_rows, n_cols, deep = sums.shape[0], blocks * CB, n_frames * ch

    def body(edge_ref, above_ref, below_ref, w_ref, z_ref, b_ref, g_ref, o_ref, top_ref, bottom_ref, lhs):
        for y, side in enumerate((above_ref, below_ref)):
            total = side_sums(edge_ref, y, side, w_ref[y], lhs) + z_ref[y] + b_ref[...]
            for s in range(n_slots):
                value = activated(total[:, s].reshape(n_cols, ch), g_ref[...]).astype(jnp.bfloat16)
                o_ref[s, y] = value
                if y == 0:
                    top_ref[s] = value
                else:
                    bottom_ref[s] = value

    row = jax.ShapeDtypeStruct((n_slots, n_cols, ch), jnp.bfloat16)
    return call(
        body,
        [jax.ShapeDtypeStruct((n_slots, n_rows, n_cols, ch), jnp.bfloat16), row, row],
        (above, below, w_sides, sums, bias, gain),
        scalars=(edges,),
        scratch=[pltpu.VMEM((blocks, n_slots, CB, deep), jnp.bfloat16)],
        flops=2 * n_slots * n_cols * w_sides.size,
        moved=2 * w_sides.size,
    )


def before_sides(above, below, act, w_sides, w_act, sums, kept, edges):
    n_frames, blocks, n_slots, _, ch = above.shape
    n_rows, n_cols, deep = sums.shape[0], blocks * CB, n_frames * ch

    def body(edge_ref, above_ref, below_ref, act_ref, tiles_ref, w_ref, wa_ref, z_ref, kept_ref, o_ref, next_ref, lhs, lhs2, sem):
        copy = pltpu.make_async_copy(tiles_ref, next_ref.at[:, 1], sem)
        copy.start()
        add_own(act_ref, wa_ref, lhs2, o_ref, z_ref)
        for y, side in enumerate((above_ref, below_ref)):
            o_ref[y] += side_sums(edge_ref, y, side, w_ref[y], lhs)
        copy.wait()

    return call(
        body,
        [jax.ShapeDtypeStruct(sums.shape, jnp.float32), jax.ShapeDtypeStruct(kept.shape, kept.dtype)],
        (above, below, act, act.reshape(n_slots, n_rows, blocks, CB, ch), w_sides, w_act, sums, kept),
        scalars=(edges,),
        scratch=[
            pltpu.VMEM((blocks, n_slots, CB, deep), jnp.bfloat16),
            pltpu.VMEM((n_slots * n_cols, n_rows * ch), jnp.bfloat16),
            pltpu.SemaphoreType.DMA,
        ],
        flops=2 * n_slots * n_cols * (w_sides.size + w_act.size),
        moved=2 * (w_sides.size + w_act.size),
        far=(7,),
        far_out=(1,),
        aliases={8: 1},
    )


def last_part(above, below, w_sides, sums, bias, frame, edges):
    n_slots, n_rows, n_cols, ch = frame.shape

    def body(edge_ref, above_ref, below_ref, w_ref, z_ref, b_ref, f_ref, o_ref, lhs):
        for y, side in enumerate((above_ref, below_ref)):
            for s in range(n_slots):
                lhs[s * n_cols : (s + 1) * n_cols] = masked(edge_ref, y, s, side[s])
            total = folded(dot(lhs[...], w_ref[y]), ch, False)
            for s in range(n_slots):
                value = (total[s] + z_ref[y, :, s] + b_ref[...]).reshape(n_cols, ch)
                o_ref[s, y] = (value + f_ref[s, y].astype(jnp.float32)).astype(jnp.bfloat16)

    return call(
        body,
        [jax.ShapeDtypeStruct(frame.shape, jnp.bfloat16)],
        (above, below, w_sides, sums, bias, frame),
        scalars=(edges,),
        scratch=[pltpu.VMEM((n_slots * n_cols, ch), jnp.bfloat16)],
        flops=2 * n_slots * n_cols * w_sides.size,
        moved=2 * w_sides.size,
    )[0]


def local(
    frame_in,
    cache_first,
    cache_second,
    gain_first,
    gain_second,
    conv_first,
    conv_second,
    bias_first,
    bias_second,
    old_slot,
    new_slot,
    old_shift,
    new_shift,
    frame_count,
):
    n_slots, n_rows, n_cols, ch = frame_in.shape
    n_groups = lax.axis_size("stream")
    n_tiles = lax.axis_size("tile")
    my_group = lax.axis_index("stream")
    my_tile = lax.axis_index("tile")
    n_flight = old_slot.shape[0]
    blocks = n_cols // CB
    slot_ids = jnp.arange(n_flight, dtype=jnp.int32)
    held_new = new_slot[None, :] == slot_ids[:, None]
    source = lookup(held_new, old_slot)
    shift_after = lookup(held_new, new_shift)
    rotation = (shift_after - lookup(held_new, old_shift)) % n_tiles
    frames_done = lookup(held_new, frame_count)
    my_piece = my_group * n_tiles + my_tile
    my_frame = (my_piece // blocks) % 2
    keep = (frames_done >= 2 - my_frame).astype(jnp.int32)
    start = my_group * n_slots
    my_number = lax.dynamic_slice_in_dim((my_tile - shift_after) % n_tiles, start, n_slots)

    edges = jnp.stack([my_number != 0, my_number != n_tiles - 1]).astype(jnp.int32)
    down = [(i, (i + 1) % n_tiles) for i in range(n_tiles)]
    up = [((i + 1) % n_tiles, i) for i in range(n_tiles)]

    def from_above(row):
        return lax.ppermute(row, "tile", down)

    def from_below(row):
        return lax.ppermute(row, "tile", up)

    sent = pack(cache_first, cache_second).reshape(n_groups * n_tiles, n_slots, CB, ch)
    held = lax.all_to_all(sent, BOTH, 0, 0, tiled=True)

    act_own_1, act_sides_1 = spread(conv_first, False)
    act_first, top, bottom = first_activation(frame_in, gain_first[None])
    act_above, act_below = from_above(bottom), from_below(top)
    held, act_first, act_above, act_below, act_own_1, act_sides_1 = lax.optimization_barrier(
        (held, act_first, act_above, act_below, act_own_1, act_sides_1)
    )

    moved = permute(held.reshape(n_groups, n_tiles, n_slots, CB, ch), source, rotation, keep)
    moved, act_later = lax.optimization_barrier((moved, act_first))
    got = lax.all_to_all(
        moved.reshape(n_groups * n_tiles, n_slots, CB, ch), BOTH, 0, 0, tiled=True
    )
    sums_1 = current_part(act_later, act_above, act_below, act_own_1, act_sides_1, edges)
    sums_1, conv_first, conv_second = lax.optimization_barrier((sums_1, conv_first, conv_second))
    act_own_2, act_sides_2 = spread(conv_second, False)
    own_1, sides_1 = spread(conv_first, True)
    own_2, sides_2 = spread(conv_second, True)
    got, sums_1, own_1, own_2, sides_1, sides_2, act_own_2, act_sides_2 = lax.optimization_barrier(
        (got, sums_1, own_1, own_2, sides_1, sides_2, act_own_2, act_sides_2)
    )
    got = got.reshape(n_rows, 2, 2, blocks, n_slots, CB, ch)

    above_1 = from_above(got[n_rows - 1, 0])
    below_1 = from_below(got[0, 0])
    above_2 = from_above(got[n_rows - 1, 1])
    below_2 = from_below(got[0, 1])
    act_tiles = act_first.reshape(n_slots, n_rows, blocks, CB, ch)
    sums_1, sums_2, next_first, kept, sides_1 = own_part(
        got, (own_1, own_2), sums_1, act_tiles, sides_1
    )
    act_second, top, bottom = second_activation(
        above_1, below_1, sides_1, sums_1, bias_first[None], gain_second[None], edges
    )
    side_above, side_below = from_above(bottom), from_below(top)
    sums_2, next_second = before_sides(
        above_2, below_2, act_second, sides_2, act_own_2, sums_2, kept, edges
    )
    mixed_frame = last_part(
        side_above, side_below, act_sides_2, sums_2, bias_second[None], frame_in, edges
    )
    whole = (n_slots, 2, n_rows, n_cols, ch)
    return (mixed_frame, next_first.reshape(whole), next_second.reshape(whole))


def solution(mesh):
    frame = P("stream", "tile", None, None)
    cache = P("stream", None, "tile", None, None)
    return jax.shard_map(
        local,
        mesh=mesh,
        in_specs=(frame, cache, cache) + (P(),) * 11,
        out_specs=(frame, cache, cache),
        check_vma=False,
    )
```

```python
import jax
import jax.numpy as jnp
from jax import lax
from jax.experimental import pallas as pl
from jax.experimental.pallas import tpu as pltpu
from jax.sharding import PartitionSpec as P

BOTH = ("stream", "tile")
CB = 8


def lookup(held_table, values):
    return jnp.sum(jnp.where(held_table, values[None, :], 0), axis=1)


def pack(first, second):
    n_slots, n_frames, n_rows, n_cols, ch = first.shape
    blocks = n_cols // CB
    parts = n_rows * 2 * n_frames

    def body(a_ref, b_ref, o_ref, held, in_sems, out_sems):
        whole = []
        for r in range(n_rows):
            for k, ref in enumerate((a_ref, b_ref)):
                for f in range(n_frames):
                    whole.append((r, k, f, ref))
        loads = []
        for p, (r, k, f, ref) in enumerate(whole):
            for s in range(n_slots):
                n = p * n_slots + s
                loads.append(
                    pltpu.make_async_copy(ref.at[s, f, r], held.at[r, k, f, :, s], in_sems.at[n])
                )
                loads[-1].start()
        stores = []
        for p, (r, k, f, _) in enumerate(whole):
            for s in range(n_slots):
                loads[p * n_slots + s].wait()
            stores.append(pltpu.make_async_copy(held.at[r, k, f], o_ref.at[r, k, f], out_sems.at[p]))
            stores[-1].start()
        for c in stores:
            c.wait()

    shape = (n_rows, 2, n_frames, blocks, n_slots, CB, ch)
    tiles = (n_slots, n_frames, n_rows, blocks, CB, ch)
    far = pl.BlockSpec(memory_space=pl.ANY)
    return pl.pallas_call(
        body,
        in_specs=[far, far],
        out_specs=far,
        out_shape=jax.ShapeDtypeStruct(shape, first.dtype),
        scratch_shapes=[
            pltpu.VMEM(shape, first.dtype),
            pltpu.SemaphoreType.DMA((parts * n_slots,)),
            pltpu.SemaphoreType.DMA((parts,)),
        ],
        compiler_params=pltpu.CompilerParams(vmem_limit_bytes=58 << 20),
    )(first.reshape(tiles), second.reshape(tiles))


def permute(held, source, rotation, keep):
    n_groups, n_tiles, n_slots, cols, ch = held.shape

    def body(source_ref, rotation_ref, keep_ref, i_ref, o_ref, made, sems):
        def stream(n, to):
            by = rotation_ref[n]
            old = source_ref[n]
            slot = lax.rem(n, n_slots)
            of, place = lax.div(old, n_slots), lax.rem(old, n_slots)

            @pl.when(keep_ref[n] != 0)
            def _():
                for t in range(n_tiles):
                    at = lax.rem(t + n_tiles - by, n_tiles)
                    made[to, t, slot] = i_ref[of, at, place]

            @pl.when(keep_ref[n] == 0)
            def _():
                made[to, :, slot] = jnp.zeros((n_tiles, cols, ch), made.dtype)

            return to

        copies = []
        for to in range(n_groups):
            lax.fori_loop(to * n_slots, (to + 1) * n_slots, stream, to)
            copies.append(pltpu.make_async_copy(made.at[to], o_ref.at[to], sems.at[to]))
            copies[-1].start()
        for c in copies:
            c.wait()

    smem = pl.BlockSpec(memory_space=pltpu.SMEM)
    return pl.pallas_call(
        body,
        in_specs=[smem, smem, smem, pl.BlockSpec(memory_space=pltpu.VMEM)],
        out_specs=pl.BlockSpec(memory_space=pl.ANY),
        out_shape=jax.ShapeDtypeStruct(held.shape, held.dtype),
        scratch_shapes=[
            pltpu.VMEM(held.shape, held.dtype),
            pltpu.SemaphoreType.DMA((n_groups,)),
        ],
        compiler_params=pltpu.CompilerParams(vmem_limit_bytes=52 << 20),
    )(source, rotation, keep, held)


VMEM_LIMIT = 16 << 20


def call(body, out_shape, operands, scalars=(), scratch=(), flops=0, moved=0, far=(), far_out=(), aliases=None, limit=VMEM_LIMIT):
    in_specs = [pl.BlockSpec(memory_space=pltpu.SMEM) for _ in scalars]
    for k, _ in enumerate(operands):
        in_specs.append(pl.BlockSpec(memory_space=pl.ANY if k in far else pltpu.VMEM))
    out_specs = []
    for k, _ in enumerate(out_shape):
        out_specs.append(pl.BlockSpec(memory_space=pl.ANY if k in far_out else pltpu.VMEM))
    return pl.pallas_call(
        body,
        in_specs=in_specs,
        out_specs=out_specs,
        out_shape=list(out_shape),
        scratch_shapes=list(scratch),
        input_output_aliases=aliases or {},
        cost_estimate=pl.CostEstimate(flops=flops, bytes_accessed=moved, transcendentals=0),
        compiler_params=pltpu.CompilerParams(vmem_limit_bytes=limit),
    )(*scalars, *operands)


def spread(weight, past):
    n_t, n_y, n_x, ci, co = weight.shape
    wide = n_x * co
    times = n_t - 1 if past else 1

    def body(w_ref, own_ref, side_ref):
        dy = pl.program_id(0)

        def side(y):
            for x in range(n_x):
                for t in range(times):
                    side_ref[y, t * ci : (t + 1) * ci, x * co : (x + 1) * co] = w_ref[t, 0, x]

        def own(row, y):
            for x in range(n_x):
                for t in range(times):
                    lo = (row * times + t) * ci
                    at = y * wide + x * co
                    own_ref[lo : lo + ci, at : at + co] = w_ref[t, 0, x]

        @pl.when(dy == 0)
        def _():
            side(0)
            own(0, 1)

        @pl.when(dy == 1)
        def _():
            own(0, 0)
            own(1, 1)

        @pl.when(dy == 2)
        def _():
            side(1)
            own(1, 0)

    shapes = [(2 * times * ci, 2 * wide), (2, times * ci, wide)]
    first = 0 if past else n_t - 1
    return pl.pallas_call(
        body,
        grid=(n_y,),
        in_specs=[pl.BlockSpec((times, 1, n_x, ci, co), lambda y: (first, y, 0, 0, 0))],
        out_specs=[pl.BlockSpec(memory_space=pltpu.VMEM) for _ in shapes],
        out_shape=[jax.ShapeDtypeStruct(shape, weight.dtype) for shape in shapes],
        cost_estimate=pl.CostEstimate(flops=0, bytes_accessed=4 * weight.size, transcendentals=0),
        compiler_params=pltpu.CompilerParams(vmem_limit_bytes=16 << 20),
    )(weight)


def activated(values, gain):
    u = values * lax.rsqrt(jnp.mean(values * values, axis=-1, keepdims=True) + 1e-06) * gain
    return u / (1.0 + jnp.exp(-u))


def first_activation(frame, gain, edges):
    n_slots, n_rows, n_cols, ch = frame.shape

    def body(edge_ref, f_ref, g_ref, o_ref, near_ref, far_ref):
        odd = edge_ref[2, 0]
        for s in range(n_slots):
            for r in range(n_rows):
                value = activated(f_ref[s, r].astype(jnp.float32), g_ref[...]).astype(jnp.bfloat16)
                o_ref[s, r] = value

                @pl.when(odd != r)
                def _(s=s, value=value):
                    near_ref[s] = value

                @pl.when(odd == r)
                def _(s=s, value=value):
                    far_ref[s] = value

    row = jax.ShapeDtypeStruct((n_slots, n_cols, ch), jnp.bfloat16)
    return call(
        body,
        [jax.ShapeDtypeStruct(frame.shape, jnp.bfloat16), row, row],
        (frame, gain),
        scalars=(edges,),
        flops=10 * frame.size,
        moved=6 * frame.size,
    )


def beside(edge_ref, near_ref, far_ref):
    odd = edge_ref[2, 0]
    return ((near_ref, 1 - odd), (far_ref, odd))


def folded(acc, ch, cols_first):
    tiles = acc.shape[0] // CB
    n_slots = 4
    blocks = tiles // n_slots
    lead = (blocks, n_slots) if cols_first else (n_slots, blocks)
    axis = 0 if cols_first else 1

    def plane(k):
        value = acc[:, k * ch : (k + 1) * ch].reshape(tiles, CB, ch)
        return value

    at = lax.broadcasted_iota(jnp.int32, (1, 1, CB, ch), 2)
    before = pltpu.roll(plane(0), 1, 1).reshape(lead + (CB, ch))
    after = pltpu.roll(plane(2), CB - 1, 1).reshape(lead + (CB, ch))
    gap = list(lead) + [CB, ch]
    gap[axis] = 1
    gap = jnp.zeros(gap, jnp.float32)
    before_prev = jnp.concatenate([gap, lax.slice_in_dim(before, 0, blocks - 1, axis=axis)], axis)
    after_next = jnp.concatenate([lax.slice_in_dim(after, 1, blocks, axis=axis), gap], axis)
    total = plane(1).reshape(lead + (CB, ch))
    total += jnp.where(at == 0, before_prev, before)
    total += jnp.where(at == CB - 1, after_next, after)
    return total


def add_into(o_ref, y, total, cols_first, base=None):
    if cols_first:
        o_ref[y] = total if base is None else base[y] + total
        return
    for s in range(total.shape[0]):
        o_ref[y, :, s] = total[s] if base is None else base[y, :, s] + total[s]


def masked(edge_ref, k, s, value):
    return jnp.where(edge_ref[k, s] != 0, value, jnp.zeros_like(value))


def dot(a, b):
    return jnp.dot(a, b, preferred_element_type=jnp.float32)


def sums_shape(blocks, n_slots, n_rows, ch):
    return jax.ShapeDtypeStruct((n_rows, blocks, n_slots, CB, ch), jnp.float32)


def add_sides(edge_ref, sides, w_ref, lhs, o_ref):
    n_slots, n_cols, ch = sides[0].shape
    for side, y in beside(edge_ref, *sides):
        for s in range(n_slots):
            lhs[s * n_cols : (s + 1) * n_cols] = masked(edge_ref, y, s, side[s])
        add_into(o_ref, y, folded(dot(lhs[...], w_ref[y]), ch, False), False, o_ref)


def add_own(act_ref, w_ref, lhs, o_ref, base):
    n_slots, n_rows, n_cols, ch = act_ref.shape
    for s in range(n_slots):
        for r in range(n_rows):
            lhs[s * n_cols : (s + 1) * n_cols, r * ch : (r + 1) * ch] = act_ref[s, r]
    both = dot(lhs[...], w_ref[...])
    wide = both.shape[1] // 2
    for y in range(n_rows):
        add_into(o_ref, y, folded(both[:, y * wide : (y + 1) * wide], ch, False), False, base)


def current_part(act, near, far, w_own, w_sides, edges):
    n_slots, n_rows, n_cols, ch = act.shape
    half = n_slots * n_cols

    def body(edge_ref, act_ref, near_ref, far_ref, wo_ref, ws_ref, o_ref, lhs, side):
        add_own(act_ref, wo_ref, lhs, o_ref, None)
        add_sides(edge_ref, (near_ref, far_ref), ws_ref, side, o_ref)

    return call(
        body,
        [sums_shape(n_cols // CB, n_slots, n_rows, ch)],
        (act, near, far, w_own, w_sides),
        scalars=(edges,),
        scratch=[
            pltpu.VMEM((half, n_rows * ch), jnp.bfloat16),
            pltpu.VMEM((half, ch), jnp.bfloat16),
        ],
        flops=2 * half * (w_own.size + w_sides.size),
        moved=2 * w_own.size + 8 * act.size,
    )[0]


def own_part(got, weights, sums, act, sides):
    n_rows, n_caches, n_frames, blocks, n_slots, _, ch = got.shape
    half = blocks * n_slots * CB
    deep = n_frames * ch
    whole = weights[0]

    def body(got_ref, w0_ref, w1_ref, z_ref, act_ref, sides_ref, o0_ref, o1_ref, n1_ref, n2_ref, near_ref, w0, w1, lhs, acc, sems, keep_sems):
        loads = []
        for r in range(n_rows):
            rows = pl.ds(r * deep, deep)
            loads.append(pltpu.make_async_copy(w0_ref.at[rows], w0.at[r], sems.at[r]))
        loads.append(pltpu.make_async_copy(w1_ref, w1, sems.at[2]))
        near = pltpu.make_async_copy(sides_ref, near_ref, sems.at[3])
        keeps = [pltpu.make_async_copy(act_ref, n1_ref.at[:, 1], sems.at[4])]
        for k, dst in enumerate((n1_ref, n2_ref)):
            for r in range(n_rows):
                for s in range(n_slots):
                    n = (k * n_rows + r) * n_slots + s
                    keeps.append(
                        pltpu.make_async_copy(
                            got_ref.at[r, k, n_frames - 1, :, s], dst.at[s, 0, r], keep_sems.at[n]
                        )
                    )
        loads[0].start()

        def fill(k, r, f):
            lo = r * deep + f * ch
            lhs[:, lo : lo + ch] = got_ref[r, k, f].reshape(half, ch)

        def give(o_ref, base):
            wide = whole.shape[1] // 2
            for y in range(n_rows):
                total = folded(acc[:, y * wide : (y + 1) * wide], ch, True)
                add_into(o_ref, y, total, True, base)

        for r in range(n_rows):
            for f in range(n_frames):
                fill(0, r, f)
        loads[0].wait()
        loads[1].start()
        acc[...] = dot(lhs[:, 0:deep], w0[0])
        loads[1].wait()
        loads[2].start()
        acc[...] += dot(lhs[:, deep : 2 * deep], w0[1])
        give(o0_ref, z_ref)
        for r in range(n_rows):
            for f in range(n_frames):
                fill(1, r, f)
        loads[2].wait()
        near.start()
        for c in keeps:
            c.start()
        acc[...] = dot(lhs[...], w1[...])
        give(o1_ref, None)
        for c in keeps:
            c.wait()
        near.wait()

    out = sums_shape(blocks, n_slots, n_rows, ch)
    nxt = jax.ShapeDtypeStruct((n_slots, 2, n_rows, blocks, CB, ch), jnp.bfloat16)
    return call(
        body,
        [out, out, nxt, nxt, jax.ShapeDtypeStruct(sides.shape, sides.dtype)],
        (got, *weights, sums, act, sides),
        scratch=[
            pltpu.VMEM((n_rows, deep, whole.shape[1]), whole.dtype),
            pltpu.VMEM(whole.shape, whole.dtype),
            pltpu.VMEM((half, n_rows * deep), jnp.bfloat16),
            pltpu.VMEM((half, whole.shape[1]), jnp.float32),
            pltpu.SemaphoreType.DMA((5,)),
            pltpu.SemaphoreType.DMA((2 * n_rows * n_slots,)),
        ],
        flops=4 * half * whole.size,
        moved=4 * whole.size,
        far=(1, 2, 5),
        far_out=(2, 3),
        limit=40 << 20,
    )


def side_sums(edge_ref, k, side_ref, w, lhs):
    n_frames, blocks, n_slots, _, ch = side_ref.shape
    for s in range(n_slots):
        for f in range(n_frames):
            value = masked(edge_ref, k, s, side_ref[f, :, s])
            lhs[:, s, :, f * ch : (f + 1) * ch] = value
    half = blocks * n_slots * CB
    return folded(dot(lhs[...].reshape(half, n_frames * ch), w), ch, True)


def second_activation(near, far, w_sides, sums, bias, gain, edges):
    n_frames, blocks, n_slots, _, ch = near.shape
    n_rows, n_cols, deep = sums.shape[0], blocks * CB, n_frames * ch

    def body(edge_ref, near_ref, far_ref, w_ref, z_ref, b_ref, g_ref, o_ref, near_out, far_out, lhs):
        for (side, y), out in zip(beside(edge_ref, near_ref, far_ref), (near_out, far_out)):
            total = side_sums(edge_ref, y, side, w_ref[y], lhs) + z_ref[y] + b_ref[...]
            for s in range(n_slots):
                value = activated(total[:, s].reshape(n_cols, ch), g_ref[...]).astype(jnp.bfloat16)
                o_ref[s, y] = value
                out[s] = value

    row = jax.ShapeDtypeStruct((n_slots, n_cols, ch), jnp.bfloat16)
    return call(
        body,
        [jax.ShapeDtypeStruct((n_slots, n_rows, n_cols, ch), jnp.bfloat16), row, row],
        (near, far, w_sides, sums, bias, gain),
        scalars=(edges,),
        scratch=[pltpu.VMEM((blocks, n_slots, CB, deep), jnp.bfloat16)],
        flops=2 * n_slots * n_cols * w_sides.size,
        moved=2 * w_sides.size,
    )


def before_sides(near, far, act, w_sides, w_act, sums, kept, edges):
    n_frames, blocks, n_slots, _, ch = near.shape
    n_rows, n_cols, deep = sums.shape[0], blocks * CB, n_frames * ch

    def body(edge_ref, near_ref, far_ref, act_ref, tiles_ref, w_ref, wa_ref, z_ref, kept_ref, o_ref, next_ref, lhs, lhs2, sem):
        copy = pltpu.make_async_copy(tiles_ref, next_ref.at[:, 1], sem)
        copy.start()
        add_own(act_ref, wa_ref, lhs2, o_ref, z_ref)
        for side, y in beside(edge_ref, near_ref, far_ref):
            o_ref[y] += side_sums(edge_ref, y, side, w_ref[y], lhs)
        copy.wait()

    return call(
        body,
        [jax.ShapeDtypeStruct(sums.shape, jnp.float32), jax.ShapeDtypeStruct(kept.shape, kept.dtype)],
        (near, far, act, act.reshape(n_slots, n_rows, blocks, CB, ch), w_sides, w_act, sums, kept),
        scalars=(edges,),
        scratch=[
            pltpu.VMEM((blocks, n_slots, CB, deep), jnp.bfloat16),
            pltpu.VMEM((n_slots * n_cols, n_rows * ch), jnp.bfloat16),
            pltpu.SemaphoreType.DMA,
        ],
        flops=2 * n_slots * n_cols * (w_sides.size + w_act.size),
        moved=2 * (w_sides.size + w_act.size),
        far=(7,),
        far_out=(1,),
        aliases={8: 1},
    )


def last_part(near, far, w_sides, sums, bias, frame, edges):
    n_slots, n_rows, n_cols, ch = frame.shape

    def body(edge_ref, near_ref, far_ref, w_ref, z_ref, b_ref, f_ref, o_ref, lhs):
        for side, y in beside(edge_ref, near_ref, far_ref):
            for s in range(n_slots):
                lhs[s * n_cols : (s + 1) * n_cols] = masked(edge_ref, y, s, side[s])
            total = folded(dot(lhs[...], w_ref[y]), ch, False)
            for s in range(n_slots):
                value = (total[s] + z_ref[y, :, s] + b_ref[...]).reshape(n_cols, ch)
                o_ref[s, y] = (value + f_ref[s, y].astype(jnp.float32)).astype(jnp.bfloat16)

    return call(
        body,
        [jax.ShapeDtypeStruct(frame.shape, jnp.bfloat16)],
        (near, far, w_sides, sums, bias, frame),
        scalars=(edges,),
        scratch=[pltpu.VMEM((n_slots * n_cols, ch), jnp.bfloat16)],
        flops=2 * n_slots * n_cols * w_sides.size,
        moved=2 * w_sides.size,
    )[0]


def local(
    frame_in,
    cache_first,
    cache_second,
    gain_first,
    gain_second,
    conv_first,
    conv_second,
    bias_first,
    bias_second,
    old_slot,
    new_slot,
    old_shift,
    new_shift,
    frame_count,
):
    n_slots, n_rows, n_cols, ch = frame_in.shape
    n_groups = lax.axis_size("stream")
    n_tiles = lax.axis_size("tile")
    my_group = lax.axis_index("stream")
    my_tile = lax.axis_index("tile")
    n_flight = old_slot.shape[0]
    blocks = n_cols // CB
    slot_ids = jnp.arange(n_flight, dtype=jnp.int32)
    held_new = new_slot[None, :] == slot_ids[:, None]
    source = lookup(held_new, old_slot)
    shift_after = lookup(held_new, new_shift)
    rotation = (shift_after - lookup(held_new, old_shift)) % n_tiles
    frames_done = lookup(held_new, frame_count)
    my_piece = my_group * n_tiles + my_tile
    my_frame = (my_piece // blocks) % 2
    keep = (frames_done >= 2 - my_frame).astype(jnp.int32)
    start = my_group * n_slots
    my_number = lax.dynamic_slice_in_dim((my_tile - shift_after) % n_tiles, start, n_slots)

    odd = my_tile % 2
    edges = jnp.stack(
        [my_number != 0, my_number != n_tiles - 1, jnp.broadcast_to(odd == 1, my_number.shape)]
    ).astype(jnp.int32)

    def swap_near(row):
        return lax.ppermute(row, "tile", [(i, i ^ 1) for i in range(n_tiles)])

    def swap_far(row):
        return lax.ppermute(
            row, "tile", [(i, (i + 2 * (i % 2) - 1) % n_tiles) for i in range(n_tiles)]
        )

    sent = pack(cache_first, cache_second).reshape(n_groups * n_tiles, n_slots, CB, ch)
    held = lax.all_to_all(sent, BOTH, 0, 0, tiled=True)

    act_own_1, act_sides_1 = spread(conv_first, False)
    act_first, near, far = first_activation(frame_in, gain_first[None], edges)
    act_near, act_far = swap_near(near), swap_far(far)
    held, act_first, act_near, act_far, act_own_1, act_sides_1 = lax.optimization_barrier(
        (held, act_first, act_near, act_far, act_own_1, act_sides_1)
    )

    moved = permute(held.reshape(n_groups, n_tiles, n_slots, CB, ch), source, rotation, keep)
    moved, act_later = lax.optimization_barrier((moved, act_first))
    got = lax.all_to_all(
        moved.reshape(n_groups * n_tiles, n_slots, CB, ch), BOTH, 0, 0, tiled=True
    )
    sums_1 = current_part(act_later, act_near, act_far, act_own_1, act_sides_1, edges)
    sums_1, conv_first, conv_second = lax.optimization_barrier((sums_1, conv_first, conv_second))
    act_own_2, act_sides_2 = spread(conv_second, False)
    own_1, sides_1 = spread(conv_first, True)
    own_2, sides_2 = spread(conv_second, True)
    got, sums_1, own_1, own_2, sides_1, sides_2, act_own_2, act_sides_2 = lax.optimization_barrier(
        (got, sums_1, own_1, own_2, sides_1, sides_2, act_own_2, act_sides_2)
    )
    got = got.reshape(n_rows, 2, 2, blocks, n_slots, CB, ch)

    def picked(cache, row):
        return lax.dynamic_index_in_dim(got[:, cache], row, 0, keepdims=False)

    near_1, far_1 = swap_near(picked(0, 1 - odd)), swap_far(picked(0, odd))
    near_2, far_2 = swap_near(picked(1, 1 - odd)), swap_far(picked(1, odd))
    act_tiles = act_first.reshape(n_slots, n_rows, blocks, CB, ch)
    sums_1, sums_2, next_first, kept, sides_1 = own_part(
        got, (own_1, own_2), sums_1, act_tiles, sides_1
    )
    act_second, near, far = second_activation(
        near_1, far_1, sides_1, sums_1, bias_first[None], gain_second[None], edges
    )
    act_near, act_far = swap_near(near), swap_far(far)
    sums_2, next_second = before_sides(
        near_2, far_2, act_second, sides_2, act_own_2, sums_2, kept, edges
    )
    mixed_frame = last_part(
        act_near, act_far, act_sides_2, sums_2, bias_second[None], frame_in, edges
    )
    whole = (n_slots, 2, n_rows, n_cols, ch)
    return (mixed_frame, next_first.reshape(whole), next_second.reshape(whole))


def solution(mesh):
    frame = P("stream", "tile", None, None)
    cache = P("stream", None, "tile", None, None)
    return jax.shard_map(
        local,
        mesh=mesh,
        in_specs=(frame, cache, cache) + (P(),) * 11,
        out_specs=(frame, cache, cache),
        check_vma=False,
    )
```

```python
import jax
import jax.numpy as jnp
from jax import lax
from jax.experimental import pallas as pl
from jax.experimental.pallas import tpu as pltpu
from jax.sharding import PartitionSpec as P

BOTH = ("stream", "tile")
CB = 8


def lookup(held_table, values):
    return jnp.sum(jnp.where(held_table, values[None, :], 0), axis=1)


def pack(first, second):
    n_slots, n_frames, n_rows, n_cols, ch = first.shape
    blocks = n_cols // CB
    parts = n_rows * 2 * n_frames

    def body(a_ref, b_ref, o_ref, held, in_sems, out_sems):
        whole = []
        for r in range(n_rows):
            for k, ref in enumerate((a_ref, b_ref)):
                for f in range(n_frames):
                    whole.append((r, k, f, ref))
        loads = []
        for p, (r, k, f, ref) in enumerate(whole):
            for s in range(n_slots):
                n = p * n_slots + s
                loads.append(
                    pltpu.make_async_copy(ref.at[s, f, r], held.at[r, k, f, :, s], in_sems.at[n])
                )
                loads[-1].start()
        stores = []
        for p, (r, k, f, _) in enumerate(whole):
            for s in range(n_slots):
                loads[p * n_slots + s].wait()
            stores.append(pltpu.make_async_copy(held.at[r, k, f], o_ref.at[r, k, f], out_sems.at[p]))
            stores[-1].start()
        for c in stores:
            c.wait()

    shape = (n_rows, 2, n_frames, blocks, n_slots, CB, ch)
    tiles = (n_slots, n_frames, n_rows, blocks, CB, ch)
    far = pl.BlockSpec(memory_space=pl.ANY)
    return pl.pallas_call(
        body,
        in_specs=[far, far],
        out_specs=far,
        out_shape=jax.ShapeDtypeStruct(shape, first.dtype),
        scratch_shapes=[
            pltpu.VMEM(shape, first.dtype),
            pltpu.SemaphoreType.DMA((parts * n_slots,)),
            pltpu.SemaphoreType.DMA((parts,)),
        ],
        compiler_params=pltpu.CompilerParams(vmem_limit_bytes=58 << 20),
    )(first.reshape(tiles), second.reshape(tiles))


def permute(held, source, rotation, keep):
    n_groups, n_tiles, n_slots, cols, ch = held.shape

    def body(source_ref, rotation_ref, keep_ref, i_ref, o_ref, made, sems):
        def stream(n, to):
            by = rotation_ref[n]
            old = source_ref[n]
            slot = lax.rem(n, n_slots)
            of, place = lax.div(old, n_slots), lax.rem(old, n_slots)

            @pl.when(keep_ref[n] != 0)
            def _():
                for t in range(n_tiles):
                    at = lax.rem(t + n_tiles - by, n_tiles)
                    made[to, t, slot] = i_ref[of, at, place]

            @pl.when(keep_ref[n] == 0)
            def _():
                made[to, :, slot] = jnp.zeros((n_tiles, cols, ch), made.dtype)

            return to

        copies = []
        for to in range(n_groups):
            lax.fori_loop(to * n_slots, (to + 1) * n_slots, stream, to)
            copies.append(pltpu.make_async_copy(made.at[to], o_ref.at[to], sems.at[to]))
            copies[-1].start()
        for c in copies:
            c.wait()

    smem = pl.BlockSpec(memory_space=pltpu.SMEM)
    return pl.pallas_call(
        body,
        in_specs=[smem, smem, smem, pl.BlockSpec(memory_space=pltpu.VMEM)],
        out_specs=pl.BlockSpec(memory_space=pl.ANY),
        out_shape=jax.ShapeDtypeStruct(held.shape, held.dtype),
        scratch_shapes=[
            pltpu.VMEM(held.shape, held.dtype),
            pltpu.SemaphoreType.DMA((n_groups,)),
        ],
        compiler_params=pltpu.CompilerParams(vmem_limit_bytes=52 << 20),
    )(source, rotation, keep, held)


VMEM_LIMIT = 16 << 20
LIMIT_A = 34
LIMIT_B = 16


def call(body, out_shape, operands, scalars=(), scratch=(), flops=0, moved=0, far=(), far_out=(), aliases=None, limit=VMEM_LIMIT):
    in_specs = [pl.BlockSpec(memory_space=pltpu.SMEM) for _ in scalars]
    for k, _ in enumerate(operands):
        in_specs.append(pl.BlockSpec(memory_space=pl.ANY if k in far else pltpu.VMEM))
    out_specs = []
    for k, _ in enumerate(out_shape):
        out_specs.append(pl.BlockSpec(memory_space=pl.ANY if k in far_out else pltpu.VMEM))
    return pl.pallas_call(
        body,
        in_specs=in_specs,
        out_specs=out_specs,
        out_shape=list(out_shape),
        scratch_shapes=list(scratch),
        input_output_aliases=aliases or {},
        cost_estimate=pl.CostEstimate(flops=flops, bytes_accessed=moved, transcendentals=0),
        compiler_params=pltpu.CompilerParams(vmem_limit_bytes=limit),
    )(*scalars, *operands)


def spread(weight, past):
    n_t, n_y, n_x, ci, co = weight.shape
    wide = n_x * co
    times = n_t - 1 if past else 1

    def body(w_ref, own_ref, side_ref):
        dy = pl.program_id(0)

        def side(y):
            for x in range(n_x):
                for t in range(times):
                    side_ref[y, t * ci : (t + 1) * ci, x * co : (x + 1) * co] = w_ref[t, 0, x]

        def own(row, y):
            for x in range(n_x):
                for t in range(times):
                    lo = (row * times + t) * ci
                    at = y * wide + x * co
                    own_ref[lo : lo + ci, at : at + co] = w_ref[t, 0, x]

        @pl.when(dy == 0)
        def _():
            side(0)
            own(0, 1)

        @pl.when(dy == 1)
        def _():
            own(0, 0)
            own(1, 1)

        @pl.when(dy == 2)
        def _():
            side(1)
            own(1, 0)

    shapes = [(2 * times * ci, 2 * wide), (2, times * ci, wide)]
    first = 0 if past else n_t - 1
    return pl.pallas_call(
        body,
        grid=(n_y,),
        in_specs=[pl.BlockSpec((times, 1, n_x, ci, co), lambda y: (first, y, 0, 0, 0))],
        out_specs=[pl.BlockSpec(memory_space=pltpu.VMEM) for _ in shapes],
        out_shape=[jax.ShapeDtypeStruct(shape, weight.dtype) for shape in shapes],
        cost_estimate=pl.CostEstimate(flops=0, bytes_accessed=4 * weight.size, transcendentals=0),
        compiler_params=pltpu.CompilerParams(vmem_limit_bytes=16 << 20),
    )(weight)


def activated(values, gain):
    u = values * lax.rsqrt(jnp.mean(values * values, axis=-1, keepdims=True) + 1e-06) * gain
    return u / (1.0 + jnp.exp(-u))


def first_activation(frame, gain, edges):
    n_slots, n_rows, n_cols, ch = frame.shape

    def body(edge_ref, f_ref, g_ref, o_ref, near_ref, far_ref):
        odd = edge_ref[2, 0]
        for s in range(n_slots):
            for r in range(n_rows):
                value = activated(f_ref[s, r].astype(jnp.float32), g_ref[...]).astype(jnp.bfloat16)
                o_ref[s, r] = value

                @pl.when(odd != r)
                def _(s=s, value=value):
                    near_ref[s] = value

                @pl.when(odd == r)
                def _(s=s, value=value):
                    far_ref[s] = value

    row = jax.ShapeDtypeStruct((n_slots, n_cols, ch), jnp.bfloat16)
    return call(
        body,
        [jax.ShapeDtypeStruct(frame.shape, jnp.bfloat16), row, row],
        (frame, gain),
        scalars=(edges,),
        flops=10 * frame.size,
        moved=6 * frame.size,
    )


def beside(edge_ref, near_ref, far_ref):
    odd = edge_ref[2, 0]
    return ((near_ref, 1 - odd), (far_ref, odd))


def folded(acc, ch, cols_first):
    tiles = acc.shape[0] // CB
    n_slots = 4
    blocks = tiles // n_slots
    lead = (blocks, n_slots) if cols_first else (n_slots, blocks)
    axis = 0 if cols_first else 1

    def plane(k):
        value = acc[:, k * ch : (k + 1) * ch].reshape(tiles, CB, ch)
        return value

    at = lax.broadcasted_iota(jnp.int32, (1, 1, CB, ch), 2)
    before = pltpu.roll(plane(0), 1, 1).reshape(lead + (CB, ch))
    after = pltpu.roll(plane(2), CB - 1, 1).reshape(lead + (CB, ch))
    gap = list(lead) + [CB, ch]
    gap[axis] = 1
    gap = jnp.zeros(gap, jnp.float32)
    before_prev = jnp.concatenate([gap, lax.slice_in_dim(before, 0, blocks - 1, axis=axis)], axis)
    after_next = jnp.concatenate([lax.slice_in_dim(after, 1, blocks, axis=axis), gap], axis)
    total = plane(1).reshape(lead + (CB, ch))
    total += jnp.where(at == 0, before_prev, before)
    total += jnp.where(at == CB - 1, after_next, after)
    return total


def add_into(o_ref, y, total, cols_first, base=None):
    if cols_first:
        o_ref[y] = total if base is None else base[y] + total
        return
    for s in range(total.shape[0]):
        o_ref[y, :, s] = total[s] if base is None else base[y, :, s] + total[s]


def masked(edge_ref, k, s, value):
    return jnp.where(edge_ref[k, s] != 0, value, jnp.zeros_like(value))


def dot(a, b):
    return jnp.dot(a, b, preferred_element_type=jnp.float32)


def sums_shape(blocks, n_slots, n_rows, ch):
    return jax.ShapeDtypeStruct((n_rows, blocks, n_slots, CB, ch), jnp.float32)


def add_sides(edge_ref, sides, w_ref, lhs, o_ref):
    n_slots, n_cols, ch = sides[0].shape
    for side, y in beside(edge_ref, *sides):
        for s in range(n_slots):
            lhs[s * n_cols : (s + 1) * n_cols] = masked(edge_ref, y, s, side[s])
        add_into(o_ref, y, folded(dot(lhs[...], w_ref[y]), ch, False), False, o_ref)


def add_own(act_ref, w_ref, lhs, o_ref, base):
    n_slots, n_rows, n_cols, ch = act_ref.shape
    for s in range(n_slots):
        for r in range(n_rows):
            lhs[s * n_cols : (s + 1) * n_cols, r * ch : (r + 1) * ch] = act_ref[s, r]
    both = dot(lhs[...], w_ref[...])
    wide = both.shape[1] // 2
    for y in range(n_rows):
        add_into(o_ref, y, folded(both[:, y * wide : (y + 1) * wide], ch, False), False, base)


def current_part(act, near, far, w_own, w_sides, edges):
    n_slots, n_rows, n_cols, ch = act.shape
    half = n_slots * n_cols

    def body(edge_ref, act_ref, near_ref, far_ref, wo_ref, ws_ref, o_ref, lhs, side):
        add_own(act_ref, wo_ref, lhs, o_ref, None)
        add_sides(edge_ref, (near_ref, far_ref), ws_ref, side, o_ref)

    return call(
        body,
        [sums_shape(n_cols // CB, n_slots, n_rows, ch)],
        (act, near, far, w_own, w_sides),
        scalars=(edges,),
        scratch=[
            pltpu.VMEM((half, n_rows * ch), jnp.bfloat16),
            pltpu.VMEM((half, ch), jnp.bfloat16),
        ],
        flops=2 * half * (w_own.size + w_sides.size),
        moved=2 * w_own.size + 8 * act.size,
    )[0]


def own_rows(got_ref, k, lhs):
    n_rows, _, n_frames, _, _, _, ch = got_ref.shape
    for r in range(n_rows):
        for f in range(n_frames):
            lo = (r * n_frames + f) * ch
            lhs[:, lo : lo + ch] = got_ref[r, k, f].reshape(lhs.shape[0], ch)


def give_rows(acc, ch, o_ref, base):
    n_rows = o_ref.shape[0]
    wide = acc.shape[1] // n_rows
    for y in range(n_rows):
        add_into(o_ref, y, folded(acc[:, y * wide : (y + 1) * wide], ch, True), True, base)


def own_first(got, weight, sums, act, sides):
    n_rows, _, n_frames, blocks, n_slots, _, ch = got.shape
    half = blocks * n_slots * CB
    deep = n_frames * ch

    def body(got_ref, w_ref, z_ref, act_ref, sides_ref, o_ref, next_ref, near_ref, w, lhs, acc, sems, keep_sems):
        loads = []
        for r in range(n_rows):
            rows = pl.ds(r * deep, deep)
            loads.append(pltpu.make_async_copy(w_ref.at[rows], w.at[r], sems.at[r]))
        loads[0].start()
        near = pltpu.make_async_copy(sides_ref, near_ref, sems.at[2])
        keeps = [pltpu.make_async_copy(act_ref, next_ref.at[:, 1], sems.at[3])]
        for r in range(n_rows):
            for s in range(n_slots):
                src = got_ref.at[r, 0, n_frames - 1, :, s]
                n = r * n_slots + s
                keeps.append(pltpu.make_async_copy(src, next_ref.at[s, 0, r], keep_sems.at[n]))
        own_rows(got_ref, 0, lhs)
        loads[0].wait()
        loads[1].start()
        acc[...] = dot(lhs[:, 0:deep], w[0])
        loads[1].wait()
        near.start()
        for c in keeps:
            c.start()
        acc[...] += dot(lhs[:, deep : 2 * deep], w[1])
        give_rows(acc, ch, o_ref, z_ref)
        for c in keeps:
            c.wait()
        near.wait()

    return call(
        body,
        [
            sums_shape(blocks, n_slots, n_rows, ch),
            jax.ShapeDtypeStruct((n_slots, 2, n_rows, blocks, CB, ch), jnp.bfloat16),
            jax.ShapeDtypeStruct(sides.shape, sides.dtype),
        ],
        (got, weight, sums, act, sides),
        scratch=[
            pltpu.VMEM((n_rows, deep, weight.shape[1]), weight.dtype),
            pltpu.VMEM((half, n_rows * deep), jnp.bfloat16),
            pltpu.VMEM((half, weight.shape[1]), jnp.float32),
            pltpu.SemaphoreType.DMA((4,)),
            pltpu.SemaphoreType.DMA((n_rows * n_slots,)),
        ],
        flops=2 * half * weight.size,
        moved=2 * weight.size,
        far=(1, 4),
        far_out=(1,),
        limit=LIMIT_A << 20,
    )


def own_second(got, weight):
    n_rows, _, n_frames, blocks, n_slots, _, ch = got.shape
    half = blocks * n_slots * CB
    deep = n_frames * ch

    def body(got_ref, w_ref, o_ref, next_ref, lhs, acc, keep_sems):
        keeps = []
        for r in range(n_rows):
            for s in range(n_slots):
                src = got_ref.at[r, 1, n_frames - 1, :, s]
                n = r * n_slots + s
                keeps.append(pltpu.make_async_copy(src, next_ref.at[s, 0, r], keep_sems.at[n]))
                keeps[-1].start()
        own_rows(got_ref, 1, lhs)
        acc[...] = dot(lhs[...], w_ref[...])
        give_rows(acc, ch, o_ref, None)
        for c in keeps:
            c.wait()

    return call(
        body,
        [
            sums_shape(blocks, n_slots, n_rows, ch),
            jax.ShapeDtypeStruct((n_slots, 2, n_rows, blocks, CB, ch), jnp.bfloat16),
        ],
        (got, weight),
        scratch=[
            pltpu.VMEM((half, n_rows * deep), jnp.bfloat16),
            pltpu.VMEM((half, weight.shape[1]), jnp.float32),
            pltpu.SemaphoreType.DMA((n_rows * n_slots,)),
        ],
        flops=2 * half * weight.size,
        moved=2 * weight.size,
        far_out=(1,),
    )


def side_sums(edge_ref, k, side_ref, w, lhs):
    n_frames, blocks, n_slots, _, ch = side_ref.shape
    for s in range(n_slots):
        for f in range(n_frames):
            value = masked(edge_ref, k, s, side_ref[f, :, s])
            lhs[:, s, :, f * ch : (f + 1) * ch] = value
    half = blocks * n_slots * CB
    return folded(dot(lhs[...].reshape(half, n_frames * ch), w), ch, True)


def second_activation(near, far, w_sides, sums, bias, gain, later, edges):
    n_frames, blocks, n_slots, _, ch = far.shape
    n_rows, n_cols, deep = sums.shape[0], blocks * CB, n_frames * ch

    def body(edge_ref, near_ref, far_ref, w_ref, z_ref, b_ref, g_ref, later_ref, o_ref, near_out, far_out, fetched_ref, lhs, sem):
        fetch = pltpu.make_async_copy(later_ref, fetched_ref, sem)
        fetch.start()
        for (side, y), out in zip(beside(edge_ref, near_ref.at[0], far_ref), (near_out, far_out)):
            total = side_sums(edge_ref, y, side, w_ref[y], lhs) + z_ref[y] + b_ref[...]
            for s in range(n_slots):
                value = activated(total[:, s].reshape(n_cols, ch), g_ref[...]).astype(jnp.bfloat16)
                o_ref[s, y] = value
                out[s] = value
        fetch.wait()

    row = jax.ShapeDtypeStruct((n_slots, n_cols, ch), jnp.bfloat16)
    return call(
        body,
        [jax.ShapeDtypeStruct((n_slots, n_rows, n_cols, ch), jnp.bfloat16), row, row, jax.ShapeDtypeStruct(later.shape, later.dtype)],
        (near, far, w_sides, sums, bias, gain, later),
        scalars=(edges,),
        scratch=[
            pltpu.VMEM((blocks, n_slots, CB, deep), jnp.bfloat16),
            pltpu.SemaphoreType.DMA,
        ],
        flops=2 * n_slots * n_cols * w_sides.size,
        moved=2 * w_sides.size,
        far=(6,),
        limit=LIMIT_B << 20,
    )


def before_sides(near, far, act, w_sides, w_act, sums, kept, edges):
    n_frames, blocks, n_slots, _, ch = far.shape
    n_rows, n_cols, deep = sums.shape[0], blocks * CB, n_frames * ch

    def body(edge_ref, near_ref, far_ref, act_ref, tiles_ref, w_ref, wa_ref, z_ref, kept_ref, o_ref, next_ref, lhs, lhs2, sem):
        copy = pltpu.make_async_copy(tiles_ref, next_ref.at[:, 1], sem)
        copy.start()
        add_own(act_ref, wa_ref, lhs2, o_ref, z_ref)
        for side, y in beside(edge_ref, near_ref.at[1], far_ref):
            o_ref[y] += side_sums(edge_ref, y, side, w_ref[y], lhs)
        copy.wait()

    return call(
        body,
        [jax.ShapeDtypeStruct(sums.shape, jnp.float32), jax.ShapeDtypeStruct(kept.shape, kept.dtype)],
        (near, far, act, act.reshape(n_slots, n_rows, blocks, CB, ch), w_sides, w_act, sums, kept),
        scalars=(edges,),
        scratch=[
            pltpu.VMEM((blocks, n_slots, CB, deep), jnp.bfloat16),
            pltpu.VMEM((n_slots * n_cols, n_rows * ch), jnp.bfloat16),
            pltpu.SemaphoreType.DMA,
        ],
        flops=2 * n_slots * n_cols * (w_sides.size + w_act.size),
        moved=2 * (w_sides.size + w_act.size),
        far=(7,),
        far_out=(1,),
        aliases={8: 1},
    )


def last_part(near, far, w_sides, sums, bias, frame, edges):
    n_slots, n_rows, n_cols, ch = frame.shape

    def body(edge_ref, near_ref, far_ref, w_ref, z_ref, b_ref, f_ref, o_ref, lhs):
        for side, y in beside(edge_ref, near_ref, far_ref):
            for s in range(n_slots):
                lhs[s * n_cols : (s + 1) * n_cols] = masked(edge_ref, y, s, side[s])
            total = folded(dot(lhs[...], w_ref[y]), ch, False)
            for s in range(n_slots):
                value = (total[s] + z_ref[y, :, s] + b_ref[...]).reshape(n_cols, ch)
                o_ref[s, y] = (value + f_ref[s, y].astype(jnp.float32)).astype(jnp.bfloat16)

    return call(
        body,
        [jax.ShapeDtypeStruct(frame.shape, jnp.bfloat16)],
        (near, far, w_sides, sums, bias, frame),
        scalars=(edges,),
        scratch=[pltpu.VMEM((n_slots * n_cols, ch), jnp.bfloat16)],
        flops=2 * n_slots * n_cols * w_sides.size,
        moved=2 * w_sides.size,
    )[0]


def local(
    frame_in,
    cache_first,
    cache_second,
    gain_first,
    gain_second,
    conv_first,
    conv_second,
    bias_first,
    bias_second,
    old_slot,
    new_slot,
    old_shift,
    new_shift,
    frame_count,
):
    n_slots, n_rows, n_cols, ch = frame_in.shape
    n_groups = lax.axis_size("stream")
    n_tiles = lax.axis_size("tile")
    my_group = lax.axis_index("stream")
    my_tile = lax.axis_index("tile")
    n_flight = old_slot.shape[0]
    blocks = n_cols // CB
    slot_ids = jnp.arange(n_flight, dtype=jnp.int32)
    held_new = new_slot[None, :] == slot_ids[:, None]
    source = lookup(held_new, old_slot)
    shift_after = lookup(held_new, new_shift)
    rotation = (shift_after - lookup(held_new, old_shift)) % n_tiles
    frames_done = lookup(held_new, frame_count)
    my_piece = my_group * n_tiles + my_tile
    my_frame = (my_piece // blocks) % 2
    keep = (frames_done >= 2 - my_frame).astype(jnp.int32)
    start = my_group * n_slots
    my_number = lax.dynamic_slice_in_dim((my_tile - shift_after) % n_tiles, start, n_slots)

    odd = my_tile % 2
    edges = jnp.stack(
        [my_number != 0, my_number != n_tiles - 1, jnp.broadcast_to(odd == 1, my_number.shape)]
    ).astype(jnp.int32)

    def swap_near(row):
        return lax.ppermute(row, "tile", [(i, i ^ 1) for i in range(n_tiles)])

    def swap_far(row):
        return lax.ppermute(
            row, "tile", [(i, (i + 2 * (i % 2) - 1) % n_tiles) for i in range(n_tiles)]
        )

    sent = pack(cache_first, cache_second).reshape(n_groups * n_tiles, n_slots, CB, ch)
    held = lax.all_to_all(sent, BOTH, 0, 0, tiled=True)

    act_own_1, act_sides_1 = spread(conv_first, False)
    act_first, near, far = first_activation(frame_in, gain_first[None], edges)
    act_near, act_far = swap_near(near), swap_far(far)
    held, act_first, act_near, act_far, act_own_1, act_sides_1 = lax.optimization_barrier(
        (held, act_first, act_near, act_far, act_own_1, act_sides_1)
    )

    moved = permute(held.reshape(n_groups, n_tiles, n_slots, CB, ch), source, rotation, keep)
    moved, act_later = lax.optimization_barrier((moved, act_first))
    got = lax.all_to_all(
        moved.reshape(n_groups * n_tiles, n_slots, CB, ch), BOTH, 0, 0, tiled=True
    )
    sums_1 = current_part(act_later, act_near, act_far, act_own_1, act_sides_1, edges)
    sums_1, conv_first, conv_second = lax.optimization_barrier((sums_1, conv_first, conv_second))
    act_own_2, act_sides_2 = spread(conv_second, False)
    own_1, sides_1 = spread(conv_first, True)
    own_2, sides_2 = spread(conv_second, True)
    got, sums_1, own_1, own_2, sides_1, sides_2, act_own_2, act_sides_2 = lax.optimization_barrier(
        (got, sums_1, own_1, own_2, sides_1, sides_2, act_own_2, act_sides_2)
    )
    got = got.reshape(n_rows, 2, 2, blocks, n_slots, CB, ch)

    def picked(row):
        return lax.dynamic_index_in_dim(got, row, 0, keepdims=False)

    rows_near, rows_far = swap_near(picked(1 - odd)), picked(odd)
    far_1, far_2 = swap_far(rows_far[0]), swap_far(rows_far[1])
    act_tiles = act_first.reshape(n_slots, n_rows, blocks, CB, ch)
    sums_1, next_first, sides_1 = own_first(got, own_1, sums_1, act_tiles, sides_1)
    act_second, near, far, own_2 = second_activation(
        rows_near, far_1, sides_1, sums_1, bias_first[None], gain_second[None], own_2, edges
    )
    act_near, act_far = swap_near(near), swap_far(far)
    got_later, act_later = lax.optimization_barrier((got, act_second))
    sums_2, kept = own_second(got_later, own_2)
    sums_2, next_second = before_sides(
        rows_near, far_2, act_later, sides_2, act_own_2, sums_2, kept, edges
    )
    mixed_frame = last_part(
        act_near, act_far, act_sides_2, sums_2, bias_second[None], frame_in, edges
    )
    whole = (n_slots, 2, n_rows, n_cols, ch)
    return (mixed_frame, next_first.reshape(whole), next_second.reshape(whole))


def solution(mesh):
    frame = P("stream", "tile", None, None)
    cache = P("stream", None, "tile", None, None)
    return jax.shard_map(
        local,
        mesh=mesh,
        in_specs=(frame, cache, cache) + (P(),) * 11,
        out_specs=(frame, cache, cache),
        check_vma=False,
    )
```

```python
import jax
import jax.numpy as jnp
from jax import lax
from jax.experimental import pallas as pl
from jax.experimental.pallas import tpu as pltpu
from jax.sharding import PartitionSpec as P

BOTH = ("stream", "tile")
CB = 8


def lookup(held_table, values):
    return jnp.sum(jnp.where(held_table, values[None, :], 0), axis=1)


def pack(first, second):
    n_slots, n_frames, n_rows, n_cols, ch = first.shape
    blocks = n_cols // CB
    parts = n_rows * 2 * n_frames

    def body(a_ref, b_ref, o_ref, held, in_sems, out_sems):
        whole = []
        for r in range(n_rows):
            for k, ref in enumerate((a_ref, b_ref)):
                for f in range(n_frames):
                    whole.append((r, k, f, ref))
        loads = []
        for p, (r, k, f, ref) in enumerate(whole):
            for s in range(n_slots):
                n = p * n_slots + s
                loads.append(
                    pltpu.make_async_copy(ref.at[s, f, r], held.at[r, k, f, :, s], in_sems.at[n])
                )
                loads[-1].start()
        stores = []
        for p, (r, k, f, _) in enumerate(whole):
            for s in range(n_slots):
                loads[p * n_slots + s].wait()
            stores.append(pltpu.make_async_copy(held.at[r, k, f], o_ref.at[r, k, f], out_sems.at[p]))
            stores[-1].start()
        for c in stores:
            c.wait()

    shape = (n_rows, 2, n_frames, blocks, n_slots, CB, ch)
    tiles = (n_slots, n_frames, n_rows, blocks, CB, ch)
    far = pl.BlockSpec(memory_space=pl.ANY)
    return pl.pallas_call(
        body,
        in_specs=[far, far],
        out_specs=far,
        out_shape=jax.ShapeDtypeStruct(shape, first.dtype),
        scratch_shapes=[
            pltpu.VMEM(shape, first.dtype),
            pltpu.SemaphoreType.DMA((parts * n_slots,)),
            pltpu.SemaphoreType.DMA((parts,)),
        ],
        compiler_params=pltpu.CompilerParams(vmem_limit_bytes=58 << 20),
    )(first.reshape(tiles), second.reshape(tiles))


def permute(held, source, rotation, keep):
    n_groups, n_tiles, n_slots, cols, ch = held.shape

    def body(source_ref, rotation_ref, keep_ref, i_ref, o_ref, made, sems):
        def stream(n, to):
            by = rotation_ref[n]
            old = source_ref[n]
            slot = lax.rem(n, n_slots)
            of, place = lax.div(old, n_slots), lax.rem(old, n_slots)

            @pl.when(keep_ref[n] != 0)
            def _():
                for t in range(n_tiles):
                    at = lax.rem(t + n_tiles - by, n_tiles)
                    made[to, t, slot] = i_ref[of, at, place]

            @pl.when(keep_ref[n] == 0)
            def _():
                made[to, :, slot] = jnp.zeros((n_tiles, cols, ch), made.dtype)

            return to

        copies = []
        for to in range(n_groups):
            lax.fori_loop(to * n_slots, (to + 1) * n_slots, stream, to)
            copies.append(pltpu.make_async_copy(made.at[to], o_ref.at[to], sems.at[to]))
            copies[-1].start()
        for c in copies:
            c.wait()

    smem = pl.BlockSpec(memory_space=pltpu.SMEM)
    return pl.pallas_call(
        body,
        in_specs=[smem, smem, smem, pl.BlockSpec(memory_space=pltpu.VMEM)],
        out_specs=pl.BlockSpec(memory_space=pl.ANY),
        out_shape=jax.ShapeDtypeStruct(held.shape, held.dtype),
        scratch_shapes=[
            pltpu.VMEM(held.shape, held.dtype),
            pltpu.SemaphoreType.DMA((n_groups,)),
        ],
        compiler_params=pltpu.CompilerParams(vmem_limit_bytes=52 << 20),
    )(source, rotation, keep, held)


VMEM_LIMIT = 16 << 20
LIMIT_A = 40
LIMIT_B = 40
LIMIT_C = 34


def call(body, out_shape, operands, scalars=(), scratch=(), flops=0, moved=0, far=(), far_out=(), aliases=None, limit=VMEM_LIMIT):
    in_specs = [pl.BlockSpec(memory_space=pltpu.SMEM) for _ in scalars]
    for k, _ in enumerate(operands):
        in_specs.append(pl.BlockSpec(memory_space=pl.ANY if k in far else pltpu.VMEM))
    out_specs = []
    for k, _ in enumerate(out_shape):
        out_specs.append(pl.BlockSpec(memory_space=pl.ANY if k in far_out else pltpu.VMEM))
    return pl.pallas_call(
        body,
        in_specs=in_specs,
        out_specs=out_specs,
        out_shape=list(out_shape),
        scratch_shapes=list(scratch),
        input_output_aliases=aliases or {},
        cost_estimate=pl.CostEstimate(flops=flops, bytes_accessed=moved, transcendentals=0),
        compiler_params=pltpu.CompilerParams(vmem_limit_bytes=limit),
    )(*scalars, *operands)


def spread(weight, own_times, side_times):
    _, n_y, n_x, ci, co = weight.shape
    wide = n_x * co
    n_own, n_side = len(own_times), len(side_times)

    def body(own_in, side_in, own_ref, side_ref):
        dy = pl.program_id(0)

        def side(y):
            for x in range(n_x):
                for t in range(n_side):
                    side_ref[y, t * ci : (t + 1) * ci, x * co : (x + 1) * co] = side_in[t, 0, x]

        def own(row, y):
            for x in range(n_x):
                for t in range(n_own):
                    lo = (row * n_own + t) * ci
                    at = y * wide + x * co
                    own_ref[lo : lo + ci, at : at + co] = own_in[t, 0, x]

        @pl.when(dy == 0)
        def _():
            side(0)
            own(0, 1)

        @pl.when(dy == 1)
        def _():
            own(0, 0)
            own(1, 1)

        @pl.when(dy == 2)
        def _():
            side(1)
            own(1, 0)

    def part(times):
        n = len(times)
        return pl.BlockSpec((n, 1, n_x, ci, co), lambda y, at=times[0] // n: (at, y, 0, 0, 0))

    shapes = [(2 * n_own * ci, 2 * wide), (2, n_side * ci, wide)]
    return pl.pallas_call(
        body,
        grid=(n_y,),
        in_specs=[part(own_times), part(side_times)],
        out_specs=[pl.BlockSpec(memory_space=pltpu.VMEM) for _ in shapes],
        out_shape=[jax.ShapeDtypeStruct(shape, weight.dtype) for shape in shapes],
        cost_estimate=pl.CostEstimate(flops=0, bytes_accessed=4 * weight.size, transcendentals=0),
        compiler_params=pltpu.CompilerParams(vmem_limit_bytes=20 << 20),
    )(weight, weight)


def activated(values, gain):
    u = values * lax.rsqrt(jnp.mean(values * values, axis=-1, keepdims=True) + 1e-06) * gain
    return u / (1.0 + jnp.exp(-u))


def first_activation(frame, gain, edges):
    n_slots, n_rows, n_cols, ch = frame.shape

    def body(edge_ref, f_ref, g_ref, o_ref, near_ref, far_ref):
        odd = edge_ref[2, 0]
        for s in range(n_slots):
            for r in range(n_rows):
                value = activated(f_ref[s, r].astype(jnp.float32), g_ref[...]).astype(jnp.bfloat16)
                o_ref[s, r] = value

                @pl.when(odd != r)
                def _(s=s, value=value):
                    near_ref[s] = value

                @pl.when(odd == r)
                def _(s=s, value=value):
                    far_ref[s] = value

    row = jax.ShapeDtypeStruct((n_slots, n_cols, ch), jnp.bfloat16)
    return call(
        body,
        [jax.ShapeDtypeStruct(frame.shape, jnp.bfloat16), row, row],
        (frame, gain),
        scalars=(edges,),
        flops=10 * frame.size,
        moved=6 * frame.size,
    )


def beside(edge_ref, near_ref, far_ref):
    odd = edge_ref[2, 0]
    return ((near_ref, 1 - odd), (far_ref, odd))


def folded(acc, ch, cols_first):
    tiles = acc.shape[0] // CB
    n_slots = 4
    blocks = tiles // n_slots
    lead = (blocks, n_slots) if cols_first else (n_slots, blocks)
    axis = 0 if cols_first else 1

    def plane(k):
        value = acc[:, k * ch : (k + 1) * ch].reshape(tiles, CB, ch)
        return value

    at = lax.broadcasted_iota(jnp.int32, (1, 1, CB, ch), 2)
    before = pltpu.roll(plane(0), 1, 1).reshape(lead + (CB, ch))
    after = pltpu.roll(plane(2), CB - 1, 1).reshape(lead + (CB, ch))
    gap = list(lead) + [CB, ch]
    gap[axis] = 1
    gap = jnp.zeros(gap, jnp.float32)
    before_prev = jnp.concatenate([gap, lax.slice_in_dim(before, 0, blocks - 1, axis=axis)], axis)
    after_next = jnp.concatenate([lax.slice_in_dim(after, 1, blocks, axis=axis), gap], axis)
    total = plane(1).reshape(lead + (CB, ch))
    total += jnp.where(at == 0, before_prev, before)
    total += jnp.where(at == CB - 1, after_next, after)
    return total


def add_into(o_ref, y, total, cols_first, base=None):
    if cols_first:
        o_ref[y] = total if base is None else base[y] + total
        return
    for s in range(total.shape[0]):
        o_ref[y, :, s] = total[s] if base is None else base[y, :, s] + total[s]


def masked(edge_ref, k, s, value):
    return jnp.where(edge_ref[k, s] != 0, value, jnp.zeros_like(value))


def dot(a, b):
    return jnp.dot(a, b, preferred_element_type=jnp.float32)


def sums_shape(blocks, n_slots, n_rows, ch):
    return jax.ShapeDtypeStruct((n_rows, blocks, n_slots, CB, ch), jnp.float32)


def add_sides(edge_ref, sides, w_ref, lhs, o_ref):
    n_slots, n_cols, ch = sides[0].shape
    for side, y in beside(edge_ref, *sides):
        for s in range(n_slots):
            lhs[s * n_cols : (s + 1) * n_cols] = masked(edge_ref, y, s, side[s])
        add_into(o_ref, y, folded(dot(lhs[...], w_ref[y]), ch, False), False, o_ref)


def add_own(act_ref, w_ref, lhs, o_ref, base):
    n_slots, n_rows, n_cols, ch = act_ref.shape
    for s in range(n_slots):
        for r in range(n_rows):
            lhs[s * n_cols : (s + 1) * n_cols, r * ch : (r + 1) * ch] = act_ref[s, r]
    both = dot(lhs[...], w_ref[...])
    wide = both.shape[1] // 2
    for y in range(n_rows):
        add_into(o_ref, y, folded(both[:, y * wide : (y + 1) * wide], ch, False), False, base)


def current_part(act, near, far, w_own, w_sides, edges):
    n_slots, n_rows, n_cols, ch = act.shape
    half = n_slots * n_cols

    def body(edge_ref, act_ref, near_ref, far_ref, wo_ref, ws_ref, o_ref, lhs, side):
        add_own(act_ref, wo_ref, lhs, o_ref, None)
        add_sides(edge_ref, (near_ref, far_ref), ws_ref, side, o_ref)

    return call(
        body,
        [sums_shape(n_cols // CB, n_slots, n_rows, ch)],
        (act, near, far, w_own, w_sides),
        scalars=(edges,),
        scratch=[
            pltpu.VMEM((half, n_rows * ch), jnp.bfloat16),
            pltpu.VMEM((half, ch), jnp.bfloat16),
        ],
        flops=2 * half * (w_own.size + w_sides.size),
        moved=2 * w_own.size + 8 * act.size,
    )[0]


def own_rows(got_ref, k, lhs):
    n_rows, _, n_frames, _, _, _, ch = got_ref.shape
    for r in range(n_rows):
        for f in range(n_frames):
            lo = (r * n_frames + f) * ch
            lhs[:, lo : lo + ch] = got_ref[r, k, f].reshape(lhs.shape[0], ch)


def give_rows(acc, ch, o_ref, base):
    n_rows = o_ref.shape[0]
    wide = acc.shape[1] // n_rows
    for y in range(n_rows):
        add_into(o_ref, y, folded(acc[:, y * wide : (y + 1) * wide], ch, True), True, base)


def own_first(got, weight, sums, act, sides):
    n_rows, _, n_frames, blocks, n_slots, _, ch = got.shape
    half = blocks * n_slots * CB
    deep = n_frames * ch

    def body(got_ref, w_ref, z_ref, act_ref, sides_ref, o_ref, next_ref, near_ref, w, lhs, acc, sems, keep_sems):
        loads = []
        for r in range(n_rows):
            rows = pl.ds(r * deep, deep)
            loads.append(pltpu.make_async_copy(w_ref.at[rows], w.at[r], sems.at[r]))
        loads[0].start()
        near = pltpu.make_async_copy(sides_ref, near_ref, sems.at[2])
        keeps = [pltpu.make_async_copy(act_ref, next_ref.at[:, 1], sems.at[3])]
        for r in range(n_rows):
            for s in range(n_slots):
                src = got_ref.at[r, 0, n_frames - 1, :, s]
                n = r * n_slots + s
                keeps.append(pltpu.make_async_copy(src, next_ref.at[s, 0, r], keep_sems.at[n]))
        own_rows(got_ref, 0, lhs)
        loads[0].wait()
        loads[1].start()
        acc[...] = dot(lhs[:, 0:deep], w[0])
        loads[1].wait()
        near.start()
        for c in keeps:
            c.start()
        acc[...] += dot(lhs[:, deep : 2 * deep], w[1])
        give_rows(acc, ch, o_ref, z_ref)
        for c in keeps:
            c.wait()
        near.wait()

    return call(
        body,
        [
            sums_shape(blocks, n_slots, n_rows, ch),
            jax.ShapeDtypeStruct((n_slots, 2, n_rows, blocks, CB, ch), jnp.bfloat16),
            jax.ShapeDtypeStruct(sides.shape, sides.dtype),
        ],
        (got, weight, sums, act, sides),
        scratch=[
            pltpu.VMEM((n_rows, deep, weight.shape[1]), weight.dtype),
            pltpu.VMEM((half, n_rows * deep), jnp.bfloat16),
            pltpu.VMEM((half, weight.shape[1]), jnp.float32),
            pltpu.SemaphoreType.DMA((4,)),
            pltpu.SemaphoreType.DMA((n_rows * n_slots,)),
        ],
        flops=2 * half * weight.size,
        moved=2 * weight.size,
        far=(1, 4),
        far_out=(1,),
        limit=LIMIT_A << 20,
    )


def side_sums(edge_ref, k, side_ref, w, lhs):
    n_frames, blocks, n_slots, _, ch = side_ref.shape
    for s in range(n_slots):
        for f in range(n_frames):
            value = masked(edge_ref, k, s, side_ref[f, :, s])
            lhs[:, s, :, f * ch : (f + 1) * ch] = value
    half = blocks * n_slots * CB
    return folded(dot(lhs[...].reshape(half, n_frames * ch), w), ch, True)


def second_activation(near, far, w_sides, sums, bias, gain, later, edges):
    n_frames, blocks, n_slots, _, ch = far.shape
    n_rows, n_cols, deep = sums.shape[0], blocks * CB, n_frames * ch
    first = later.shape[0] // 2

    def body(edge_ref, near_ref, far_ref, w_ref, z_ref, b_ref, g_ref, later_ref, o_ref, near_out, far_out, fetched_ref, lhs, sem):
        fetch = pltpu.make_async_copy(later_ref.at[pl.ds(0, first)], fetched_ref, sem)
        fetch.start()
        for (side, y), out in zip(beside(edge_ref, near_ref, far_ref), (near_out, far_out)):
            total = side_sums(edge_ref, y, side, w_ref[y], lhs) + z_ref[y] + b_ref[...]
            for s in range(n_slots):
                value = activated(total[:, s].reshape(n_cols, ch), g_ref[...]).astype(jnp.bfloat16)
                o_ref[s, y] = value
                out[s] = value
        fetch.wait()

    row = jax.ShapeDtypeStruct((n_slots, n_cols, ch), jnp.bfloat16)
    return call(
        body,
        [jax.ShapeDtypeStruct((n_slots, n_rows, n_cols, ch), jnp.bfloat16), row, row, jax.ShapeDtypeStruct((first, later.shape[1]), later.dtype)],
        (near, far, w_sides, sums, bias, gain, later),
        scalars=(edges,),
        scratch=[
            pltpu.VMEM((blocks, n_slots, CB, deep), jnp.bfloat16),
            pltpu.SemaphoreType.DMA,
        ],
        flops=2 * n_slots * n_cols * w_sides.size,
        moved=2 * w_sides.size,
        far=(6,),
        limit=LIMIT_B << 20,
    )


def before_sides(near, far, got, act, w_first, w_own, w_sides, edges):
    n_frames, blocks, n_slots, _, ch = far.shape
    n_rows = act.shape[1]
    half, deep = blocks * n_slots * CB, n_frames * ch
    row_deep = deep + ch
    tiles = act.reshape(n_slots, n_rows, blocks, CB, ch)

    def body(edge_ref, near_ref, far_ref, got_ref, act_ref, tiles_ref, w1_ref, w_ref, ws_ref, o_ref, next_ref, w2, lhs, side, acc, sems, keep_sems):
        load = pltpu.make_async_copy(w_ref.at[pl.ds(row_deep, row_deep)], w2, sems.at[0])
        load.start()
        keeps = [pltpu.make_async_copy(tiles_ref, next_ref.at[:, 1], sems.at[1])]
        for r in range(n_rows):
            for s in range(n_slots):
                src = got_ref.at[r, 1, n_frames - 1, :, s]
                n = r * n_slots + s
                keeps.append(pltpu.make_async_copy(src, next_ref.at[s, 0, r], keep_sems.at[n]))
        for r in range(n_rows):
            for f in range(n_frames):
                lhs[r, :, :, :, f * ch : (f + 1) * ch] = got_ref[r, 1, f]
            for s in range(n_slots):
                lhs[r, :, s, :, deep:row_deep] = act_ref[s, r].reshape(blocks, CB, ch)
        acc[...] = dot(lhs[0].reshape(half, row_deep), w1_ref[...])
        load.wait()
        for c in keeps:
            c.start()
        acc[...] += dot(lhs[1].reshape(half, row_deep), w2[...])
        give_rows(acc, ch, o_ref, None)
        for rows, y in beside(edge_ref, near_ref, far_ref):
            o_ref[y] += side_sums(edge_ref, y, rows, ws_ref[y], side)
        for c in keeps:
            c.wait()

    return call(
        body,
        [
            sums_shape(blocks, n_slots, n_rows, ch),
            jax.ShapeDtypeStruct((n_slots, 2, n_rows, blocks, CB, ch), jnp.bfloat16),
        ],
        (near, far, got, act, tiles, w_first, w_own, w_sides),
        scalars=(edges,),
        scratch=[
            pltpu.VMEM(w_first.shape, w_first.dtype),
            pltpu.VMEM((n_rows, blocks, n_slots, CB, row_deep), jnp.bfloat16),
            pltpu.VMEM((blocks, n_slots, CB, deep), jnp.bfloat16),
            pltpu.VMEM((half, w_own.shape[1]), jnp.float32),
            pltpu.SemaphoreType.DMA((2,)),
            pltpu.SemaphoreType.DMA((n_rows * n_slots,)),
        ],
        flops=2 * half * (w_own.size + w_sides.size),
        moved=2 * (w_own.size + w_sides.size),
        far=(6,),
        far_out=(1,),
        limit=LIMIT_C << 20,
    )


def last_part(near, far, w_sides, sums, bias, frame, edges):
    n_slots, n_rows, n_cols, ch = frame.shape

    def body(edge_ref, near_ref, far_ref, w_ref, z_ref, b_ref, f_ref, o_ref, lhs):
        for side, y in beside(edge_ref, near_ref, far_ref):
            for s in range(n_slots):
                lhs[s * n_cols : (s + 1) * n_cols] = masked(edge_ref, y, s, side[s])
            total = folded(dot(lhs[...], w_ref[y]), ch, False)
            for s in range(n_slots):
                value = (total[s] + z_ref[y, :, s] + b_ref[...]).reshape(n_cols, ch)
                o_ref[s, y] = (value + f_ref[s, y].astype(jnp.float32)).astype(jnp.bfloat16)

    return call(
        body,
        [jax.ShapeDtypeStruct(frame.shape, jnp.bfloat16)],
        (near, far, w_sides, sums, bias, frame),
        scalars=(edges,),
        scratch=[pltpu.VMEM((n_slots * n_cols, ch), jnp.bfloat16)],
        flops=2 * n_slots * n_cols * w_sides.size,
        moved=2 * w_sides.size,
    )[0]


def local(
    frame_in,
    cache_first,
    cache_second,
    gain_first,
    gain_second,
    conv_first,
    conv_second,
    bias_first,
    bias_second,
    old_slot,
    new_slot,
    old_shift,
    new_shift,
    frame_count,
):
    n_slots, n_rows, n_cols, ch = frame_in.shape
    n_groups = lax.axis_size("stream")
    n_tiles = lax.axis_size("tile")
    my_group = lax.axis_index("stream")
    my_tile = lax.axis_index("tile")
    n_flight = old_slot.shape[0]
    blocks = n_cols // CB
    slot_ids = jnp.arange(n_flight, dtype=jnp.int32)
    held_new = new_slot[None, :] == slot_ids[:, None]
    source = lookup(held_new, old_slot)
    shift_after = lookup(held_new, new_shift)
    rotation = (shift_after - lookup(held_new, old_shift)) % n_tiles
    frames_done = lookup(held_new, frame_count)
    my_piece = my_group * n_tiles + my_tile
    my_frame = (my_piece // blocks) % 2
    keep = (frames_done >= 2 - my_frame).astype(jnp.int32)
    start = my_group * n_slots
    my_number = lax.dynamic_slice_in_dim((my_tile - shift_after) % n_tiles, start, n_slots)

    odd = my_tile % 2
    edges = jnp.stack(
        [my_number != 0, my_number != n_tiles - 1, jnp.broadcast_to(odd == 1, my_number.shape)]
    ).astype(jnp.int32)

    def swap_near(row):
        return lax.ppermute(row, "tile", [(i, i ^ 1) for i in range(n_tiles)])

    def swap_far(row):
        return lax.ppermute(
            row, "tile", [(i, (i + 2 * (i % 2) - 1) % n_tiles) for i in range(n_tiles)]
        )

    sent = pack(cache_first, cache_second).reshape(n_groups * n_tiles, n_slots, CB, ch)
    held = lax.all_to_all(sent, BOTH, 0, 0, tiled=True)

    act_own_1, act_sides_1 = spread(conv_first, [2], [2])
    act_first, near, far = first_activation(frame_in, gain_first[None], edges)
    act_near, act_far = swap_near(near), swap_far(far)
    held, act_first, act_near, act_far, act_own_1, act_sides_1 = lax.optimization_barrier(
        (held, act_first, act_near, act_far, act_own_1, act_sides_1)
    )

    moved = permute(held.reshape(n_groups, n_tiles, n_slots, CB, ch), source, rotation, keep)
    moved, act_later = lax.optimization_barrier((moved, act_first))
    got = lax.all_to_all(
        moved.reshape(n_groups * n_tiles, n_slots, CB, ch), BOTH, 0, 0, tiled=True
    )
    sums_1 = current_part(act_later, act_near, act_far, act_own_1, act_sides_1, edges)
    sums_1, conv_first, conv_second = lax.optimization_barrier((sums_1, conv_first, conv_second))
    own_1, sides_1 = spread(conv_first, [0, 1], [0, 1])
    own_2, sides_2 = spread(conv_second, [0, 1, 2], [0, 1])
    act_sides_2 = conv_second[2, 0::2].transpose(0, 2, 1, 3).reshape(2, ch, 3 * ch)
    got, sums_1, own_1, own_2, sides_1, sides_2, act_sides_2 = lax.optimization_barrier(
        (got, sums_1, own_1, own_2, sides_1, sides_2, act_sides_2)
    )
    got = got.reshape(n_rows, 2, 2, blocks, n_slots, CB, ch)

    def picked(cache, row):
        return lax.dynamic_index_in_dim(got[:, cache], row, 0, keepdims=False)

    near_1, far_1 = swap_near(picked(0, 1 - odd)), swap_far(picked(0, odd))
    near_2, far_2 = swap_near(picked(1, 1 - odd)), swap_far(picked(1, odd))
    act_tiles = act_first.reshape(n_slots, n_rows, blocks, CB, ch)
    sums_1, next_first, sides_1 = own_first(got, own_1, sums_1, act_tiles, sides_1)
    act_second, near, far, own_first_half = second_activation(
        near_1, far_1, sides_1, sums_1, bias_first[None], gain_second[None], own_2, edges
    )
    act_near, act_far = swap_near(near), swap_far(far)
    sums_2, next_second = before_sides(
        near_2, far_2, got, act_second, own_first_half, own_2, sides_2, edges
    )
    mixed_frame = last_part(
        act_near, act_far, act_sides_2, sums_2, bias_second[None], frame_in, edges
    )
    whole = (n_slots, 2, n_rows, n_cols, ch)
    return (mixed_frame, next_first.reshape(whole), next_second.reshape(whole))


def solution(mesh):
    frame = P("stream", "tile", None, None)
    cache = P("stream", None, "tile", None, None)
    return jax.shard_map(
        local,
        mesh=mesh,
        in_specs=(frame, cache, cache) + (P(),) * 11,
        out_specs=(frame, cache, cache),
        check_vma=False,
    )
```

```python
import jax
import jax.numpy as jnp
from jax import lax
from jax.experimental import pallas as pl
from jax.experimental.pallas import tpu as pltpu
from jax.sharding import PartitionSpec as P

BOTH = ("stream", "tile")
CB = 8


def lookup(held_table, values):
    return jnp.sum(jnp.where(held_table, values[None, :], 0), axis=1)


def pack(first, second):
    n_slots, n_frames, n_rows, n_cols, ch = first.shape
    blocks = n_cols // CB
    parts = n_rows * 2 * n_frames

    def body(a_ref, b_ref, o_ref, held, in_sems, out_sems):
        whole = []
        for r in range(n_rows):
            for k, ref in enumerate((a_ref, b_ref)):
                for f in range(n_frames):
                    whole.append((r, k, f, ref))
        loads = []
        for p, (r, k, f, ref) in enumerate(whole):
            for s in range(n_slots):
                n = p * n_slots + s
                loads.append(
                    pltpu.make_async_copy(ref.at[s, f, r], held.at[r, k, f, :, s], in_sems.at[n])
                )
                loads[-1].start()
        stores = []
        for p, (r, k, f, _) in enumerate(whole):
            for s in range(n_slots):
                loads[p * n_slots + s].wait()
            stores.append(pltpu.make_async_copy(held.at[r, k, f], o_ref.at[r, k, f], out_sems.at[p]))
            stores[-1].start()
        for c in stores:
            c.wait()

    shape = (n_rows, 2, n_frames, blocks, n_slots, CB, ch)
    tiles = (n_slots, n_frames, n_rows, blocks, CB, ch)
    far = pl.BlockSpec(memory_space=pl.ANY)
    return pl.pallas_call(
        body,
        in_specs=[far, far],
        out_specs=far,
        out_shape=jax.ShapeDtypeStruct(shape, first.dtype),
        scratch_shapes=[
            pltpu.VMEM(shape, first.dtype),
            pltpu.SemaphoreType.DMA((parts * n_slots,)),
            pltpu.SemaphoreType.DMA((parts,)),
        ],
        compiler_params=pltpu.CompilerParams(vmem_limit_bytes=58 << 20),
    )(first.reshape(tiles), second.reshape(tiles))


def permute(held, source, rotation, keep):
    n_groups, n_tiles, n_slots, cols, ch = held.shape

    def body(source_ref, rotation_ref, keep_ref, i_ref, o_ref):
        def stream(n, _):
            by = rotation_ref[n]
            old = source_ref[n]
            to, slot = lax.div(n, n_slots), lax.rem(n, n_slots)
            of, place = lax.div(old, n_slots), lax.rem(old, n_slots)

            @pl.when(keep_ref[n] != 0)
            def _():
                for t in range(n_tiles):
                    at = lax.rem(t + n_tiles - by, n_tiles)
                    o_ref[to, t, slot] = i_ref[of, at, place]

            @pl.when(keep_ref[n] == 0)
            def _():
                o_ref[to, :, slot] = jnp.zeros((n_tiles, cols, ch), o_ref.dtype)

            return 0

        lax.fori_loop(0, n_groups * n_slots, stream, 0)

    smem, vmem = pl.BlockSpec(memory_space=pltpu.SMEM), pl.BlockSpec(memory_space=pltpu.VMEM)
    return pl.pallas_call(
        body,
        in_specs=[smem, smem, smem, vmem],
        out_specs=vmem,
        out_shape=jax.ShapeDtypeStruct(held.shape, held.dtype),
        compiler_params=pltpu.CompilerParams(vmem_limit_bytes=16 << 20),
    )(source, rotation, keep, held)


VMEM_LIMIT = 13 << 20


def call(body, out_shape, operands, scalars=(), scratch=(), flops=0, moved=0, far=(), far_out=(), aliases=None, limit=VMEM_LIMIT):
    in_specs = [pl.BlockSpec(memory_space=pltpu.SMEM) for _ in scalars]
    for k, _ in enumerate(operands):
        in_specs.append(pl.BlockSpec(memory_space=pl.ANY if k in far else pltpu.VMEM))
    out_specs = []
    for k, _ in enumerate(out_shape):
        out_specs.append(pl.BlockSpec(memory_space=pl.ANY if k in far_out else pltpu.VMEM))
    return pl.pallas_call(
        body,
        in_specs=in_specs,
        out_specs=out_specs,
        out_shape=list(out_shape),
        scratch_shapes=list(scratch),
        input_output_aliases=aliases or {},
        cost_estimate=pl.CostEstimate(flops=flops, bytes_accessed=moved, transcendentals=0),
        compiler_params=pltpu.CompilerParams(vmem_limit_bytes=limit),
    )(*scalars, *operands)


def spread(weight, past):
    n_t, n_y, n_x, ci, co = weight.shape
    wide = n_x * co
    times = n_t - 1 if past else 1

    def body(w_ref, own_ref, side_ref):
        dy = pl.program_id(0)

        def side(y):
            for x in range(n_x):
                for t in range(times):
                    side_ref[y, t * ci : (t + 1) * ci, x * co : (x + 1) * co] = w_ref[t, 0, x]

        def own(row, y):
            for x in range(n_x):
                for t in range(times):
                    lo = (row * times + t) * ci
                    at = y * wide + x * co
                    own_ref[lo : lo + ci, at : at + co] = w_ref[t, 0, x]

        @pl.when(dy == 0)
        def _():
            side(0)
            own(0, 1)

        @pl.when(dy == 1)
        def _():
            own(0, 0)
            own(1, 1)

        @pl.when(dy == 2)
        def _():
            side(1)
            own(1, 0)

    shapes = [(2 * times * ci, 2 * wide), (2, times * ci, wide)]
    first = 0 if past else n_t - 1
    return pl.pallas_call(
        body,
        grid=(n_y,),
        in_specs=[pl.BlockSpec((times, 1, n_x, ci, co), lambda y: (first, y, 0, 0, 0))],
        out_specs=[pl.BlockSpec(memory_space=pltpu.VMEM) for _ in shapes],
        out_shape=[jax.ShapeDtypeStruct(shape, weight.dtype) for shape in shapes],
        cost_estimate=pl.CostEstimate(flops=0, bytes_accessed=4 * weight.size, transcendentals=0),
        compiler_params=pltpu.CompilerParams(vmem_limit_bytes=16 << 20),
    )(weight)


def activated(values, gain):
    u = values * lax.rsqrt(jnp.mean(values * values, axis=-1, keepdims=True) + 1e-06) * gain
    return u / (1.0 + jnp.exp(-u))


def first_activation(frame, gain, edges):
    n_slots, n_rows, n_cols, ch = frame.shape

    def body(edge_ref, f_ref, g_ref, o_ref, near_ref, far_ref):
        odd = edge_ref[2, 0]
        for s in range(n_slots):
            for r in range(n_rows):
                value = activated(f_ref[s, r].astype(jnp.float32), g_ref[...]).astype(jnp.bfloat16)
                o_ref[s, r] = value

                @pl.when(odd != r)
                def _(s=s, value=value):
                    near_ref[s] = value

                @pl.when(odd == r)
                def _(s=s, value=value):
                    far_ref[s] = value

    row = jax.ShapeDtypeStruct((n_slots, n_cols, ch), jnp.bfloat16)
    return call(
        body,
        [jax.ShapeDtypeStruct(frame.shape, jnp.bfloat16), row, row],
        (frame, gain),
        scalars=(edges,),
        flops=10 * frame.size,
        moved=6 * frame.size,
    )


def beside(edge_ref, near_ref, far_ref):
    odd = edge_ref[2, 0]
    return ((near_ref, 1 - odd), (far_ref, odd))


def folded(acc, ch, cols_first):
    tiles = acc.shape[0] // CB
    n_slots = 4
    blocks = tiles // n_slots
    lead = (blocks, n_slots) if cols_first else (n_slots, blocks)
    axis = 0 if cols_first else 1

    def plane(k):
        value = acc[:, k * ch : (k + 1) * ch].reshape(tiles, CB, ch)
        return value

    at = lax.broadcasted_iota(jnp.int32, (1, 1, CB, ch), 2)
    before = pltpu.roll(plane(0), 1, 1).reshape(lead + (CB, ch))
    after = pltpu.roll(plane(2), CB - 1, 1).reshape(lead + (CB, ch))
    gap = list(lead) + [CB, ch]
    gap[axis] = 1
    gap = jnp.zeros(gap, jnp.float32)
    before_prev = jnp.concatenate([gap, lax.slice_in_dim(before, 0, blocks - 1, axis=axis)], axis)
    after_next = jnp.concatenate([lax.slice_in_dim(after, 1, blocks, axis=axis), gap], axis)
    total = plane(1).reshape(lead + (CB, ch))
    total += jnp.where(at == 0, before_prev, before)
    total += jnp.where(at == CB - 1, after_next, after)
    return total


def add_into(o_ref, y, total, cols_first, base=None):
    if cols_first:
        o_ref[y] = total if base is None else base[y] + total
        return
    for s in range(total.shape[0]):
        o_ref[y, :, s] = total[s] if base is None else base[y, :, s] + total[s]


def masked(edge_ref, k, s, value):
    return jnp.where(edge_ref[k, s] != 0, value, jnp.zeros_like(value))


def dot(a, b):
    return jnp.dot(a, b, preferred_element_type=jnp.float32)


def sums_shape(blocks, n_slots, n_rows, ch):
    return jax.ShapeDtypeStruct((n_rows, blocks, n_slots, CB, ch), jnp.float32)


def add_sides(edge_ref, sides, w_ref, lhs, o_ref):
    n_slots, n_cols, ch = sides[0].shape
    for side, y in beside(edge_ref, *sides):
        for s in range(n_slots):
            lhs[s * n_cols : (s + 1) * n_cols] = masked(edge_ref, y, s, side[s])
        add_into(o_ref, y, folded(dot(lhs[...], w_ref[y]), ch, False), False, o_ref)


def add_own(act_ref, w_ref, lhs, o_ref, base):
    n_slots, n_rows, n_cols, ch = act_ref.shape
    for s in range(n_slots):
        for r in range(n_rows):
            lhs[s * n_cols : (s + 1) * n_cols, r * ch : (r + 1) * ch] = act_ref[s, r]
    both = dot(lhs[...], w_ref[...])
    wide = both.shape[1] // 2
    for y in range(n_rows):
        add_into(o_ref, y, folded(both[:, y * wide : (y + 1) * wide], ch, False), False, base)


def current_part(act, near, far, w_own, w_sides, edges):
    n_slots, n_rows, n_cols, ch = act.shape
    half = n_slots * n_cols

    def body(edge_ref, act_ref, near_ref, far_ref, wo_ref, ws_ref, o_ref, lhs, side):
        add_own(act_ref, wo_ref, lhs, o_ref, None)
        add_sides(edge_ref, (near_ref, far_ref), ws_ref, side, o_ref)

    return call(
        body,
        [sums_shape(n_cols // CB, n_slots, n_rows, ch)],
        (act, near, far, w_own, w_sides),
        scalars=(edges,),
        scratch=[
            pltpu.VMEM((half, n_rows * ch), jnp.bfloat16),
            pltpu.VMEM((half, ch), jnp.bfloat16),
        ],
        flops=2 * half * (w_own.size + w_sides.size),
        moved=2 * w_own.size + 8 * act.size,
    )[0]


def own_rows(got_ref, k, lhs):
    n_rows, _, n_frames, _, _, _, ch = got_ref.shape
    for r in range(n_rows):
        for f in range(n_frames):
            lo = (r * n_frames + f) * ch
            lhs[:, lo : lo + ch] = got_ref[r, k, f].reshape(lhs.shape[0], ch)


def give_rows(acc, ch, o_ref, base):
    n_rows = o_ref.shape[0]
    wide = acc.shape[1] // n_rows
    for y in range(n_rows):
        add_into(o_ref, y, folded(acc[:, y * wide : (y + 1) * wide], ch, True), True, base)


def own_first(got, weight, sums, act):
    n_rows, _, n_frames, blocks, n_slots, _, ch = got.shape
    half = blocks * n_slots * CB
    deep = n_frames * ch

    def body(got_ref, w_ref, z_ref, act_ref, o_ref, next_ref, lhs, acc, keep_sems, act_sem):
        keeps = [pltpu.make_async_copy(act_ref, next_ref.at[:, 1], act_sem)]
        for r in range(n_rows):
            for s in range(n_slots):
                src = got_ref.at[r, 0, n_frames - 1, :, s]
                n = r * n_slots + s
                keeps.append(pltpu.make_async_copy(src, next_ref.at[s, 0, r], keep_sems.at[n]))
        for c in keeps:
            c.start()
        own_rows(got_ref, 0, lhs)
        acc[...] = dot(lhs[...], w_ref[...])
        give_rows(acc, ch, o_ref, z_ref)
        for c in keeps:
            c.wait()

    return call(
        body,
        [
            sums_shape(blocks, n_slots, n_rows, ch),
            jax.ShapeDtypeStruct((n_slots, 2, n_rows, blocks, CB, ch), jnp.bfloat16),
        ],
        (got, weight, sums, act),
        scratch=[
            pltpu.VMEM((half, n_rows * deep), jnp.bfloat16),
            pltpu.VMEM((half, weight.shape[1]), jnp.float32),
            pltpu.SemaphoreType.DMA((n_rows * n_slots,)),
            pltpu.SemaphoreType.DMA,
        ],
        flops=2 * half * weight.size,
        moved=2 * weight.size,
        far_out=(1,),
    )


def own_second(got, weight):
    n_rows, _, n_frames, blocks, n_slots, _, ch = got.shape
    half = blocks * n_slots * CB
    deep = n_frames * ch

    def body(got_ref, w_ref, o_ref, next_ref, lhs, acc, keep_sems):
        keeps = []
        for r in range(n_rows):
            for s in range(n_slots):
                src = got_ref.at[r, 1, n_frames - 1, :, s]
                n = r * n_slots + s
                keeps.append(pltpu.make_async_copy(src, next_ref.at[s, 0, r], keep_sems.at[n]))
                keeps[-1].start()
        own_rows(got_ref, 1, lhs)
        acc[...] = dot(lhs[...], w_ref[...])
        give_rows(acc, ch, o_ref, None)
        for c in keeps:
            c.wait()

    return call(
        body,
        [
            sums_shape(blocks, n_slots, n_rows, ch),
            jax.ShapeDtypeStruct((n_slots, 2, n_rows, blocks, CB, ch), jnp.bfloat16),
        ],
        (got, weight),
        scratch=[
            pltpu.VMEM((half, n_rows * deep), jnp.bfloat16),
            pltpu.VMEM((half, weight.shape[1]), jnp.float32),
            pltpu.SemaphoreType.DMA((n_rows * n_slots,)),
        ],
        flops=2 * half * weight.size,
        moved=2 * weight.size,
        far_out=(1,),
    )


def side_sums(edge_ref, k, side_ref, w, lhs):
    n_frames, blocks, n_slots, _, ch = side_ref.shape
    for s in range(n_slots):
        for f in range(n_frames):
            value = masked(edge_ref, k, s, side_ref[f, :, s])
            lhs[:, s, :, f * ch : (f + 1) * ch] = value
    half = blocks * n_slots * CB
    return folded(dot(lhs[...].reshape(half, n_frames * ch), w), ch, True)


def second_activation(near, far, w_sides, sums, bias, gain, edges):
    n_frames, blocks, n_slots, _, ch = far.shape
    n_rows, n_cols, deep = sums.shape[0], blocks * CB, n_frames * ch

    def body(edge_ref, near_ref, far_ref, w_ref, z_ref, b_ref, g_ref, o_ref, near_out, far_out, lhs):
        for (side, y), out in zip(beside(edge_ref, near_ref, far_ref), (near_out, far_out)):
            total = side_sums(edge_ref, y, side, w_ref[y], lhs) + z_ref[y] + b_ref[...]
            for s in range(n_slots):
                value = activated(total[:, s].reshape(n_cols, ch), g_ref[...]).astype(jnp.bfloat16)
                o_ref[s, y] = value
                out[s] = value

    row = jax.ShapeDtypeStruct((n_slots, n_cols, ch), jnp.bfloat16)
    return call(
        body,
        [jax.ShapeDtypeStruct((n_slots, n_rows, n_cols, ch), jnp.bfloat16), row, row],
        (near, far, w_sides, sums, bias, gain),
        scalars=(edges,),
        scratch=[
            pltpu.VMEM((blocks, n_slots, CB, deep), jnp.bfloat16),
        ],
        flops=2 * n_slots * n_cols * w_sides.size,
        moved=2 * w_sides.size,
    )


def before_sides(near, far, act, w_sides, w_act, sums, kept, edges):
    n_frames, blocks, n_slots, _, ch = far.shape
    n_rows, n_cols, deep = sums.shape[0], blocks * CB, n_frames * ch

    def body(edge_ref, near_ref, far_ref, act_ref, tiles_ref, w_ref, wa_ref, z_ref, kept_ref, o_ref, next_ref, lhs, lhs2, sem):
        copy = pltpu.make_async_copy(tiles_ref, next_ref.at[:, 1], sem)
        copy.start()
        add_own(act_ref, wa_ref, lhs2, o_ref, z_ref)
        for side, y in beside(edge_ref, near_ref, far_ref):
            o_ref[y] += side_sums(edge_ref, y, side, w_ref[y], lhs)
        copy.wait()

    return call(
        body,
        [jax.ShapeDtypeStruct(sums.shape, jnp.float32), jax.ShapeDtypeStruct(kept.shape, kept.dtype)],
        (near, far, act, act.reshape(n_slots, n_rows, blocks, CB, ch), w_sides, w_act, sums, kept),
        scalars=(edges,),
        scratch=[
            pltpu.VMEM((blocks, n_slots, CB, deep), jnp.bfloat16),
            pltpu.VMEM((n_slots * n_cols, n_rows * ch), jnp.bfloat16),
            pltpu.SemaphoreType.DMA,
        ],
        flops=2 * n_slots * n_cols * (w_sides.size + w_act.size),
        moved=2 * (w_sides.size + w_act.size),
        far=(7,),
        far_out=(1,),
        aliases={8: 1},
    )


def last_part(near, far, w_sides, sums, bias, frame, edges):
    n_slots, n_rows, n_cols, ch = frame.shape

    def body(edge_ref, near_ref, far_ref, w_ref, z_ref, b_ref, f_ref, o_ref, lhs):
        for side, y in beside(edge_ref, near_ref, far_ref):
            for s in range(n_slots):
                lhs[s * n_cols : (s + 1) * n_cols] = masked(edge_ref, y, s, side[s])
            total = folded(dot(lhs[...], w_ref[y]), ch, False)
            for s in range(n_slots):
                value = (total[s] + z_ref[y, :, s] + b_ref[...]).reshape(n_cols, ch)
                o_ref[s, y] = (value + f_ref[s, y].astype(jnp.float32)).astype(jnp.bfloat16)

    return call(
        body,
        [jax.ShapeDtypeStruct(frame.shape, jnp.bfloat16)],
        (near, far, w_sides, sums, bias, frame),
        scalars=(edges,),
        scratch=[pltpu.VMEM((n_slots * n_cols, ch), jnp.bfloat16)],
        flops=2 * n_slots * n_cols * w_sides.size,
        moved=2 * w_sides.size,
    )[0]


def local(
    frame_in,
    cache_first,
    cache_second,
    gain_first,
    gain_second,
    conv_first,
    conv_second,
    bias_first,
    bias_second,
    old_slot,
    new_slot,
    old_shift,
    new_shift,
    frame_count,
):
    n_slots, n_rows, n_cols, ch = frame_in.shape
    n_groups = lax.axis_size("stream")
    n_tiles = lax.axis_size("tile")
    my_group = lax.axis_index("stream")
    my_tile = lax.axis_index("tile")
    n_flight = old_slot.shape[0]
    blocks = n_cols // CB
    slot_ids = jnp.arange(n_flight, dtype=jnp.int32)
    held_new = new_slot[None, :] == slot_ids[:, None]
    source = lookup(held_new, old_slot)
    shift_after = lookup(held_new, new_shift)
    rotation = (shift_after - lookup(held_new, old_shift)) % n_tiles
    frames_done = lookup(held_new, frame_count)
    my_piece = my_group * n_tiles + my_tile
    my_frame = (my_piece // blocks) % 2
    keep = (frames_done >= 2 - my_frame).astype(jnp.int32)
    start = my_group * n_slots
    my_number = lax.dynamic_slice_in_dim((my_tile - shift_after) % n_tiles, start, n_slots)

    odd = my_tile % 2
    edges = jnp.stack(
        [my_number != 0, my_number != n_tiles - 1, jnp.broadcast_to(odd == 1, my_number.shape)]
    ).astype(jnp.int32)

    def swap_near(row):
        return lax.ppermute(row, "tile", [(i, i ^ 1) for i in range(n_tiles)])

    def swap_far(row):
        return lax.ppermute(
            row, "tile", [(i, (i + 2 * (i % 2) - 1) % n_tiles) for i in range(n_tiles)]
        )

    sent = pack(cache_first, cache_second).reshape(n_groups * n_tiles, n_slots, CB, ch)
    held = lax.all_to_all(sent, BOTH, 0, 0, tiled=True)

    act_own_1, act_sides_1 = spread(conv_first, False)
    act_first, near, far = first_activation(frame_in, gain_first[None], edges)
    act_near, act_far = swap_near(near), swap_far(far)
    held, act_first, act_near, act_far, act_own_1, act_sides_1 = lax.optimization_barrier(
        (held, act_first, act_near, act_far, act_own_1, act_sides_1)
    )

    moved = permute(held.reshape(n_groups, n_tiles, n_slots, CB, ch), source, rotation, keep)
    moved, act_later = lax.optimization_barrier((moved, act_first))
    got = lax.all_to_all(
        moved.reshape(n_groups * n_tiles, n_slots, CB, ch), BOTH, 0, 0, tiled=True
    )
    sums_1 = current_part(act_later, act_near, act_far, act_own_1, act_sides_1, edges)
    sums_1, conv_first, conv_second = lax.optimization_barrier((sums_1, conv_first, conv_second))
    act_own_2, act_sides_2 = spread(conv_second, False)
    own_1, sides_1 = spread(conv_first, True)
    own_2, sides_2 = spread(conv_second, True)
    got, sums_1, own_1, own_2, sides_1, sides_2, act_own_2, act_sides_2 = lax.optimization_barrier(
        (got, sums_1, own_1, own_2, sides_1, sides_2, act_own_2, act_sides_2)
    )
    got = got.reshape(n_rows, 2, 2, blocks, n_slots, CB, ch)

    def picked(cache, row):
        return lax.dynamic_index_in_dim(got[:, cache], row, 0, keepdims=False)

    near_1, far_1 = swap_near(picked(0, 1 - odd)), swap_far(picked(0, odd))
    near_2, far_2 = swap_near(picked(1, 1 - odd)), swap_far(picked(1, odd))
    act_tiles = act_first.reshape(n_slots, n_rows, blocks, CB, ch)
    sums_1, next_first = own_first(got, own_1, sums_1, act_tiles)
    act_second, near, far = second_activation(
        near_1, far_1, sides_1, sums_1, bias_first[None], gain_second[None], edges
    )
    act_near, act_far = swap_near(near), swap_far(far)
    got_later, act_later = lax.optimization_barrier((got, act_second))
    sums_2, kept = own_second(got_later, own_2)
    sums_2, next_second = before_sides(
        near_2, far_2, act_later, sides_2, act_own_2, sums_2, kept, edges
    )
    mixed_frame = last_part(
        act_near, act_far, act_sides_2, sums_2, bias_second[None], frame_in, edges
    )
    whole = (n_slots, 2, n_rows, n_cols, ch)
    return (mixed_frame, next_first.reshape(whole), next_second.reshape(whole))


def solution(mesh):
    frame = P("stream", "tile", None, None)
    cache = P("stream", None, "tile", None, None)
    return jax.shard_map(
        local,
        mesh=mesh,
        in_specs=(frame, cache, cache) + (P(),) * 11,
        out_specs=(frame, cache, cache),
        check_vma=False,
    )
```

```python
import jax
import jax.numpy as jnp
from jax import lax
from jax.experimental import pallas as pl
from jax.experimental.pallas import tpu as pltpu
from jax.sharding import PartitionSpec as P

BOTH = ("stream", "tile")
CB = 8


def lookup(held_table, values):
    return jnp.sum(jnp.where(held_table, values[None, :], 0), axis=1)


def pack(first, second):
    n_slots, n_frames, n_rows, n_cols, ch = first.shape
    blocks = n_cols // CB
    parts = n_rows * 2 * n_frames

    def body(a_ref, b_ref, o_ref, held, in_sems, out_sems):
        whole = []
        for r in range(n_rows):
            for k, ref in enumerate((a_ref, b_ref)):
                for f in range(n_frames):
                    whole.append((r, k, f, ref))
        loads = []
        for p, (r, k, f, ref) in enumerate(whole):
            for s in range(n_slots):
                n = p * n_slots + s
                loads.append(
                    pltpu.make_async_copy(ref.at[s, f, r], held.at[r, k, f, :, s], in_sems.at[n])
                )
                loads[-1].start()
        stores = []
        for p, (r, k, f, _) in enumerate(whole):
            for s in range(n_slots):
                loads[p * n_slots + s].wait()
            stores.append(pltpu.make_async_copy(held.at[r, k, f], o_ref.at[r, k, f], out_sems.at[p]))
            stores[-1].start()
        for c in stores:
            c.wait()

    shape = (n_rows, 2, n_frames, blocks, n_slots, CB, ch)
    tiles = (n_slots, n_frames, n_rows, blocks, CB, ch)
    far = pl.BlockSpec(memory_space=pl.ANY)
    return pl.pallas_call(
        body,
        in_specs=[far, far],
        out_specs=far,
        out_shape=jax.ShapeDtypeStruct(shape, first.dtype),
        scratch_shapes=[
            pltpu.VMEM(shape, first.dtype),
            pltpu.SemaphoreType.DMA((parts * n_slots,)),
            pltpu.SemaphoreType.DMA((parts,)),
        ],
        compiler_params=pltpu.CompilerParams(vmem_limit_bytes=58 << 20),
    )(first.reshape(tiles), second.reshape(tiles))


def permute(held, source, rotation, keep):
    n_groups, n_tiles, n_slots, cols, ch = held.shape

    def body(source_ref, rotation_ref, keep_ref, i_ref, o_ref):
        def stream(n, _):
            by = rotation_ref[n]
            old = source_ref[n]
            to, slot = lax.div(n, n_slots), lax.rem(n, n_slots)
            of, place = lax.div(old, n_slots), lax.rem(old, n_slots)

            @pl.when(keep_ref[n] != 0)
            def _():
                for t in range(n_tiles):
                    at = lax.rem(t + n_tiles - by, n_tiles)
                    o_ref[to, t, slot] = i_ref[of, at, place]

            @pl.when(keep_ref[n] == 0)
            def _():
                o_ref[to, :, slot] = jnp.zeros((n_tiles, cols, ch), o_ref.dtype)

            return 0

        lax.fori_loop(0, n_groups * n_slots, stream, 0)

    smem, vmem = pl.BlockSpec(memory_space=pltpu.SMEM), pl.BlockSpec(memory_space=pltpu.VMEM)
    return pl.pallas_call(
        body,
        in_specs=[smem, smem, smem, vmem],
        out_specs=vmem,
        out_shape=jax.ShapeDtypeStruct(held.shape, held.dtype),
        compiler_params=pltpu.CompilerParams(vmem_limit_bytes=16 << 20),
    )(source, rotation, keep, held)


VMEM_LIMIT = 13 << 20


def call(body, out_shape, operands, scalars=(), scratch=(), flops=0, moved=0, far=(), far_out=(), aliases=None, limit=VMEM_LIMIT):
    in_specs = [pl.BlockSpec(memory_space=pltpu.SMEM) for _ in scalars]
    for k, _ in enumerate(operands):
        in_specs.append(pl.BlockSpec(memory_space=pl.ANY if k in far else pltpu.VMEM))
    out_specs = []
    for k, _ in enumerate(out_shape):
        out_specs.append(pl.BlockSpec(memory_space=pl.ANY if k in far_out else pltpu.VMEM))
    return pl.pallas_call(
        body,
        in_specs=in_specs,
        out_specs=out_specs,
        out_shape=list(out_shape),
        scratch_shapes=list(scratch),
        input_output_aliases=aliases or {},
        cost_estimate=pl.CostEstimate(flops=flops, bytes_accessed=moved, transcendentals=0),
        compiler_params=pltpu.CompilerParams(vmem_limit_bytes=limit),
    )(*scalars, *operands)


def spread(weight, past):
    n_t, n_y, n_x, ci, co = weight.shape
    wide = n_x * co
    times = n_t - 1 if past else 1

    def body(w_ref, own_ref, side_ref):
        dy = pl.program_id(0)

        def side(y):
            for x in range(n_x):
                for t in range(times):
                    side_ref[y, t * ci : (t + 1) * ci, x * co : (x + 1) * co] = w_ref[t, 0, x]

        def own(row, y):
            for x in range(n_x):
                for t in range(times):
                    lo = (row * times + t) * ci
                    at = y * wide + x * co
                    own_ref[lo : lo + ci, at : at + co] = w_ref[t, 0, x]

        @pl.when(dy == 0)
        def _():
            side(0)
            own(0, 1)

        @pl.when(dy == 1)
        def _():
            own(0, 0)
            own(1, 1)

        @pl.when(dy == 2)
        def _():
            side(1)
            own(1, 0)

    shapes = [(2 * times * ci, 2 * wide), (2, times * ci, wide)]
    first = 0 if past else n_t - 1
    return pl.pallas_call(
        body,
        grid=(n_y,),
        in_specs=[pl.BlockSpec((times, 1, n_x, ci, co), lambda y: (first, y, 0, 0, 0))],
        out_specs=[pl.BlockSpec(memory_space=pltpu.VMEM) for _ in shapes],
        out_shape=[jax.ShapeDtypeStruct(shape, weight.dtype) for shape in shapes],
        cost_estimate=pl.CostEstimate(flops=0, bytes_accessed=4 * weight.size, transcendentals=0),
        compiler_params=pltpu.CompilerParams(vmem_limit_bytes=16 << 20),
    )(weight)


def activated(values, gain):
    u = values * lax.rsqrt(jnp.mean(values * values, axis=-1, keepdims=True) + 1e-06) * gain
    return u / (1.0 + jnp.exp(-u))


def first_activation(frame, gain, edges):
    n_slots, n_rows, n_cols, ch = frame.shape

    def body(edge_ref, f_ref, g_ref, o_ref, near_ref, far_ref):
        odd = edge_ref[2, 0]
        for s in range(n_slots):
            for r in range(n_rows):
                value = activated(f_ref[s, r].astype(jnp.float32), g_ref[...]).astype(jnp.bfloat16)
                o_ref[s, r] = value

                @pl.when(odd != r)
                def _(s=s, value=value):
                    near_ref[s] = value

                @pl.when(odd == r)
                def _(s=s, value=value):
                    far_ref[s] = value

    row = jax.ShapeDtypeStruct((n_slots, n_cols, ch), jnp.bfloat16)
    return call(
        body,
        [jax.ShapeDtypeStruct(frame.shape, jnp.bfloat16), row, row],
        (frame, gain),
        scalars=(edges,),
        flops=10 * frame.size,
        moved=6 * frame.size,
    )


def beside(edge_ref, near_ref, far_ref):
    odd = edge_ref[2, 0]
    return ((near_ref, 1 - odd), (far_ref, odd))


def folded(acc, ch, cols_first):
    tiles = acc.shape[0] // CB
    n_slots = 4
    blocks = tiles // n_slots
    lead = (blocks, n_slots) if cols_first else (n_slots, blocks)
    axis = 0 if cols_first else 1

    def plane(k):
        value = acc[:, k * ch : (k + 1) * ch].reshape(tiles, CB, ch)
        return value

    at = lax.broadcasted_iota(jnp.int32, (1, 1, CB, ch), 2)
    before = pltpu.roll(plane(0), 1, 1).reshape(lead + (CB, ch))
    after = pltpu.roll(plane(2), CB - 1, 1).reshape(lead + (CB, ch))
    gap = list(lead) + [CB, ch]
    gap[axis] = 1
    gap = jnp.zeros(gap, jnp.float32)
    before_prev = jnp.concatenate([gap, lax.slice_in_dim(before, 0, blocks - 1, axis=axis)], axis)
    after_next = jnp.concatenate([lax.slice_in_dim(after, 1, blocks, axis=axis), gap], axis)
    total = plane(1).reshape(lead + (CB, ch))
    total += jnp.where(at == 0, before_prev, before)
    total += jnp.where(at == CB - 1, after_next, after)
    return total


def add_into(o_ref, y, total, cols_first, base=None):
    if cols_first:
        o_ref[y] = total if base is None else base[y] + total
        return
    for s in range(total.shape[0]):
        o_ref[y, :, s] = total[s] if base is None else base[y, :, s] + total[s]


def masked(edge_ref, k, s, value):
    return jnp.where(edge_ref[k, s] != 0, value, jnp.zeros_like(value))


def dot(a, b):
    return jnp.dot(a, b, preferred_element_type=jnp.float32)


def sums_shape(blocks, n_slots, n_rows, ch):
    return jax.ShapeDtypeStruct((n_rows, blocks, n_slots, CB, ch), jnp.float32)


def add_sides(edge_ref, sides, w_ref, lhs, o_ref):
    n_slots, n_cols, ch = sides[0].shape
    for side, y in beside(edge_ref, *sides):
        for s in range(n_slots):
            lhs[s * n_cols : (s + 1) * n_cols] = masked(edge_ref, y, s, side[s])
        add_into(o_ref, y, folded(dot(lhs[...], w_ref[y]), ch, False), False, o_ref)


def add_own(act_ref, w_ref, lhs, o_ref, base):
    n_slots, n_rows, n_cols, ch = act_ref.shape
    for s in range(n_slots):
        for r in range(n_rows):
            lhs[s * n_cols : (s + 1) * n_cols, r * ch : (r + 1) * ch] = act_ref[s, r]
    both = dot(lhs[...], w_ref[...])
    wide = both.shape[1] // 2
    for y in range(n_rows):
        add_into(o_ref, y, folded(both[:, y * wide : (y + 1) * wide], ch, False), False, base)


def current_part(act, w_own):
    n_slots, n_rows, n_cols, ch = act.shape
    half = n_slots * n_cols

    def body(act_ref, w_ref, o_ref, lhs):
        add_own(act_ref, w_ref, lhs, o_ref, None)

    return call(
        body,
        [sums_shape(n_cols // CB, n_slots, n_rows, ch)],
        (act, w_own),
        scratch=[pltpu.VMEM((half, n_rows * ch), jnp.bfloat16)],
        flops=2 * half * w_own.size,
        moved=2 * w_own.size + 8 * act.size,
    )[0]


def own_rows(got_ref, k, lhs):
    n_rows, _, n_frames, _, _, _, ch = got_ref.shape
    for r in range(n_rows):
        for f in range(n_frames):
            lo = (r * n_frames + f) * ch
            lhs[:, lo : lo + ch] = got_ref[r, k, f].reshape(lhs.shape[0], ch)


def give_rows(acc, ch, o_ref, base):
    n_rows = o_ref.shape[0]
    wide = acc.shape[1] // n_rows
    for y in range(n_rows):
        add_into(o_ref, y, folded(acc[:, y * wide : (y + 1) * wide], ch, True), True, base)


def own_first(got, weight, sums, act, near, far, w_sides, edges):
    n_rows, _, n_frames, blocks, n_slots, _, ch = got.shape
    half = blocks * n_slots * CB
    deep = n_frames * ch

    def body(edge_ref, got_ref, w_ref, z_ref, act_ref, near_ref, far_ref, ws_ref, o_ref, next_ref, lhs, acc, side, keep_sems, act_sem):
        keeps = [pltpu.make_async_copy(act_ref, next_ref.at[:, 1], act_sem)]
        for r in range(n_rows):
            for s in range(n_slots):
                src = got_ref.at[r, 0, n_frames - 1, :, s]
                n = r * n_slots + s
                keeps.append(pltpu.make_async_copy(src, next_ref.at[s, 0, r], keep_sems.at[n]))
        for c in keeps:
            c.start()
        own_rows(got_ref, 0, lhs)
        acc[...] = dot(lhs[...], w_ref[...])
        give_rows(acc, ch, o_ref, z_ref)
        add_sides(edge_ref, (near_ref, far_ref), ws_ref, side, o_ref)
        for c in keeps:
            c.wait()

    return call(
        body,
        [
            sums_shape(blocks, n_slots, n_rows, ch),
            jax.ShapeDtypeStruct((n_slots, 2, n_rows, blocks, CB, ch), jnp.bfloat16),
        ],
        (got, weight, sums, act, near, far, w_sides),
        scalars=(edges,),
        scratch=[
            pltpu.VMEM((half, n_rows * deep), jnp.bfloat16),
            pltpu.VMEM((half, weight.shape[1]), jnp.float32),
            pltpu.VMEM((half, ch), jnp.bfloat16),
            pltpu.SemaphoreType.DMA((n_rows * n_slots,)),
            pltpu.SemaphoreType.DMA,
        ],
        flops=2 * half * (weight.size + w_sides.size),
        moved=2 * weight.size,
        far_out=(1,),
    )


def own_second(got, weight):
    n_rows, _, n_frames, blocks, n_slots, _, ch = got.shape
    half = blocks * n_slots * CB
    deep = n_frames * ch

    def body(got_ref, w_ref, o_ref, next_ref, lhs, acc, keep_sems):
        keeps = []
        for r in range(n_rows):
            for s in range(n_slots):
                src = got_ref.at[r, 1, n_frames - 1, :, s]
                n = r * n_slots + s
                keeps.append(pltpu.make_async_copy(src, next_ref.at[s, 0, r], keep_sems.at[n]))
                keeps[-1].start()
        own_rows(got_ref, 1, lhs)
        acc[...] = dot(lhs[...], w_ref[...])
        give_rows(acc, ch, o_ref, None)
        for c in keeps:
            c.wait()

    return call(
        body,
        [
            sums_shape(blocks, n_slots, n_rows, ch),
            jax.ShapeDtypeStruct((n_slots, 2, n_rows, blocks, CB, ch), jnp.bfloat16),
        ],
        (got, weight),
        scratch=[
            pltpu.VMEM((half, n_rows * deep), jnp.bfloat16),
            pltpu.VMEM((half, weight.shape[1]), jnp.float32),
            pltpu.SemaphoreType.DMA((n_rows * n_slots,)),
        ],
        flops=2 * half * weight.size,
        moved=2 * weight.size,
        far_out=(1,),
    )


def side_sums(edge_ref, k, side_ref, w, lhs):
    n_frames, blocks, n_slots, _, ch = side_ref.shape
    for s in range(n_slots):
        for f in range(n_frames):
            value = masked(edge_ref, k, s, side_ref[f, :, s])
            lhs[:, s, :, f * ch : (f + 1) * ch] = value
    half = blocks * n_slots * CB
    return folded(dot(lhs[...].reshape(half, n_frames * ch), w), ch, True)


def second_activation(near, far, w_sides, sums, bias, gain, edges):
    n_frames, blocks, n_slots, _, ch = far.shape
    n_rows, n_cols, deep = sums.shape[0], blocks * CB, n_frames * ch

    def body(edge_ref, near_ref, far_ref, w_ref, z_ref, b_ref, g_ref, o_ref, near_out, far_out, lhs):
        for (side, y), out in zip(beside(edge_ref, near_ref, far_ref), (near_out, far_out)):
            total = side_sums(edge_ref, y, side, w_ref[y], lhs) + z_ref[y] + b_ref[...]
            for s in range(n_slots):
                value = activated(total[:, s].reshape(n_cols, ch), g_ref[...]).astype(jnp.bfloat16)
                o_ref[s, y] = value
                out[s] = value

    row = jax.ShapeDtypeStruct((n_slots, n_cols, ch), jnp.bfloat16)
    return call(
        body,
        [jax.ShapeDtypeStruct((n_slots, n_rows, n_cols, ch), jnp.bfloat16), row, row],
        (near, far, w_sides, sums, bias, gain),
        scalars=(edges,),
        scratch=[
            pltpu.VMEM((blocks, n_slots, CB, deep), jnp.bfloat16),
        ],
        flops=2 * n_slots * n_cols * w_sides.size,
        moved=2 * w_sides.size,
    )


def before_sides(near, far, act, w_sides, w_act, sums, kept, edges):
    n_frames, blocks, n_slots, _, ch = far.shape
    n_rows, n_cols, deep = sums.shape[0], blocks * CB, n_frames * ch

    def body(edge_ref, near_ref, far_ref, act_ref, tiles_ref, w_ref, wa_ref, z_ref, kept_ref, o_ref, next_ref, lhs, lhs2, sem):
        copy = pltpu.make_async_copy(tiles_ref, next_ref.at[:, 1], sem)
        copy.start()
        add_own(act_ref, wa_ref, lhs2, o_ref, z_ref)
        for side, y in beside(edge_ref, near_ref, far_ref):
            o_ref[y] += side_sums(edge_ref, y, side, w_ref[y], lhs)
        copy.wait()

    return call(
        body,
        [jax.ShapeDtypeStruct(sums.shape, jnp.float32), jax.ShapeDtypeStruct(kept.shape, kept.dtype)],
        (near, far, act, act.reshape(n_slots, n_rows, blocks, CB, ch), w_sides, w_act, sums, kept),
        scalars=(edges,),
        scratch=[
            pltpu.VMEM((blocks, n_slots, CB, deep), jnp.bfloat16),
            pltpu.VMEM((n_slots * n_cols, n_rows * ch), jnp.bfloat16),
            pltpu.SemaphoreType.DMA,
        ],
        flops=2 * n_slots * n_cols * (w_sides.size + w_act.size),
        moved=2 * (w_sides.size + w_act.size),
        far=(7,),
        far_out=(1,),
        aliases={8: 1},
    )


def last_part(near, far, w_sides, sums, bias, frame, edges):
    n_slots, n_rows, n_cols, ch = frame.shape

    def body(edge_ref, near_ref, far_ref, w_ref, z_ref, b_ref, f_ref, o_ref, lhs):
        for side, y in beside(edge_ref, near_ref, far_ref):
            for s in range(n_slots):
                lhs[s * n_cols : (s + 1) * n_cols] = masked(edge_ref, y, s, side[s])
            total = folded(dot(lhs[...], w_ref[y]), ch, False)
            for s in range(n_slots):
                value = (total[s] + z_ref[y, :, s] + b_ref[...]).reshape(n_cols, ch)
                o_ref[s, y] = (value + f_ref[s, y].astype(jnp.float32)).astype(jnp.bfloat16)

    return call(
        body,
        [jax.ShapeDtypeStruct(frame.shape, jnp.bfloat16)],
        (near, far, w_sides, sums, bias, frame),
        scalars=(edges,),
        scratch=[pltpu.VMEM((n_slots * n_cols, ch), jnp.bfloat16)],
        flops=2 * n_slots * n_cols * w_sides.size,
        moved=2 * w_sides.size,
    )[0]


def local(
    frame_in,
    cache_first,
    cache_second,
    gain_first,
    gain_second,
    conv_first,
    conv_second,
    bias_first,
    bias_second,
    old_slot,
    new_slot,
    old_shift,
    new_shift,
    frame_count,
):
    n_slots, n_rows, n_cols, ch = frame_in.shape
    n_groups = lax.axis_size("stream")
    n_tiles = lax.axis_size("tile")
    my_group = lax.axis_index("stream")
    my_tile = lax.axis_index("tile")
    n_flight = old_slot.shape[0]
    blocks = n_cols // CB
    slot_ids = jnp.arange(n_flight, dtype=jnp.int32)
    held_new = new_slot[None, :] == slot_ids[:, None]
    source = lookup(held_new, old_slot)
    shift_after = lookup(held_new, new_shift)
    rotation = (shift_after - lookup(held_new, old_shift)) % n_tiles
    frames_done = lookup(held_new, frame_count)
    my_piece = my_group * n_tiles + my_tile
    my_frame = (my_piece // blocks) % 2
    keep = (frames_done >= 2 - my_frame).astype(jnp.int32)
    start = my_group * n_slots
    my_number = lax.dynamic_slice_in_dim((my_tile - shift_after) % n_tiles, start, n_slots)

    odd = my_tile % 2
    edges = jnp.stack(
        [my_number != 0, my_number != n_tiles - 1, jnp.broadcast_to(odd == 1, my_number.shape)]
    ).astype(jnp.int32)

    def swap_near(row):
        return lax.ppermute(row, "tile", [(i, i ^ 1) for i in range(n_tiles)])

    def swap_far(row):
        return lax.ppermute(
            row, "tile", [(i, (i + 2 * (i % 2) - 1) % n_tiles) for i in range(n_tiles)]
        )

    sent = pack(cache_first, cache_second).reshape(n_groups * n_tiles, n_slots, CB, ch)
    held = lax.all_to_all(sent, BOTH, 0, 0, tiled=True)

    act_own_1, act_sides_1 = spread(conv_first, False)
    act_first, near, far = first_activation(frame_in, gain_first[None], edges)
    act_near, act_far = swap_near(near), swap_far(far)
    sums_1 = current_part(act_first, act_own_1)
    own_1, sides_1 = spread(conv_first, True)
    own_2, sides_2 = spread(conv_second, True)
    act_own_2, act_sides_2 = spread(conv_second, False)
    (
        held, sums_1, act_near, act_far, act_sides_1, own_1, sides_1, own_2, sides_2, act_own_2, act_sides_2,
    ) = lax.optimization_barrier((
        held, sums_1, act_near, act_far, act_sides_1, own_1, sides_1, own_2, sides_2, act_own_2, act_sides_2,
    ))

    moved = permute(held.reshape(n_groups, n_tiles, n_slots, CB, ch), source, rotation, keep)
    got = lax.all_to_all(
        moved.reshape(n_groups * n_tiles, n_slots, CB, ch), BOTH, 0, 0, tiled=True
    )
    got = got.reshape(n_rows, 2, 2, blocks, n_slots, CB, ch)

    def picked(cache, row):
        return lax.dynamic_index_in_dim(got[:, cache], row, 0, keepdims=False)

    near_1, far_1 = swap_near(picked(0, 1 - odd)), swap_far(picked(0, odd))
    near_2, far_rows = swap_near(picked(1, 1 - odd)), picked(1, odd)
    act_tiles = act_first.reshape(n_slots, n_rows, blocks, CB, ch)
    sums_1, next_first = own_first(
        got, own_1, sums_1, act_tiles, act_near, act_far, act_sides_1, edges
    )
    far_rows, sums_1 = lax.optimization_barrier((far_rows, sums_1))
    far_2 = swap_far(far_rows)
    act_second, near, far = second_activation(
        near_1, far_1, sides_1, sums_1, bias_first[None], gain_second[None], edges
    )
    act_near, act_far = swap_near(near), swap_far(far)
    got_later, act_later = lax.optimization_barrier((got, act_second))
    sums_2, kept = own_second(got_later, own_2)
    sums_2, next_second = before_sides(
        near_2, far_2, act_later, sides_2, act_own_2, sums_2, kept, edges
    )
    mixed_frame = last_part(
        act_near, act_far, act_sides_2, sums_2, bias_second[None], frame_in, edges
    )
    whole = (n_slots, 2, n_rows, n_cols, ch)
    return (mixed_frame, next_first.reshape(whole), next_second.reshape(whole))


def solution(mesh):
    frame = P("stream", "tile", None, None)
    cache = P("stream", None, "tile", None, None)
    return jax.shard_map(
        local,
        mesh=mesh,
        in_specs=(frame, cache, cache) + (P(),) * 11,
        out_specs=(frame, cache, cache),
        check_vma=False,
    )
```

```python
import jax
import jax.numpy as jnp
from jax import lax
from jax.experimental import pallas as pl
from jax.experimental.pallas import tpu as pltpu
from jax.sharding import PartitionSpec as P

BOTH = ("stream", "tile")
CB = 8


def lookup(held_table, values):
    return jnp.sum(jnp.where(held_table, values[None, :], 0), axis=1)


def pack(first, second):
    n_slots, n_frames, n_rows, n_cols, ch = first.shape
    blocks = n_cols // CB
    parts = n_rows * 2 * n_frames

    def body(a_ref, b_ref, o_ref, held, in_sems, out_sems):
        whole = []
        for r in range(n_rows):
            for k, ref in enumerate((a_ref, b_ref)):
                for f in range(n_frames):
                    whole.append((r, k, f, ref))
        loads = []
        for p, (r, k, f, ref) in enumerate(whole):
            for s in range(n_slots):
                n = p * n_slots + s
                loads.append(
                    pltpu.make_async_copy(ref.at[s, f, r], held.at[r, k, f, :, s], in_sems.at[n])
                )
                loads[-1].start()
        stores = []
        for p, (r, k, f, _) in enumerate(whole):
            for s in range(n_slots):
                loads[p * n_slots + s].wait()
            stores.append(pltpu.make_async_copy(held.at[r, k, f], o_ref.at[r, k, f], out_sems.at[p]))
            stores[-1].start()
        for c in stores:
            c.wait()

    shape = (n_rows, 2, n_frames, blocks, n_slots, CB, ch)
    tiles = (n_slots, n_frames, n_rows, blocks, CB, ch)
    far = pl.BlockSpec(memory_space=pl.ANY)
    return pl.pallas_call(
        body,
        in_specs=[far, far],
        out_specs=far,
        out_shape=jax.ShapeDtypeStruct(shape, first.dtype),
        scratch_shapes=[
            pltpu.VMEM(shape, first.dtype),
            pltpu.SemaphoreType.DMA((parts * n_slots,)),
            pltpu.SemaphoreType.DMA((parts,)),
        ],
        compiler_params=pltpu.CompilerParams(vmem_limit_bytes=58 << 20),
    )(first.reshape(tiles), second.reshape(tiles))


def permute(held, source, rotation, keep):
    n_groups, n_tiles, n_slots, cols, ch = held.shape

    def body(source_ref, rotation_ref, keep_ref, i_ref, o_ref):
        def stream(n, _):
            by = rotation_ref[n]
            old = source_ref[n]
            to, slot = lax.div(n, n_slots), lax.rem(n, n_slots)
            of, place = lax.div(old, n_slots), lax.rem(old, n_slots)

            @pl.when(keep_ref[n] != 0)
            def _():
                for t in range(n_tiles):
                    at = lax.rem(t + n_tiles - by, n_tiles)
                    o_ref[to, t, slot] = i_ref[of, at, place]

            @pl.when(keep_ref[n] == 0)
            def _():
                o_ref[to, :, slot] = jnp.zeros((n_tiles, cols, ch), o_ref.dtype)

            return 0

        lax.fori_loop(0, n_groups * n_slots, stream, 0)

    smem, vmem = pl.BlockSpec(memory_space=pltpu.SMEM), pl.BlockSpec(memory_space=pltpu.VMEM)
    return pl.pallas_call(
        body,
        in_specs=[smem, smem, smem, vmem],
        out_specs=vmem,
        out_shape=jax.ShapeDtypeStruct(held.shape, held.dtype),
        compiler_params=pltpu.CompilerParams(vmem_limit_bytes=16 << 20),
    )(source, rotation, keep, held)


VMEM_LIMIT = 13 << 20


def call(body, out_shape, operands, scalars=(), scratch=(), flops=0, moved=0, far=(), far_out=(), aliases=None, limit=VMEM_LIMIT):
    in_specs = [pl.BlockSpec(memory_space=pltpu.SMEM) for _ in scalars]
    for k, _ in enumerate(operands):
        in_specs.append(pl.BlockSpec(memory_space=pl.ANY if k in far else pltpu.VMEM))
    out_specs = []
    for k, _ in enumerate(out_shape):
        out_specs.append(pl.BlockSpec(memory_space=pl.ANY if k in far_out else pltpu.VMEM))
    return pl.pallas_call(
        body,
        in_specs=in_specs,
        out_specs=out_specs,
        out_shape=list(out_shape),
        scratch_shapes=list(scratch),
        input_output_aliases=aliases or {},
        cost_estimate=pl.CostEstimate(flops=flops, bytes_accessed=moved, transcendentals=0),
        compiler_params=pltpu.CompilerParams(vmem_limit_bytes=limit),
    )(*scalars, *operands)


def spread(weight, past):
    n_t, n_y, n_x, ci, co = weight.shape
    wide = n_x * co
    times = n_t - 1 if past else 1

    def body(w_ref, own_ref, side_ref):
        dy = pl.program_id(0)

        def side(y):
            for x in range(n_x):
                for t in range(times):
                    side_ref[y, t * ci : (t + 1) * ci, x * co : (x + 1) * co] = w_ref[t, 0, x]

        def own(row, y):
            for x in range(n_x):
                for t in range(times):
                    lo = (row * times + t) * ci
                    at = y * wide + x * co
                    own_ref[lo : lo + ci, at : at + co] = w_ref[t, 0, x]

        @pl.when(dy == 0)
        def _():
            side(0)
            own(0, 1)

        @pl.when(dy == 1)
        def _():
            own(0, 0)
            own(1, 1)

        @pl.when(dy == 2)
        def _():
            side(1)
            own(1, 0)

    shapes = [(2 * times * ci, 2 * wide), (2, times * ci, wide)]
    first = 0 if past else n_t - 1
    return pl.pallas_call(
        body,
        grid=(n_y,),
        in_specs=[pl.BlockSpec((times, 1, n_x, ci, co), lambda y: (first, y, 0, 0, 0))],
        out_specs=[pl.BlockSpec(memory_space=pltpu.VMEM) for _ in shapes],
        out_shape=[jax.ShapeDtypeStruct(shape, weight.dtype) for shape in shapes],
        cost_estimate=pl.CostEstimate(flops=0, bytes_accessed=4 * weight.size, transcendentals=0),
        compiler_params=pltpu.CompilerParams(vmem_limit_bytes=16 << 20),
    )(weight)


def activated(values, gain):
    u = values * lax.rsqrt(jnp.mean(values * values, axis=-1, keepdims=True) + 1e-06) * gain
    return u / (1.0 + jnp.exp(-u))


def first_activation(frame, gain, edges):
    n_slots, n_rows, n_cols, ch = frame.shape

    def body(edge_ref, f_ref, g_ref, o_ref, near_ref, far_ref):
        odd = edge_ref[2, 0]
        for s in range(n_slots):
            for r in range(n_rows):
                value = activated(f_ref[s, r].astype(jnp.float32), g_ref[...]).astype(jnp.bfloat16)
                o_ref[s, r] = value

                @pl.when(odd != r)
                def _(s=s, value=value):
                    near_ref[s] = value

                @pl.when(odd == r)
                def _(s=s, value=value):
                    far_ref[s] = value

    row = jax.ShapeDtypeStruct((n_slots, n_cols, ch), jnp.bfloat16)
    return call(
        body,
        [jax.ShapeDtypeStruct(frame.shape, jnp.bfloat16), row, row],
        (frame, gain),
        scalars=(edges,),
        flops=10 * frame.size,
        moved=6 * frame.size,
    )


def beside(edge_ref, near_ref, far_ref):
    odd = edge_ref[2, 0]
    return ((near_ref, 1 - odd), (far_ref, odd))


def folded(acc, ch, cols_first):
    tiles = acc.shape[0] // CB
    n_slots = 4
    blocks = tiles // n_slots
    lead = (blocks, n_slots) if cols_first else (n_slots, blocks)
    axis = 0 if cols_first else 1

    def plane(k):
        value = acc[:, k * ch : (k + 1) * ch].reshape(tiles, CB, ch)
        return value

    at = lax.broadcasted_iota(jnp.int32, (1, 1, CB, ch), 2)
    before = pltpu.roll(plane(0), 1, 1).reshape(lead + (CB, ch))
    after = pltpu.roll(plane(2), CB - 1, 1).reshape(lead + (CB, ch))
    gap = list(lead) + [CB, ch]
    gap[axis] = 1
    gap = jnp.zeros(gap, jnp.float32)
    before_prev = jnp.concatenate([gap, lax.slice_in_dim(before, 0, blocks - 1, axis=axis)], axis)
    after_next = jnp.concatenate([lax.slice_in_dim(after, 1, blocks, axis=axis), gap], axis)
    total = plane(1).reshape(lead + (CB, ch))
    total += jnp.where(at == 0, before_prev, before)
    total += jnp.where(at == CB - 1, after_next, after)
    return total


def add_into(o_ref, y, total, cols_first, base=None):
    if cols_first:
        o_ref[y] = total if base is None else base[y] + total
        return
    for s in range(total.shape[0]):
        o_ref[y, :, s] = total[s] if base is None else base[y, :, s] + total[s]


def masked(edge_ref, k, s, value):
    return jnp.where(edge_ref[k, s] != 0, value, jnp.zeros_like(value))


def dot(a, b):
    return jnp.dot(a, b, preferred_element_type=jnp.float32)


def sums_shape(blocks, n_slots, n_rows, ch):
    return jax.ShapeDtypeStruct((n_rows, blocks, n_slots, CB, ch), jnp.float32)


def add_sides(edge_ref, pairs, w_ref, lhs, o_ref):
    for side, y in pairs:
        n_slots, n_cols, ch = side.shape
        for s in range(n_slots):
            lhs[s * n_cols : (s + 1) * n_cols] = masked(edge_ref, y, s, side[s])
        add_into(o_ref, y, folded(dot(lhs[...], w_ref[y]), ch, False), False, o_ref)


def add_own(act_ref, w_ref, lhs, o_ref, base):
    n_slots, n_rows, n_cols, ch = act_ref.shape
    for s in range(n_slots):
        for r in range(n_rows):
            lhs[s * n_cols : (s + 1) * n_cols, r * ch : (r + 1) * ch] = act_ref[s, r]
    both = dot(lhs[...], w_ref[...])
    wide = both.shape[1] // 2
    for y in range(n_rows):
        add_into(o_ref, y, folded(both[:, y * wide : (y + 1) * wide], ch, False), False, base)


def current_part(act, near, far, w_own, w_sides, edges):
    n_slots, n_rows, n_cols, ch = act.shape
    half = n_slots * n_cols

    def body(edge_ref, act_ref, near_ref, far_ref, wo_ref, ws_ref, o_ref, lhs, side):
        add_own(act_ref, wo_ref, lhs, o_ref, None)
        add_sides(edge_ref, beside(edge_ref, near_ref, far_ref), ws_ref, side, o_ref)

    return call(
        body,
        [sums_shape(n_cols // CB, n_slots, n_rows, ch)],
        (act, near, far, w_own, w_sides),
        scalars=(edges,),
        scratch=[
            pltpu.VMEM((half, n_rows * ch), jnp.bfloat16),
            pltpu.VMEM((half, ch), jnp.bfloat16),
        ],
        flops=2 * half * (w_own.size + w_sides.size),
        moved=2 * w_own.size + 8 * act.size,
    )[0]


def own_rows(got_ref, k, lhs):
    n_rows, _, n_frames, _, _, _, ch = got_ref.shape
    for r in range(n_rows):
        for f in range(n_frames):
            lo = (r * n_frames + f) * ch
            lhs[:, lo : lo + ch] = got_ref[r, k, f].reshape(lhs.shape[0], ch)


def give_rows(acc, ch, o_ref, base):
    n_rows = o_ref.shape[0]
    wide = acc.shape[1] // n_rows
    for y in range(n_rows):
        add_into(o_ref, y, folded(acc[:, y * wide : (y + 1) * wide], ch, True), True, base)


def own_first(got, weight, sums, act):
    n_rows, _, n_frames, blocks, n_slots, _, ch = got.shape
    half = blocks * n_slots * CB
    deep = n_frames * ch

    def body(got_ref, w_ref, z_ref, act_ref, o_ref, next_ref, lhs, acc, keep_sems, act_sem):
        keeps = [pltpu.make_async_copy(act_ref, next_ref.at[:, 1], act_sem)]
        for r in range(n_rows):
            for s in range(n_slots):
                src = got_ref.at[r, 0, n_frames - 1, :, s]
                n = r * n_slots + s
                keeps.append(pltpu.make_async_copy(src, next_ref.at[s, 0, r], keep_sems.at[n]))
        for c in keeps:
            c.start()
        own_rows(got_ref, 0, lhs)
        acc[...] = dot(lhs[...], w_ref[...])
        give_rows(acc, ch, o_ref, z_ref)
        for c in keeps:
            c.wait()

    return call(
        body,
        [
            sums_shape(blocks, n_slots, n_rows, ch),
            jax.ShapeDtypeStruct((n_slots, 2, n_rows, blocks, CB, ch), jnp.bfloat16),
        ],
        (got, weight, sums, act),
        scratch=[
            pltpu.VMEM((half, n_rows * deep), jnp.bfloat16),
            pltpu.VMEM((half, weight.shape[1]), jnp.float32),
            pltpu.SemaphoreType.DMA((n_rows * n_slots,)),
            pltpu.SemaphoreType.DMA,
        ],
        flops=2 * half * weight.size,
        moved=2 * weight.size,
        far_out=(1,),
    )


def own_second(got, weight):
    n_rows, _, n_frames, blocks, n_slots, _, ch = got.shape
    half = blocks * n_slots * CB
    deep = n_frames * ch

    def body(got_ref, w_ref, o_ref, next_ref, lhs, acc, keep_sems):
        keeps = []
        for r in range(n_rows):
            for s in range(n_slots):
                src = got_ref.at[r, 1, n_frames - 1, :, s]
                n = r * n_slots + s
                keeps.append(pltpu.make_async_copy(src, next_ref.at[s, 0, r], keep_sems.at[n]))
                keeps[-1].start()
        own_rows(got_ref, 1, lhs)
        acc[...] = dot(lhs[...], w_ref[...])
        give_rows(acc, ch, o_ref, None)
        for c in keeps:
            c.wait()

    return call(
        body,
        [
            sums_shape(blocks, n_slots, n_rows, ch),
            jax.ShapeDtypeStruct((n_slots, 2, n_rows, blocks, CB, ch), jnp.bfloat16),
        ],
        (got, weight),
        scratch=[
            pltpu.VMEM((half, n_rows * deep), jnp.bfloat16),
            pltpu.VMEM((half, weight.shape[1]), jnp.float32),
            pltpu.SemaphoreType.DMA((n_rows * n_slots,)),
        ],
        flops=half,
        moved=half,
        far_out=(1,),
    )


def side_sums(edge_ref, k, side_ref, w, lhs):
    n_frames, blocks, n_slots, _, ch = side_ref.shape
    for s in range(n_slots):
        for f in range(n_frames):
            value = masked(edge_ref, k, s, side_ref[f, :, s])
            lhs[:, s, :, f * ch : (f + 1) * ch] = value
    half = blocks * n_slots * CB
    return folded(dot(lhs[...].reshape(half, n_frames * ch), w), ch, True)


def second_activation(near, far, w_sides, sums, bias, gain, edges):
    n_frames, blocks, n_slots, _, ch = far.shape
    n_rows, n_cols, deep = sums.shape[0], blocks * CB, n_frames * ch

    def body(edge_ref, near_ref, far_ref, w_ref, z_ref, b_ref, g_ref, o_ref, near_out, far_out, lhs):
        for (side, y), out in zip(beside(edge_ref, near_ref, far_ref), (near_out, far_out)):
            total = side_sums(edge_ref, y, side, w_ref[y], lhs) + z_ref[y] + b_ref[...]
            for s in range(n_slots):
                value = activated(total[:, s].reshape(n_cols, ch), g_ref[...]).astype(jnp.bfloat16)
                o_ref[s, y] = value
                out[s] = value

    row = jax.ShapeDtypeStruct((n_slots, n_cols, ch), jnp.bfloat16)
    return call(
        body,
        [jax.ShapeDtypeStruct((n_slots, n_rows, n_cols, ch), jnp.bfloat16), row, row],
        (near, far, w_sides, sums, bias, gain),
        scalars=(edges,),
        scratch=[
            pltpu.VMEM((blocks, n_slots, CB, deep), jnp.bfloat16),
        ],
        flops=2 * n_slots * n_cols * w_sides.size,
        moved=2 * w_sides.size,
    )


def act_part(act, near, w_own, w_sides, sums, kept, edges):
    n_slots, n_rows, n_cols, ch = act.shape
    half = n_slots * n_cols
    tiles = act.reshape(n_slots, n_rows, n_cols // CB, CB, ch)

    def body(edge_ref, act_ref, tiles_ref, near_ref, wo_ref, ws_ref, z_ref, kept_ref, o_ref, next_ref, lhs, side, sem):
        copy = pltpu.make_async_copy(tiles_ref, next_ref.at[:, 1], sem)
        copy.start()
        add_own(act_ref, wo_ref, lhs, o_ref, z_ref)
        add_sides(edge_ref, beside(edge_ref, near_ref, None)[:1], ws_ref, side, o_ref)
        copy.wait()

    return call(
        body,
        [jax.ShapeDtypeStruct(sums.shape, jnp.float32), jax.ShapeDtypeStruct(kept.shape, kept.dtype)],
        (act, tiles, near, w_own, w_sides, sums, kept),
        scalars=(edges,),
        scratch=[
            pltpu.VMEM((half, n_rows * ch), jnp.bfloat16),
            pltpu.VMEM((half, ch), jnp.bfloat16),
            pltpu.SemaphoreType.DMA,
        ],
        flops=2 * half * w_own.size,
        moved=2 * (w_sides.size + w_own.size),
        far=(6,),
        far_out=(1,),
        aliases={7: 1},
    )


def cached_sides(near, far, w_sides, sums, edges):
    n_frames, blocks, n_slots, _, ch = far.shape
    deep = n_frames * ch

    def body(edge_ref, near_ref, far_ref, w_ref, z_ref, o_ref, lhs):
        for side, y in beside(edge_ref, near_ref, far_ref):
            o_ref[y] = z_ref[y] + side_sums(edge_ref, y, side, w_ref[y], lhs)

    return call(
        body,
        [jax.ShapeDtypeStruct(sums.shape, jnp.float32)],
        (near, far, w_sides, sums),
        scalars=(edges,),
        scratch=[pltpu.VMEM((blocks, n_slots, CB, deep), jnp.bfloat16)],
        flops=2 * blocks * n_slots * CB * w_sides.size,
        moved=2 * w_sides.size,
    )[0]


def last_part(far, w_sides, sums, bias, frame, edges):
    n_slots, n_rows, n_cols, ch = frame.shape

    def body(edge_ref, far_ref, w_ref, z_ref, b_ref, f_ref, o_ref, lhs):
        def give(y, total):
            for s in range(n_slots):
                value = z_ref[y, :, s] + b_ref[...]
                if total is not None:
                    value += total[s]
                value = value.reshape(n_cols, ch) + f_ref[s, y].astype(jnp.float32)
                o_ref[s, y] = value.astype(jnp.bfloat16)

        (_, done), (side, y) = beside(edge_ref, None, far_ref)
        for s in range(n_slots):
            lhs[s * n_cols : (s + 1) * n_cols] = masked(edge_ref, y, s, side[s])
        give(done, None)
        give(y, folded(dot(lhs[...], w_ref[y]), ch, False))

    return call(
        body,
        [jax.ShapeDtypeStruct(frame.shape, jnp.bfloat16)],
        (far, w_sides, sums, bias, frame),
        scalars=(edges,),
        scratch=[pltpu.VMEM((n_slots * n_cols, ch), jnp.bfloat16)],
        flops=n_slots * n_cols * w_sides.size,
        moved=2 * w_sides.size,
    )[0]


def local(
    frame_in,
    cache_first,
    cache_second,
    gain_first,
    gain_second,
    conv_first,
    conv_second,
    bias_first,
    bias_second,
    old_slot,
    new_slot,
    old_shift,
    new_shift,
    frame_count,
):
    n_slots, n_rows, n_cols, ch = frame_in.shape
    n_groups = lax.axis_size("stream")
    n_tiles = lax.axis_size("tile")
    my_group = lax.axis_index("stream")
    my_tile = lax.axis_index("tile")
    n_flight = old_slot.shape[0]
    blocks = n_cols // CB
    slot_ids = jnp.arange(n_flight, dtype=jnp.int32)
    held_new = new_slot[None, :] == slot_ids[:, None]
    source = lookup(held_new, old_slot)
    shift_after = lookup(held_new, new_shift)
    rotation = (shift_after - lookup(held_new, old_shift)) % n_tiles
    frames_done = lookup(held_new, frame_count)
    my_piece = my_group * n_tiles + my_tile
    my_frame = (my_piece // blocks) % 2
    keep = (frames_done >= 2 - my_frame).astype(jnp.int32)
    start = my_group * n_slots
    my_number = lax.dynamic_slice_in_dim((my_tile - shift_after) % n_tiles, start, n_slots)

    odd = my_tile % 2
    edges = jnp.stack(
        [my_number != 0, my_number != n_tiles - 1, jnp.broadcast_to(odd == 1, my_number.shape)]
    ).astype(jnp.int32)

    def swap_near(row):
        return lax.ppermute(row, "tile", [(i, i ^ 1) for i in range(n_tiles)])

    def swap_far(row):
        return lax.ppermute(
            row, "tile", [(i, (i + 2 * (i % 2) - 1) % n_tiles) for i in range(n_tiles)]
        )

    sent = pack(cache_first, cache_second).reshape(n_groups * n_tiles, n_slots, CB, ch)
    held = lax.all_to_all(sent, BOTH, 0, 0, tiled=True)

    act_own_1, act_sides_1 = spread(conv_first, False)
    act_first, near, far = first_activation(frame_in, gain_first[None], edges)
    act_near, act_far = swap_near(near), swap_far(far)
    held, act_first, act_near, act_far, act_own_1, act_sides_1 = lax.optimization_barrier(
        (held, act_first, act_near, act_far, act_own_1, act_sides_1)
    )

    moved = permute(held.reshape(n_groups, n_tiles, n_slots, CB, ch), source, rotation, keep)
    moved, act_later = lax.optimization_barrier((moved, act_first))
    got = lax.all_to_all(
        moved.reshape(n_groups * n_tiles, n_slots, CB, ch), BOTH, 0, 0, tiled=True
    )
    sums_1 = current_part(act_later, act_near, act_far, act_own_1, act_sides_1, edges)
    sums_1, conv_first, conv_second = lax.optimization_barrier((sums_1, conv_first, conv_second))
    act_own_2, act_sides_2 = spread(conv_second, False)
    own_1, sides_1 = spread(conv_first, True)
    own_2, sides_2 = spread(conv_second, True)
    got, sums_1, own_1, own_2, sides_1, sides_2, act_own_2, act_sides_2 = lax.optimization_barrier(
        (got, sums_1, own_1, own_2, sides_1, sides_2, act_own_2, act_sides_2)
    )
    got = got.reshape(n_rows, 2, 2, blocks, n_slots, CB, ch)

    def picked(cache, row):
        return lax.dynamic_index_in_dim(got[:, cache], row, 0, keepdims=False)

    near_1, far_1 = swap_near(picked(0, 1 - odd)), swap_far(picked(0, odd))
    near_2, far_2 = swap_near(picked(1, 1 - odd)), swap_far(picked(1, odd))
    act_tiles = act_first.reshape(n_slots, n_rows, blocks, CB, ch)
    sums_1, next_first = own_first(got, own_1, sums_1, act_tiles)
    got_later, sums_1 = lax.optimization_barrier((got, sums_1))
    sums_2, kept = own_second(got_later, own_2)
    sums_1, sums_2, kept = lax.optimization_barrier((sums_1, sums_2, kept))
    act_second, near, far = second_activation(
        near_1, far_1, sides_1, sums_1, bias_first[None], gain_second[None], edges
    )
    act_near, act_far = swap_near(near), swap_far(far)
    sums_2, next_second = act_part(
        act_second, act_near, act_own_2, act_sides_2, sums_2, kept, edges
    )
    sums_2 = cached_sides(near_2, far_2, sides_2, sums_2, edges)
    mixed_frame = last_part(act_far, act_sides_2, sums_2, bias_second[None], frame_in, edges)
    whole = (n_slots, 2, n_rows, n_cols, ch)
    return (mixed_frame, next_first.reshape(whole), next_second.reshape(whole))


def solution(mesh):
    frame = P("stream", "tile", None, None)
    cache = P("stream", None, "tile", None, None)
    return jax.shard_map(
        local,
        mesh=mesh,
        in_specs=(frame, cache, cache) + (P(),) * 11,
        out_specs=(frame, cache, cache),
        check_vma=False,
    )
```

```python
import jax
import jax.numpy as jnp
from jax import lax
from jax.experimental import pallas as pl
from jax.experimental.pallas import tpu as pltpu
from jax.sharding import PartitionSpec as P

BOTH = ("stream", "tile")
CB = 8


def lookup(held_table, values):
    return jnp.sum(jnp.where(held_table, values[None, :], 0), axis=1)


def pack(first, second):
    n_slots, n_frames, n_rows, n_cols, ch = first.shape
    blocks = n_cols // CB
    parts = n_rows * 2 * n_frames

    def body(a_ref, b_ref, o_ref, held, in_sems, out_sems):
        whole = []
        for r in range(n_rows):
            for k, ref in enumerate((a_ref, b_ref)):
                for f in range(n_frames):
                    whole.append((r, k, f, ref))
        loads = []
        for p, (r, k, f, ref) in enumerate(whole):
            for s in range(n_slots):
                n = p * n_slots + s
                loads.append(
                    pltpu.make_async_copy(ref.at[s, f, r], held.at[r, k, f, :, s], in_sems.at[n])
                )
                loads[-1].start()
        stores = []
        for p, (r, k, f, _) in enumerate(whole):
            for s in range(n_slots):
                loads[p * n_slots + s].wait()
            stores.append(pltpu.make_async_copy(held.at[r, k, f], o_ref.at[r, k, f], out_sems.at[p]))
            stores[-1].start()
        for c in stores:
            c.wait()

    shape = (n_rows, 2, n_frames, blocks, n_slots, CB, ch)
    tiles = (n_slots, n_frames, n_rows, blocks, CB, ch)
    far = pl.BlockSpec(memory_space=pl.ANY)
    return pl.pallas_call(
        body,
        in_specs=[far, far],
        out_specs=far,
        out_shape=jax.ShapeDtypeStruct(shape, first.dtype),
        scratch_shapes=[
            pltpu.VMEM(shape, first.dtype),
            pltpu.SemaphoreType.DMA((parts * n_slots,)),
            pltpu.SemaphoreType.DMA((parts,)),
        ],
        compiler_params=pltpu.CompilerParams(vmem_limit_bytes=58 << 20),
    )(first.reshape(tiles), second.reshape(tiles))


def permute(held, source, rotation, keep):
    n_groups, n_tiles, n_slots, cols, ch = held.shape

    def body(source_ref, rotation_ref, keep_ref, i_ref, o_ref):
        def stream(n, _):
            by = rotation_ref[n]
            old = source_ref[n]
            to, slot = lax.div(n, n_slots), lax.rem(n, n_slots)
            of, place = lax.div(old, n_slots), lax.rem(old, n_slots)

            @pl.when(keep_ref[n] != 0)
            def _():
                for t in range(n_tiles):
                    at = lax.rem(t + n_tiles - by, n_tiles)
                    o_ref[to, t, slot] = i_ref[of, at, place]

            @pl.when(keep_ref[n] == 0)
            def _():
                o_ref[to, :, slot] = jnp.zeros((n_tiles, cols, ch), o_ref.dtype)

            return 0

        lax.fori_loop(0, n_groups * n_slots, stream, 0)

    smem, vmem = pl.BlockSpec(memory_space=pltpu.SMEM), pl.BlockSpec(memory_space=pltpu.VMEM)
    return pl.pallas_call(
        body,
        in_specs=[smem, smem, smem, vmem],
        out_specs=vmem,
        out_shape=jax.ShapeDtypeStruct(held.shape, held.dtype),
        compiler_params=pltpu.CompilerParams(vmem_limit_bytes=16 << 20),
    )(source, rotation, keep, held)


VMEM_LIMIT = 13 << 20


def call(body, out_shape, operands, scalars=(), scratch=(), flops=0, moved=0, far=(), far_out=(), aliases=None, limit=VMEM_LIMIT):
    in_specs = [pl.BlockSpec(memory_space=pltpu.SMEM) for _ in scalars]
    for k, _ in enumerate(operands):
        in_specs.append(pl.BlockSpec(memory_space=pl.ANY if k in far else pltpu.VMEM))
    out_specs = []
    for k, _ in enumerate(out_shape):
        out_specs.append(pl.BlockSpec(memory_space=pl.ANY if k in far_out else pltpu.VMEM))
    return pl.pallas_call(
        body,
        in_specs=in_specs,
        out_specs=out_specs,
        out_shape=list(out_shape),
        scratch_shapes=list(scratch),
        input_output_aliases=aliases or {},
        cost_estimate=pl.CostEstimate(flops=flops, bytes_accessed=moved, transcendentals=0),
        compiler_params=pltpu.CompilerParams(vmem_limit_bytes=limit),
    )(*scalars, *operands)


def spread(weight, past):
    n_t, n_y, n_x, ci, co = weight.shape
    wide = n_x * co
    times = n_t - 1 if past else 1

    def body(w_ref, own_ref, side_ref):
        dy = pl.program_id(0)

        def side(y):
            for x in range(n_x):
                for t in range(times):
                    side_ref[y, t * ci : (t + 1) * ci, x * co : (x + 1) * co] = w_ref[t, 0, x]

        def own(row, y):
            for x in range(n_x):
                for t in range(times):
                    lo = (row * times + t) * ci
                    at = y * wide + x * co
                    own_ref[lo : lo + ci, at : at + co] = w_ref[t, 0, x]

        @pl.when(dy == 0)
        def _():
            side(0)
            own(0, 1)

        @pl.when(dy == 1)
        def _():
            own(0, 0)
            own(1, 1)

        @pl.when(dy == 2)
        def _():
            side(1)
            own(1, 0)

    shapes = [(2 * times * ci, 2 * wide), (2, times * ci, wide)]
    first = 0 if past else n_t - 1
    return pl.pallas_call(
        body,
        grid=(n_y,),
        in_specs=[pl.BlockSpec((times, 1, n_x, ci, co), lambda y: (first, y, 0, 0, 0))],
        out_specs=[pl.BlockSpec(memory_space=pltpu.VMEM) for _ in shapes],
        out_shape=[jax.ShapeDtypeStruct(shape, weight.dtype) for shape in shapes],
        cost_estimate=pl.CostEstimate(flops=0, bytes_accessed=4 * weight.size, transcendentals=0),
        compiler_params=pltpu.CompilerParams(vmem_limit_bytes=16 << 20),
    )(weight)


def activated(values, gain):
    u = values * lax.rsqrt(jnp.mean(values * values, axis=-1, keepdims=True) + 1e-06) * gain
    return u / (1.0 + jnp.exp(-u))


def first_activation(frame, gain, edges):
    n_slots, n_rows, n_cols, ch = frame.shape

    def body(edge_ref, f_ref, g_ref, o_ref, near_ref, far_ref):
        odd = edge_ref[2, 0]
        for s in range(n_slots):
            for r in range(n_rows):
                value = activated(f_ref[s, r].astype(jnp.float32), g_ref[...]).astype(jnp.bfloat16)
                o_ref[s, r] = value

                @pl.when(odd != r)
                def _(s=s, value=value):
                    near_ref[s] = value

                @pl.when(odd == r)
                def _(s=s, value=value):
                    far_ref[s] = value

    row = jax.ShapeDtypeStruct((n_slots, n_cols, ch), jnp.bfloat16)
    return call(
        body,
        [jax.ShapeDtypeStruct(frame.shape, jnp.bfloat16), row, row],
        (frame, gain),
        scalars=(edges,),
        flops=10 * frame.size,
        moved=6 * frame.size,
    )


def beside(edge_ref, near_ref, far_ref):
    odd = edge_ref[2, 0]
    return ((near_ref, 1 - odd), (far_ref, odd))


def folded(acc, ch, cols_first):
    tiles = acc.shape[0] // CB
    n_slots = 4
    blocks = tiles // n_slots
    lead = (blocks, n_slots) if cols_first else (n_slots, blocks)
    axis = 0 if cols_first else 1

    def plane(k):
        value = acc[:, k * ch : (k + 1) * ch].reshape(tiles, CB, ch)
        return value

    at = lax.broadcasted_iota(jnp.int32, (1, 1, CB, ch), 2)
    before = pltpu.roll(plane(0), 1, 1).reshape(lead + (CB, ch))
    after = pltpu.roll(plane(2), CB - 1, 1).reshape(lead + (CB, ch))
    gap = list(lead) + [CB, ch]
    gap[axis] = 1
    gap = jnp.zeros(gap, jnp.float32)
    before_prev = jnp.concatenate([gap, lax.slice_in_dim(before, 0, blocks - 1, axis=axis)], axis)
    after_next = jnp.concatenate([lax.slice_in_dim(after, 1, blocks, axis=axis), gap], axis)
    total = plane(1).reshape(lead + (CB, ch))
    total += jnp.where(at == 0, before_prev, before)
    total += jnp.where(at == CB - 1, after_next, after)
    return total


def add_into(o_ref, y, total, cols_first, base=None):
    if cols_first:
        o_ref[y] = total if base is None else base[y] + total
        return
    for s in range(total.shape[0]):
        o_ref[y, :, s] = total[s] if base is None else base[y, :, s] + total[s]


def masked(edge_ref, k, s, value):
    return jnp.where(edge_ref[k, s] != 0, value, jnp.zeros_like(value))


def dot(a, b):
    return jnp.dot(a, b, preferred_element_type=jnp.float32)


def sums_shape(blocks, n_slots, n_rows, ch):
    return jax.ShapeDtypeStruct((n_rows, blocks, n_slots, CB, ch), jnp.float32)


def add_sides(edge_ref, pairs, w_ref, lhs, o_ref):
    for side, y in pairs:
        n_slots, n_cols, ch = side.shape
        for s in range(n_slots):
            lhs[s * n_cols : (s + 1) * n_cols] = masked(edge_ref, y, s, side[s])
        add_into(o_ref, y, folded(dot(lhs[...], w_ref[y]), ch, False), False, o_ref)


def add_own(act_ref, w_ref, lhs, o_ref, base):
    n_slots, n_rows, n_cols, ch = act_ref.shape
    for s in range(n_slots):
        for r in range(n_rows):
            lhs[s * n_cols : (s + 1) * n_cols, r * ch : (r + 1) * ch] = act_ref[s, r]
    both = dot(lhs[...], w_ref[...])
    wide = both.shape[1] // 2
    for y in range(n_rows):
        add_into(o_ref, y, folded(both[:, y * wide : (y + 1) * wide], ch, False), False, base)


def current_part(act, near, far, w_own, w_sides, edges):
    n_slots, n_rows, n_cols, ch = act.shape
    half = n_slots * n_cols

    def body(edge_ref, act_ref, near_ref, far_ref, wo_ref, ws_ref, o_ref, lhs, side):
        add_own(act_ref, wo_ref, lhs, o_ref, None)
        add_sides(edge_ref, beside(edge_ref, near_ref, far_ref), ws_ref, side, o_ref)

    return call(
        body,
        [sums_shape(n_cols // CB, n_slots, n_rows, ch)],
        (act, near, far, w_own, w_sides),
        scalars=(edges,),
        scratch=[
            pltpu.VMEM((half, n_rows * ch), jnp.bfloat16),
            pltpu.VMEM((half, ch), jnp.bfloat16),
        ],
        flops=2 * half * (w_own.size + w_sides.size),
        moved=2 * w_own.size + 8 * act.size,
    )[0]


def own_rows(got_ref, k, lhs):
    n_rows, _, n_frames, _, _, _, ch = got_ref.shape
    for r in range(n_rows):
        for f in range(n_frames):
            lo = (r * n_frames + f) * ch
            lhs[:, lo : lo + ch] = got_ref[r, k, f].reshape(lhs.shape[0], ch)


def give_rows(acc, ch, o_ref, base):
    n_rows = o_ref.shape[0]
    wide = acc.shape[1] // n_rows
    for y in range(n_rows):
        add_into(o_ref, y, folded(acc[:, y * wide : (y + 1) * wide], ch, True), True, base)


def own_first(got, weight, sums, act):
    n_rows, _, n_frames, blocks, n_slots, _, ch = got.shape
    half = blocks * n_slots * CB
    deep = n_frames * ch

    def body(got_ref, w_ref, z_ref, act_ref, o_ref, next_ref, lhs, acc, keep_sems, act_sem):
        keeps = [pltpu.make_async_copy(act_ref, next_ref.at[:, 1], act_sem)]
        for r in range(n_rows):
            for s in range(n_slots):
                src = got_ref.at[r, 0, n_frames - 1, :, s]
                n = r * n_slots + s
                keeps.append(pltpu.make_async_copy(src, next_ref.at[s, 0, r], keep_sems.at[n]))
        for c in keeps:
            c.start()
        own_rows(got_ref, 0, lhs)
        acc[...] = dot(lhs[...], w_ref[...])
        give_rows(acc, ch, o_ref, z_ref)
        for c in keeps:
            c.wait()

    return call(
        body,
        [
            sums_shape(blocks, n_slots, n_rows, ch),
            jax.ShapeDtypeStruct((n_slots, 2, n_rows, blocks, CB, ch), jnp.bfloat16),
        ],
        (got, weight, sums, act),
        scratch=[
            pltpu.VMEM((half, n_rows * deep), jnp.bfloat16),
            pltpu.VMEM((half, weight.shape[1]), jnp.float32),
            pltpu.SemaphoreType.DMA((n_rows * n_slots,)),
            pltpu.SemaphoreType.DMA,
        ],
        flops=2 * half * weight.size,
        moved=2 * weight.size,
        far_out=(1,),
    )


def own_second(got, weight):
    n_rows, _, n_frames, blocks, n_slots, _, ch = got.shape
    half = blocks * n_slots * CB
    deep = n_frames * ch

    def body(got_ref, w_ref, o_ref, next_ref, lhs, acc, keep_sems):
        keeps = []
        for r in range(n_rows):
            for s in range(n_slots):
                src = got_ref.at[r, 1, n_frames - 1, :, s]
                n = r * n_slots + s
                keeps.append(pltpu.make_async_copy(src, next_ref.at[s, 0, r], keep_sems.at[n]))
                keeps[-1].start()
        own_rows(got_ref, 1, lhs)
        acc[...] = dot(lhs[...], w_ref[...])
        give_rows(acc, ch, o_ref, None)
        for c in keeps:
            c.wait()

    return call(
        body,
        [
            sums_shape(blocks, n_slots, n_rows, ch),
            jax.ShapeDtypeStruct((n_slots, 2, n_rows, blocks, CB, ch), jnp.bfloat16),
        ],
        (got, weight),
        scratch=[
            pltpu.VMEM((half, n_rows * deep), jnp.bfloat16),
            pltpu.VMEM((half, weight.shape[1]), jnp.float32),
            pltpu.SemaphoreType.DMA((n_rows * n_slots,)),
        ],
        flops=2 * half * weight.size,
        moved=2 * weight.size,
        far_out=(1,),
    )


def side_sums(edge_ref, k, side_ref, w, lhs):
    n_frames, blocks, n_slots, _, ch = side_ref.shape
    for s in range(n_slots):
        for f in range(n_frames):
            value = masked(edge_ref, k, s, side_ref[f, :, s])
            lhs[:, s, :, f * ch : (f + 1) * ch] = value
    half = blocks * n_slots * CB
    return folded(dot(lhs[...].reshape(half, n_frames * ch), w), ch, True)


def second_activation(near, far, w_sides, sums, bias, gain, edges):
    n_frames, blocks, n_slots, _, ch = far.shape
    n_rows, n_cols, deep = sums.shape[0], blocks * CB, n_frames * ch

    def body(edge_ref, near_ref, far_ref, w_ref, z_ref, b_ref, g_ref, o_ref, near_out, far_out, lhs):
        for (side, y), out in zip(beside(edge_ref, near_ref, far_ref), (near_out, far_out)):
            total = side_sums(edge_ref, y, side, w_ref[y], lhs) + z_ref[y] + b_ref[...]
            for s in range(n_slots):
                value = activated(total[:, s].reshape(n_cols, ch), g_ref[...]).astype(jnp.bfloat16)
                o_ref[s, y] = value
                out[s] = value

    row = jax.ShapeDtypeStruct((n_slots, n_cols, ch), jnp.bfloat16)
    return call(
        body,
        [jax.ShapeDtypeStruct((n_slots, n_rows, n_cols, ch), jnp.bfloat16), row, row],
        (near, far, w_sides, sums, bias, gain),
        scalars=(edges,),
        scratch=[
            pltpu.VMEM((blocks, n_slots, CB, deep), jnp.bfloat16),
        ],
        flops=2 * n_slots * n_cols * w_sides.size,
        moved=2 * w_sides.size,
    )


def act_part(act, near, w_own, w_sides, sums, kept, edges):
    n_slots, n_rows, n_cols, ch = act.shape
    half = n_slots * n_cols
    tiles = act.reshape(n_slots, n_rows, n_cols // CB, CB, ch)

    def body(edge_ref, act_ref, tiles_ref, near_ref, wo_ref, ws_ref, z_ref, kept_ref, o_ref, next_ref, lhs, side, sem):
        copy = pltpu.make_async_copy(tiles_ref, next_ref.at[:, 1], sem)
        copy.start()
        add_own(act_ref, wo_ref, lhs, o_ref, z_ref)
        add_sides(edge_ref, beside(edge_ref, near_ref, None)[:1], ws_ref, side, o_ref)
        copy.wait()

    return call(
        body,
        [jax.ShapeDtypeStruct(sums.shape, jnp.float32), jax.ShapeDtypeStruct(kept.shape, kept.dtype)],
        (act, tiles, near, w_own, w_sides, sums, kept),
        scalars=(edges,),
        scratch=[
            pltpu.VMEM((half, n_rows * ch), jnp.bfloat16),
            pltpu.VMEM((half, ch), jnp.bfloat16),
            pltpu.SemaphoreType.DMA,
        ],
        flops=2 * half * w_own.size,
        moved=2 * (w_sides.size + w_own.size),
        far=(6,),
        far_out=(1,),
        aliases={7: 1},
    )


def cached_sides(near, far, w_sides, sums, edges):
    n_frames, blocks, n_slots, _, ch = far.shape
    deep = n_frames * ch

    def body(edge_ref, near_ref, far_ref, w_ref, z_ref, o_ref, lhs):
        for side, y in beside(edge_ref, near_ref, far_ref):
            o_ref[y] = z_ref[y] + side_sums(edge_ref, y, side, w_ref[y], lhs)

    return call(
        body,
        [jax.ShapeDtypeStruct(sums.shape, jnp.float32)],
        (near, far, w_sides, sums),
        scalars=(edges,),
        scratch=[pltpu.VMEM((blocks, n_slots, CB, deep), jnp.bfloat16)],
        flops=2 * blocks * n_slots * CB * w_sides.size,
        moved=2 * w_sides.size,
    )[0]


def last_part(far, w_sides, sums, bias, frame, edges):
    n_slots, n_rows, n_cols, ch = frame.shape

    def body(edge_ref, far_ref, w_ref, z_ref, b_ref, f_ref, o_ref, lhs):
        def give(y, total):
            for s in range(n_slots):
                value = z_ref[y, :, s] + b_ref[...]
                if total is not None:
                    value += total[s]
                value = value.reshape(n_cols, ch) + f_ref[s, y].astype(jnp.float32)
                o_ref[s, y] = value.astype(jnp.bfloat16)

        (_, done), (side, y) = beside(edge_ref, None, far_ref)
        for s in range(n_slots):
            lhs[s * n_cols : (s + 1) * n_cols] = masked(edge_ref, y, s, side[s])
        give(done, None)
        give(y, folded(dot(lhs[...], w_ref[y]), ch, False))

    return call(
        body,
        [jax.ShapeDtypeStruct(frame.shape, jnp.bfloat16)],
        (far, w_sides, sums, bias, frame),
        scalars=(edges,),
        scratch=[pltpu.VMEM((n_slots * n_cols, ch), jnp.bfloat16)],
        flops=n_slots * n_cols * w_sides.size,
        moved=2 * w_sides.size,
    )[0]


def local(
    frame_in,
    cache_first,
    cache_second,
    gain_first,
    gain_second,
    conv_first,
    conv_second,
    bias_first,
    bias_second,
    old_slot,
    new_slot,
    old_shift,
    new_shift,
    frame_count,
):
    n_slots, n_rows, n_cols, ch = frame_in.shape
    n_groups = lax.axis_size("stream")
    n_tiles = lax.axis_size("tile")
    my_group = lax.axis_index("stream")
    my_tile = lax.axis_index("tile")
    n_flight = old_slot.shape[0]
    blocks = n_cols // CB
    slot_ids = jnp.arange(n_flight, dtype=jnp.int32)
    held_new = new_slot[None, :] == slot_ids[:, None]
    source = lookup(held_new, old_slot)
    shift_after = lookup(held_new, new_shift)
    rotation = (shift_after - lookup(held_new, old_shift)) % n_tiles
    frames_done = lookup(held_new, frame_count)
    my_piece = my_group * n_tiles + my_tile
    my_frame = (my_piece // blocks) % 2
    keep = (frames_done >= 2 - my_frame).astype(jnp.int32)
    start = my_group * n_slots
    my_number = lax.dynamic_slice_in_dim((my_tile - shift_after) % n_tiles, start, n_slots)

    odd = my_tile % 2
    edges = jnp.stack(
        [my_number != 0, my_number != n_tiles - 1, jnp.broadcast_to(odd == 1, my_number.shape)]
    ).astype(jnp.int32)

    def swap_near(row):
        return lax.ppermute(row, "tile", [(i, i ^ 1) for i in range(n_tiles)])

    def swap_far(row):
        return lax.ppermute(
            row, "tile", [(i, (i + 2 * (i % 2) - 1) % n_tiles) for i in range(n_tiles)]
        )

    sent = pack(cache_first, cache_second).reshape(n_groups * n_tiles, n_slots, CB, ch)
    held = lax.all_to_all(sent, BOTH, 0, 0, tiled=True)

    act_own_1, act_sides_1 = spread(conv_first, False)
    act_first, near, far = first_activation(frame_in, gain_first[None], edges)
    act_near, act_far = swap_near(near), swap_far(far)
    held, act_first, act_near, act_far, act_own_1, act_sides_1 = lax.optimization_barrier(
        (held, act_first, act_near, act_far, act_own_1, act_sides_1)
    )

    moved = permute(held.reshape(n_groups, n_tiles, n_slots, CB, ch), source, rotation, keep)
    moved, act_later = lax.optimization_barrier((moved, act_first))
    got = lax.all_to_all(
        moved.reshape(n_groups * n_tiles, n_slots, CB, ch), BOTH, 0, 0, tiled=True
    )
    sums_1 = current_part(act_later, act_near, act_far, act_own_1, act_sides_1, edges)
    sums_1, conv_first, conv_second = lax.optimization_barrier((sums_1, conv_first, conv_second))
    act_own_2, act_sides_2 = spread(conv_second, False)
    own_1, sides_1 = spread(conv_first, True)
    own_2, sides_2 = spread(conv_second, True)
    got, sums_1, own_1, own_2, sides_1, sides_2, act_own_2, act_sides_2 = lax.optimization_barrier(
        (got, sums_1, own_1, own_2, sides_1, sides_2, act_own_2, act_sides_2)
    )
    got = got.reshape(n_rows, 2, 2, blocks, n_slots, CB, ch)

    def picked(cache, row):
        return lax.dynamic_index_in_dim(got[:, cache], row, 0, keepdims=False)

    near_1, far_1 = swap_near(picked(0, 1 - odd)), swap_far(picked(0, odd))
    near_rows, far_rows = picked(1, 1 - odd), picked(1, odd)
    act_tiles = act_first.reshape(n_slots, n_rows, blocks, CB, ch)
    sums_1, next_first = own_first(got, own_1, sums_1, act_tiles)
    near_rows, far_rows, sums_1 = lax.optimization_barrier((near_rows, far_rows, sums_1))
    near_2, far_2 = swap_near(near_rows), swap_far(far_rows)
    act_second, near, far = second_activation(
        near_1, far_1, sides_1, sums_1, bias_first[None], gain_second[None], edges
    )
    act_near, act_far = swap_near(near), swap_far(far)
    got_later, act_second = lax.optimization_barrier((got, act_second))
    sums_2, kept = own_second(got_later, own_2)
    sums_2, next_second = act_part(
        act_second, act_near, act_own_2, act_sides_2, sums_2, kept, edges
    )
    sums_2 = cached_sides(near_2, far_2, sides_2, sums_2, edges)
    mixed_frame = last_part(act_far, act_sides_2, sums_2, bias_second[None], frame_in, edges)
    whole = (n_slots, 2, n_rows, n_cols, ch)
    return (mixed_frame, next_first.reshape(whole), next_second.reshape(whole))


def solution(mesh):
    frame = P("stream", "tile", None, None)
    cache = P("stream", None, "tile", None, None)
    return jax.shard_map(
        local,
        mesh=mesh,
        in_specs=(frame, cache, cache) + (P(),) * 11,
        out_specs=(frame, cache, cache),
        check_vma=False,
    )
```

```python
import jax
import jax.numpy as jnp
from jax import lax
from jax.experimental import pallas as pl
from jax.experimental.pallas import tpu as pltpu
from jax.sharding import PartitionSpec as P

BOTH = ("stream", "tile")
CB = 8


def lookup(held_table, values):
    return jnp.sum(jnp.where(held_table, values[None, :], 0), axis=1)


def pack(first, second):
    n_slots, n_frames, n_rows, n_cols, ch = first.shape
    blocks = n_cols // CB
    parts = n_rows * 2 * n_frames

    def body(a_ref, b_ref, o_ref, held, in_sems, out_sems):
        whole = []
        for r in range(n_rows):
            for k, ref in enumerate((a_ref, b_ref)):
                for f in range(n_frames):
                    whole.append((r, k, f, ref))
        loads = []
        for p, (r, k, f, ref) in enumerate(whole):
            for s in range(n_slots):
                n = p * n_slots + s
                loads.append(
                    pltpu.make_async_copy(ref.at[s, f, r], held.at[r, k, f, :, s], in_sems.at[n])
                )
                loads[-1].start()
        stores = []
        for p, (r, k, f, _) in enumerate(whole):
            for s in range(n_slots):
                loads[p * n_slots + s].wait()
            stores.append(pltpu.make_async_copy(held.at[r, k, f], o_ref.at[r, k, f], out_sems.at[p]))
            stores[-1].start()
        for c in stores:
            c.wait()

    shape = (n_rows, 2, n_frames, blocks, n_slots, CB, ch)
    tiles = (n_slots, n_frames, n_rows, blocks, CB, ch)
    far = pl.BlockSpec(memory_space=pl.ANY)
    return pl.pallas_call(
        body,
        in_specs=[far, far],
        out_specs=far,
        out_shape=jax.ShapeDtypeStruct(shape, first.dtype),
        scratch_shapes=[
            pltpu.VMEM(shape, first.dtype),
            pltpu.SemaphoreType.DMA((parts * n_slots,)),
            pltpu.SemaphoreType.DMA((parts,)),
        ],
        compiler_params=pltpu.CompilerParams(vmem_limit_bytes=58 << 20),
    )(first.reshape(tiles), second.reshape(tiles))


def permute(held, source, rotation, keep):
    n_groups, n_tiles, n_slots, cols, ch = held.shape

    def body(source_ref, rotation_ref, keep_ref, i_ref, o_ref):
        def stream(n, _):
            by = rotation_ref[n]
            old = source_ref[n]
            to, slot = lax.div(n, n_slots), lax.rem(n, n_slots)
            of, place = lax.div(old, n_slots), lax.rem(old, n_slots)

            @pl.when(keep_ref[n] != 0)
            def _():
                for t in range(n_tiles):
                    at = lax.rem(t + n_tiles - by, n_tiles)
                    o_ref[to, t, slot] = i_ref[of, at, place]

            @pl.when(keep_ref[n] == 0)
            def _():
                o_ref[to, :, slot] = jnp.zeros((n_tiles, cols, ch), o_ref.dtype)

            return 0

        lax.fori_loop(0, n_groups * n_slots, stream, 0)

    smem, vmem = pl.BlockSpec(memory_space=pltpu.SMEM), pl.BlockSpec(memory_space=pltpu.VMEM)
    return pl.pallas_call(
        body,
        in_specs=[smem, smem, smem, vmem],
        out_specs=vmem,
        out_shape=jax.ShapeDtypeStruct(held.shape, held.dtype),
        compiler_params=pltpu.CompilerParams(vmem_limit_bytes=16 << 20),
    )(source, rotation, keep, held)


VMEM_LIMIT = 13 << 20


def call(body, out_shape, operands, scalars=(), scratch=(), flops=0, moved=0, far=(), far_out=(), aliases=None, limit=VMEM_LIMIT):
    in_specs = [pl.BlockSpec(memory_space=pltpu.SMEM) for _ in scalars]
    for k, _ in enumerate(operands):
        in_specs.append(pl.BlockSpec(memory_space=pl.ANY if k in far else pltpu.VMEM))
    out_specs = []
    for k, _ in enumerate(out_shape):
        out_specs.append(pl.BlockSpec(memory_space=pl.ANY if k in far_out else pltpu.VMEM))
    return pl.pallas_call(
        body,
        in_specs=in_specs,
        out_specs=out_specs,
        out_shape=list(out_shape),
        scratch_shapes=list(scratch),
        input_output_aliases=aliases or {},
        cost_estimate=pl.CostEstimate(flops=flops, bytes_accessed=moved, transcendentals=0),
        compiler_params=pltpu.CompilerParams(vmem_limit_bytes=limit),
    )(*scalars, *operands)


def spread(weight, past):
    n_t, n_y, n_x, ci, co = weight.shape
    wide = n_x * co
    times = n_t - 1 if past else 1

    def body(w_ref, own_ref, side_ref):
        dy = pl.program_id(0)

        def side(y):
            for x in range(n_x):
                for t in range(times):
                    side_ref[y, t * ci : (t + 1) * ci, x * co : (x + 1) * co] = w_ref[t, 0, x]

        def own(row, y):
            for x in range(n_x):
                for t in range(times):
                    lo = (row * times + t) * ci
                    at = y * wide + x * co
                    own_ref[lo : lo + ci, at : at + co] = w_ref[t, 0, x]

        @pl.when(dy == 0)
        def _():
            side(0)
            own(0, 1)

        @pl.when(dy == 1)
        def _():
            own(0, 0)
            own(1, 1)

        @pl.when(dy == 2)
        def _():
            side(1)
            own(1, 0)

    shapes = [(2 * times * ci, 2 * wide), (2, times * ci, wide)]
    first = 0 if past else n_t - 1
    return pl.pallas_call(
        body,
        grid=(n_y,),
        in_specs=[pl.BlockSpec((times, 1, n_x, ci, co), lambda y: (first, y, 0, 0, 0))],
        out_specs=[pl.BlockSpec(memory_space=pltpu.VMEM) for _ in shapes],
        out_shape=[jax.ShapeDtypeStruct(shape, weight.dtype) for shape in shapes],
        cost_estimate=pl.CostEstimate(flops=0, bytes_accessed=4 * weight.size, transcendentals=0),
        compiler_params=pltpu.CompilerParams(vmem_limit_bytes=16 << 20),
    )(weight)


def activated(values, gain):
    u = values * lax.rsqrt(jnp.mean(values * values, axis=-1, keepdims=True) + 1e-06) * gain
    return u / (1.0 + jnp.exp(-u))


def first_activation(frame, gain, edges):
    n_slots, n_rows, n_cols, ch = frame.shape

    def body(edge_ref, f_ref, g_ref, o_ref, near_ref, far_ref):
        odd = edge_ref[2, 0]
        for s in range(n_slots):
            for r in range(n_rows):
                value = activated(f_ref[s, r].astype(jnp.float32), g_ref[...]).astype(jnp.bfloat16)
                o_ref[s, r] = value

                @pl.when(odd != r)
                def _(s=s, value=value):
                    near_ref[s] = value

                @pl.when(odd == r)
                def _(s=s, value=value):
                    far_ref[s] = value

    row = jax.ShapeDtypeStruct((n_slots, n_cols, ch), jnp.bfloat16)
    return call(
        body,
        [jax.ShapeDtypeStruct(frame.shape, jnp.bfloat16), row, row],
        (frame, gain),
        scalars=(edges,),
        flops=10 * frame.size,
        moved=6 * frame.size,
    )


def beside(edge_ref, near_ref, far_ref):
    odd = edge_ref[2, 0]
    return ((near_ref, 1 - odd), (far_ref, odd))


def folded(acc, ch, cols_first):
    tiles = acc.shape[0] // CB
    n_slots = 4
    blocks = tiles // n_slots
    lead = (blocks, n_slots) if cols_first else (n_slots, blocks)
    axis = 0 if cols_first else 1

    def plane(k):
        value = acc[:, k * ch : (k + 1) * ch].reshape(tiles, CB, ch)
        return value

    at = lax.broadcasted_iota(jnp.int32, (1, 1, CB, ch), 2)
    before = pltpu.roll(plane(0), 1, 1).reshape(lead + (CB, ch))
    after = pltpu.roll(plane(2), CB - 1, 1).reshape(lead + (CB, ch))
    gap = list(lead) + [CB, ch]
    gap[axis] = 1
    gap = jnp.zeros(gap, jnp.float32)
    before_prev = jnp.concatenate([gap, lax.slice_in_dim(before, 0, blocks - 1, axis=axis)], axis)
    after_next = jnp.concatenate([lax.slice_in_dim(after, 1, blocks, axis=axis), gap], axis)
    total = plane(1).reshape(lead + (CB, ch))
    total += jnp.where(at == 0, before_prev, before)
    total += jnp.where(at == CB - 1, after_next, after)
    return total


def add_into(o_ref, y, total, cols_first, base=None):
    if cols_first:
        o_ref[y] = total if base is None else base[y] + total
        return
    for s in range(total.shape[0]):
        o_ref[y, :, s] = total[s] if base is None else base[y, :, s] + total[s]


def masked(edge_ref, k, s, value):
    return jnp.where(edge_ref[k, s] != 0, value, jnp.zeros_like(value))


def dot(a, b):
    return jnp.dot(a, b, preferred_element_type=jnp.float32)


def sums_shape(blocks, n_slots, n_rows, ch):
    return jax.ShapeDtypeStruct((n_rows, blocks, n_slots, CB, ch), jnp.float32)


def add_sides(edge_ref, pairs, w_ref, lhs, o_ref):
    for side, y in pairs:
        n_slots, n_cols, ch = side.shape
        for s in range(n_slots):
            lhs[s * n_cols : (s + 1) * n_cols] = masked(edge_ref, y, s, side[s])
        add_into(o_ref, y, folded(dot(lhs[...], w_ref[y]), ch, False), False, o_ref)


def add_own(act_ref, w_ref, lhs, o_ref, base):
    n_slots, n_rows, n_cols, ch = act_ref.shape
    for s in range(n_slots):
        for r in range(n_rows):
            lhs[s * n_cols : (s + 1) * n_cols, r * ch : (r + 1) * ch] = act_ref[s, r]
    both = dot(lhs[...], w_ref[...])
    wide = both.shape[1] // 2
    for y in range(n_rows):
        add_into(o_ref, y, folded(both[:, y * wide : (y + 1) * wide], ch, False), False, base)


def current_part(act, near, far, w_own, w_sides, edges):
    n_slots, n_rows, n_cols, ch = act.shape
    half = n_slots * n_cols

    def body(edge_ref, act_ref, near_ref, far_ref, wo_ref, ws_ref, o_ref, lhs, side):
        add_own(act_ref, wo_ref, lhs, o_ref, None)
        add_sides(edge_ref, beside(edge_ref, near_ref, far_ref), ws_ref, side, o_ref)

    return call(
        body,
        [sums_shape(n_cols // CB, n_slots, n_rows, ch)],
        (act, near, far, w_own, w_sides),
        scalars=(edges,),
        scratch=[
            pltpu.VMEM((half, n_rows * ch), jnp.bfloat16),
            pltpu.VMEM((half, ch), jnp.bfloat16),
        ],
        flops=2 * half * (w_own.size + w_sides.size),
        moved=2 * w_own.size + 8 * act.size,
    )[0]


def own_rows(got_ref, k, lhs):
    n_rows, _, n_frames, _, _, _, ch = got_ref.shape
    for r in range(n_rows):
        for f in range(n_frames):
            lo = (r * n_frames + f) * ch
            lhs[:, lo : lo + ch] = got_ref[r, k, f].reshape(lhs.shape[0], ch)


def give_rows(acc, ch, o_ref, base):
    n_rows = o_ref.shape[0]
    wide = acc.shape[1] // n_rows
    for y in range(n_rows):
        add_into(o_ref, y, folded(acc[:, y * wide : (y + 1) * wide], ch, True), True, base)


def own_first(got, weight, sums, act):
    n_rows, _, n_frames, blocks, n_slots, _, ch = got.shape
    half = blocks * n_slots * CB
    deep = n_frames * ch

    def body(got_ref, w_ref, z_ref, act_ref, o_ref, next_ref, lhs, acc, keep_sems, act_sem):
        keeps = [pltpu.make_async_copy(act_ref, next_ref.at[:, 1], act_sem)]
        for r in range(n_rows):
            for s in range(n_slots):
                src = got_ref.at[r, 0, n_frames - 1, :, s]
                n = r * n_slots + s
                keeps.append(pltpu.make_async_copy(src, next_ref.at[s, 0, r], keep_sems.at[n]))
        for c in keeps:
            c.start()
        own_rows(got_ref, 0, lhs)
        acc[...] = dot(lhs[...], w_ref[...])
        give_rows(acc, ch, o_ref, z_ref)
        for c in keeps:
            c.wait()

    return call(
        body,
        [
            sums_shape(blocks, n_slots, n_rows, ch),
            jax.ShapeDtypeStruct((n_slots, 2, n_rows, blocks, CB, ch), jnp.bfloat16),
        ],
        (got, weight, sums, act),
        scratch=[
            pltpu.VMEM((half, n_rows * deep), jnp.bfloat16),
            pltpu.VMEM((half, weight.shape[1]), jnp.float32),
            pltpu.SemaphoreType.DMA((n_rows * n_slots,)),
            pltpu.SemaphoreType.DMA,
        ],
        flops=2 * half * weight.size,
        moved=2 * weight.size,
        far_out=(1,),
    )


def own_second(got, weight):
    n_rows, _, n_frames, blocks, n_slots, _, ch = got.shape
    half = blocks * n_slots * CB
    deep = n_frames * ch

    def body(got_ref, w_ref, o_ref, next_ref, lhs, acc, keep_sems):
        keeps = []
        for r in range(n_rows):
            for s in range(n_slots):
                src = got_ref.at[r, 1, n_frames - 1, :, s]
                n = r * n_slots + s
                keeps.append(pltpu.make_async_copy(src, next_ref.at[s, 0, r], keep_sems.at[n]))
                keeps[-1].start()
        own_rows(got_ref, 1, lhs)
        acc[...] = dot(lhs[...], w_ref[...])
        give_rows(acc, ch, o_ref, None)
        for c in keeps:
            c.wait()

    return call(
        body,
        [
            sums_shape(blocks, n_slots, n_rows, ch),
            jax.ShapeDtypeStruct((n_slots, 2, n_rows, blocks, CB, ch), jnp.bfloat16),
        ],
        (got, weight),
        scratch=[
            pltpu.VMEM((half, n_rows * deep), jnp.bfloat16),
            pltpu.VMEM((half, weight.shape[1]), jnp.float32),
            pltpu.SemaphoreType.DMA((n_rows * n_slots,)),
        ],
        flops=2 * half * weight.size,
        moved=2 * weight.size,
        far_out=(1,),
    )


def side_sums(edge_ref, k, side_ref, w, lhs):
    n_frames, blocks, n_slots, _, ch = side_ref.shape
    for s in range(n_slots):
        for f in range(n_frames):
            value = masked(edge_ref, k, s, side_ref[f, :, s])
            lhs[:, s, :, f * ch : (f + 1) * ch] = value
    half = blocks * n_slots * CB
    return folded(dot(lhs[...].reshape(half, n_frames * ch), w), ch, True)


def activation_row(which, side, w_sides, sums, bias, gain, edges):
    n_frames, blocks, n_slots, _, ch = side.shape
    n_cols, deep = blocks * CB, n_frames * ch

    def body(edge_ref, side_ref, w_ref, z_ref, b_ref, g_ref, o_ref, lhs):
        rows, y = beside(edge_ref, side_ref, side_ref)[which]
        total = side_sums(edge_ref, y, rows, w_ref[y], lhs) + z_ref[y] + b_ref[...]
        for s in range(n_slots):
            value = activated(total[:, s].reshape(n_cols, ch), g_ref[...])
            o_ref[s] = value.astype(jnp.bfloat16)

    return call(
        body,
        [jax.ShapeDtypeStruct((n_slots, n_cols, ch), jnp.bfloat16)],
        (side, w_sides, sums, bias, gain),
        scalars=(edges,),
        scratch=[pltpu.VMEM((blocks, n_slots, CB, deep), jnp.bfloat16)],
        flops=n_slots * n_cols * w_sides.size,
        moved=w_sides.size,
    )[0]


def act_part(near_row, far_row, near, w_own, w_sides, sums, kept, edges):
    n_slots, n_cols, ch = near_row.shape
    n_rows = sums.shape[0]
    half = n_slots * n_cols
    tiles = (n_slots, n_cols // CB, CB, ch)

    def body(edge_ref, nr_ref, fr_ref, nt_ref, ft_ref, near_ref, wo_ref, ws_ref, z_ref, kept_ref, o_ref, next_ref, lhs, side, sems):
        odd = edge_ref[2, 0]
        copies = [
            pltpu.make_async_copy(nt_ref, next_ref.at[:, 1, 1 - odd], sems.at[0]),
            pltpu.make_async_copy(ft_ref, next_ref.at[:, 1, odd], sems.at[1]),
        ]
        for c in copies:
            c.start()
        for s in range(n_slots):
            at = slice(s * n_cols, (s + 1) * n_cols)
            lhs[at, 0:ch] = jnp.where(odd != 0, nr_ref[s], fr_ref[s])
            lhs[at, ch : 2 * ch] = jnp.where(odd != 0, fr_ref[s], nr_ref[s])
        both = dot(lhs[...], wo_ref[...])
        wide = both.shape[1] // n_rows
        for y in range(n_rows):
            add_into(o_ref, y, folded(both[:, y * wide : (y + 1) * wide], ch, False), False, z_ref)
        add_sides(edge_ref, beside(edge_ref, near_ref, None)[:1], ws_ref, side, o_ref)
        for c in copies:
            c.wait()

    return call(
        body,
        [jax.ShapeDtypeStruct(sums.shape, jnp.float32), jax.ShapeDtypeStruct(kept.shape, kept.dtype)],
        (
            near_row, far_row, near_row.reshape(tiles), far_row.reshape(tiles),
            near, w_own, w_sides, sums, kept,
        ),
        scalars=(edges,),
        scratch=[
            pltpu.VMEM((half, n_rows * ch), jnp.bfloat16),
            pltpu.VMEM((half, ch), jnp.bfloat16),
            pltpu.SemaphoreType.DMA((2,)),
        ],
        flops=2 * half * w_own.size,
        moved=2 * (w_sides.size + w_own.size),
        far=(8,),
        far_out=(1,),
        aliases={9: 1},
    )


def cached_sides(near, far, w_sides, sums, edges):
    n_frames, blocks, n_slots, _, ch = far.shape
    deep = n_frames * ch

    def body(edge_ref, near_ref, far_ref, w_ref, z_ref, o_ref, lhs):
        for side, y in beside(edge_ref, near_ref, far_ref):
            o_ref[y] = z_ref[y] + side_sums(edge_ref, y, side, w_ref[y], lhs)

    return call(
        body,
        [jax.ShapeDtypeStruct(sums.shape, jnp.float32)],
        (near, far, w_sides, sums),
        scalars=(edges,),
        scratch=[pltpu.VMEM((blocks, n_slots, CB, deep), jnp.bfloat16)],
        flops=2 * blocks * n_slots * CB * w_sides.size,
        moved=2 * w_sides.size,
    )[0]


def last_part(far, w_sides, sums, bias, frame, edges):
    n_slots, n_rows, n_cols, ch = frame.shape

    def body(edge_ref, far_ref, w_ref, z_ref, b_ref, f_ref, o_ref, lhs):
        def give(y, total):
            for s in range(n_slots):
                value = z_ref[y, :, s] + b_ref[...]
                if total is not None:
                    value += total[s]
                value = value.reshape(n_cols, ch) + f_ref[s, y].astype(jnp.float32)
                o_ref[s, y] = value.astype(jnp.bfloat16)

        (_, done), (side, y) = beside(edge_ref, None, far_ref)
        for s in range(n_slots):
            lhs[s * n_cols : (s + 1) * n_cols] = masked(edge_ref, y, s, side[s])
        give(done, None)
        give(y, folded(dot(lhs[...], w_ref[y]), ch, False))

    return call(
        body,
        [jax.ShapeDtypeStruct(frame.shape, jnp.bfloat16)],
        (far, w_sides, sums, bias, frame),
        scalars=(edges,),
        scratch=[pltpu.VMEM((n_slots * n_cols, ch), jnp.bfloat16)],
        flops=n_slots * n_cols * w_sides.size,
        moved=2 * w_sides.size,
    )[0]


def local(
    frame_in,
    cache_first,
    cache_second,
    gain_first,
    gain_second,
    conv_first,
    conv_second,
    bias_first,
    bias_second,
    old_slot,
    new_slot,
    old_shift,
    new_shift,
    frame_count,
):
    n_slots, n_rows, n_cols, ch = frame_in.shape
    n_groups = lax.axis_size("stream")
    n_tiles = lax.axis_size("tile")
    my_group = lax.axis_index("stream")
    my_tile = lax.axis_index("tile")
    n_flight = old_slot.shape[0]
    blocks = n_cols // CB
    slot_ids = jnp.arange(n_flight, dtype=jnp.int32)
    held_new = new_slot[None, :] == slot_ids[:, None]
    source = lookup(held_new, old_slot)
    shift_after = lookup(held_new, new_shift)
    rotation = (shift_after - lookup(held_new, old_shift)) % n_tiles
    frames_done = lookup(held_new, frame_count)
    my_piece = my_group * n_tiles + my_tile
    my_frame = (my_piece // blocks) % 2
    keep = (frames_done >= 2 - my_frame).astype(jnp.int32)
    start = my_group * n_slots
    my_number = lax.dynamic_slice_in_dim((my_tile - shift_after) % n_tiles, start, n_slots)

    odd = my_tile % 2
    edges = jnp.stack(
        [my_number != 0, my_number != n_tiles - 1, jnp.broadcast_to(odd == 1, my_number.shape)]
    ).astype(jnp.int32)

    def swap_near(row):
        return lax.ppermute(row, "tile", [(i, i ^ 1) for i in range(n_tiles)])

    def swap_far(row):
        return lax.ppermute(
            row, "tile", [(i, (i + 2 * (i % 2) - 1) % n_tiles) for i in range(n_tiles)]
        )

    sent = pack(cache_first, cache_second).reshape(n_groups * n_tiles, n_slots, CB, ch)
    held = lax.all_to_all(sent, BOTH, 0, 0, tiled=True)

    act_own_1, act_sides_1 = spread(conv_first, False)
    act_first, near, far = first_activation(frame_in, gain_first[None], edges)
    act_near, act_far = swap_near(near), swap_far(far)
    held, act_first, act_near, act_far, act_own_1, act_sides_1 = lax.optimization_barrier(
        (held, act_first, act_near, act_far, act_own_1, act_sides_1)
    )

    moved = permute(held.reshape(n_groups, n_tiles, n_slots, CB, ch), source, rotation, keep)
    moved, act_later = lax.optimization_barrier((moved, act_first))
    got = lax.all_to_all(
        moved.reshape(n_groups * n_tiles, n_slots, CB, ch), BOTH, 0, 0, tiled=True
    )
    sums_1 = current_part(act_later, act_near, act_far, act_own_1, act_sides_1, edges)
    sums_1, conv_first, conv_second = lax.optimization_barrier((sums_1, conv_first, conv_second))
    act_own_2, act_sides_2 = spread(conv_second, False)
    own_1, sides_1 = spread(conv_first, True)
    own_2, sides_2 = spread(conv_second, True)
    got, sums_1, own_1, own_2, sides_1, sides_2, act_own_2, act_sides_2 = lax.optimization_barrier(
        (got, sums_1, own_1, own_2, sides_1, sides_2, act_own_2, act_sides_2)
    )
    got = got.reshape(n_rows, 2, 2, blocks, n_slots, CB, ch)

    def picked(cache, row):
        return lax.dynamic_index_in_dim(got[:, cache], row, 0, keepdims=False)

    near_1, far_1 = swap_near(picked(0, 1 - odd)), swap_far(picked(0, odd))
    near_rows, far_rows = picked(1, 1 - odd), picked(1, odd)
    act_tiles = act_first.reshape(n_slots, n_rows, blocks, CB, ch)
    sums_1, next_first = own_first(got, own_1, sums_1, act_tiles)
    near_rows, far_rows, sums_1 = lax.optimization_barrier((near_rows, far_rows, sums_1))
    near_2, far_2 = swap_near(near_rows), swap_far(far_rows)
    scale = (bias_first[None], gain_second[None], edges)
    near = activation_row(0, near_1, sides_1, sums_1, *scale)
    far = activation_row(1, far_1, sides_1, sums_1, *scale)
    act_near, act_far = swap_near(near), swap_far(far)
    got_later, far = lax.optimization_barrier((got, far))
    sums_2, kept = own_second(got_later, own_2)
    sums_2, next_second = act_part(
        near, far, act_near, act_own_2, act_sides_2, sums_2, kept, edges
    )
    sums_2 = cached_sides(near_2, far_2, sides_2, sums_2, edges)
    mixed_frame = last_part(act_far, act_sides_2, sums_2, bias_second[None], frame_in, edges)
    whole = (n_slots, 2, n_rows, n_cols, ch)
    return (mixed_frame, next_first.reshape(whole), next_second.reshape(whole))


def solution(mesh):
    frame = P("stream", "tile", None, None)
    cache = P("stream", None, "tile", None, None)
    return jax.shard_map(
        local,
        mesh=mesh,
        in_specs=(frame, cache, cache) + (P(),) * 11,
        out_specs=(frame, cache, cache),
        check_vma=False,
    )
```
